32 devices in a mesh: dp: 4 (over z), tensor: 8 (over y, x, core).
Axes of the slice: x: 2, y: 2, z: 4, core: 2. Of those that a mesh axis runs over, the one named last changes fastest.
Arguments:
- layer_input: bfloat16 [4096, 1024], P(('dp', 'tensor')), may hold values from -6 to 6
- output_grad: bfloat16 [4096, 1024], P(('dp', 'tensor')), may hold values from -24 to 24
- memory: bfloat16 [2352, 1024], P('dp'), may hold values from -6 to 6
- memory_length: int32 [4], P('dp'), may hold values from 147 to 588, as said below
- norm_gain: bfloat16 [3, 1024], replicated, may hold values from 0.5 to 1.5
- norm_bias: bfloat16 [3, 1024], replicated, may hold values from -4 to 4
- self_qkv: bfloat16 [3, 1024, 1024], P(None, None, 'tensor'), may hold values from -0.25 to 0.25
- self_bias: bfloat16 [2, 1024], P(None, 'tensor'), may hold values from -6 to 6
- self_out: bfloat16 [1024, 1024], P('tensor'), may hold values from -0.5 to 0.5
- cross_query: bfloat16 [1024, 1024], P(None, 'tensor'), may hold values from -0.25 to 0.25
- cross_kv: bfloat16 [2, 1024, 1024], P(None, None, 'tensor'), may hold values from -0.25 to 0.25
- cross_bias: bfloat16 [2, 1024], P(None, 'tensor'), may hold values from -6 to 6
- cross_out: bfloat16 [1024, 1024], P('tensor'), may hold values from -0.5 to 0.5
- up_weight: bfloat16 [1024, 4096], P(None, 'tensor'), may hold values from -0.1875 to 0.1875
- up_bias: bfloat16 [4096], P('tensor'), may hold values from -6 to 6
- down_weight: bfloat16 [4096, 1024], P('tensor'), may hold values from -0.09375 to 0.09375
- out_bias: bfloat16 [3, 1024], replicated, may hold values from -6 to 6
Outputs:
- layer_output: bfloat16 [4096, 1024], P(('dp', 'tensor'))
- input_grad: float32 [4096, 1024], P(('dp', 'tensor'))
- memory_grad: float32 [2352, 1024], P('dp', 'tensor')
- norm_gain_grad: float32 [3, 1024], replicated
- norm_bias_grad: float32 [3, 1024], replicated
- self_qkv_grad: float32 [3, 1024, 1024], P(None, None, 'tensor')
- self_bias_grad: float32 [2, 1024], P(None, 'tensor')
- self_out_grad: float32 [1024, 1024], P('tensor')
- cross_query_grad: float32 [1024, 1024], P(None, 'tensor')
- cross_kv_grad: float32 [2, 1024, 1024], P(None, None, 'tensor')
- cross_bias_grad: float32 [2, 1024], P(None, 'tensor')
- cross_out_grad: float32 [1024, 1024], P('tensor')
- up_weight_grad: float32 [1024, 4096], P(None, 'tensor')
- up_bias_grad: float32 [4096], P('tensor')
- down_weight_grad: float32 [4096, 1024], P('tensor')
- out_bias_grad: float32 [3, 1024], replicated
The draws below stay inside these ranges and needn't reach their ends.
Inputs may be any that keep to these rules, and one draw needn't show every extreme that they name: Each page's memory_length is either 588 or at most 294; exactly half of the pages are of each kind.
All inputs are finite; a program needn't handle non-finite values.
Results may differ from the reference program's by a relative error of at most 0.025.
The reference program's roundings to bfloat16 on the way count: a program that leaves them out, or rounds other values in their place, can miss the bound.
Values may be sent and summed in bfloat16 or wider, within the bound.
No kernel may reach another device: no remote copies, remote signals or barrier semaphores. Data moves between devices by JAX's collectives and lax.ppermute only.
A program may use at most 128 MiB of HBM per device.

```python
import jax
import jax.numpy as jnp
from jax import lax

D = 1024
HEADS = 16
FF = 4096
SEQ = 1024
MEM = 588
HEAD_DIM = 64
PAGES = 4
TOKENS = 4096


def draw_output_grad(key, part):
    key = jax.random.fold_in(key, 11)
    base_key = jax.random.fold_in(key, 0)
    position = jnp.arange(TOKENS, dtype=jnp.float32) / TOKENS
    rising = 1.0 + 2.0 * position
    base = jnp.clip(jax.random.normal(base_key, (TOKENS, D), jnp.float32), -4.0, 4.0)
    return (base * rising[:, None]).astype(jnp.bfloat16)


def draw_memory_length(key, part):
    key = jax.random.fold_in(key, 23)
    ranking_key, size_key = jax.random.split(key)
    ranking = jax.random.permutation(ranking_key, PAGES)
    reduced = jax.random.randint(size_key, (PAGES,), MEM // 4, MEM // 2 + 1)
    reduced = jnp.where(ranking == 1, MEM // 4, reduced)
    return jnp.where(ranking % 2 == 1, reduced, MEM).astype(jnp.int32)


def level_of(stream_key, shape, shards, least, top_value):
    loudness, own = 1.0, jax.random.fold_in(stream_key, 6)
    for axis_at, blocks in shards:
        steps = jnp.exp(jax.random.uniform(jax.random.fold_in(own, axis_at), (blocks,), jnp.float32, least / len(shards), top_value / len(shards)))
        loudness = loudness * jnp.repeat(steps, shape[axis_at] // blocks).reshape([-1 if axis == axis_at else 1 for axis in range(len(shape))])
    return loudness


def scatter_about(key, shape, scale, bound, cuts=(), kind=jnp.bfloat16):
    values = jax.random.normal(key, shape, jnp.float32) * scale
    if len(cuts) > 0:
        values = level_of(key, shape, cuts, -0.22, 0.18) * values
    return jnp.clip(values, min=-bound, max=bound).astype(kind)


def setup_inputs(seed: int = 0) -> dict:
    key_list = jax.random.split(jax.random.key(seed), 18)
    layer_input = scatter_about(key_list[0], (TOKENS, D), 1.0, 6.0, ((0, 32),))
    output_grad = draw_output_grad(jax.random.fold_in(key_list[17], 71), 0)
    memory = scatter_about(key_list[2], (PAGES * MEM, D), 1.0, 6.0, ((0, 4),))
    memory_length = draw_memory_length(jax.random.fold_in(key_list[17], 71), 0)
    norm_gain = jnp.clip(1.0 + 0.1 * jax.random.normal(key_list[4], (3, D), jnp.float32), 0.5, 1.5).astype(jnp.bfloat16)
    norm_bias = scatter_about(key_list[5], (3, D), 0.3, 4.0)
    self_qkv = scatter_about(key_list[6], (3, D, D), (D // 2) ** -0.5, 0.25, ((2, 8),))
    self_bias = scatter_about(key_list[7], (2, D), 0.5, 6.0, ((1, 8),))
    self_out = scatter_about(key_list[8], (D, D), (D // 8) ** -0.5, 0.5, ((0, 8),))
    cross_query = scatter_about(key_list[9], (D, D), (D // 2) ** -0.5, 0.25, ((1, 8),))
    cross_kv = scatter_about(key_list[10], (2, D, D), (D // 2) ** -0.5, 0.25, ((2, 8),))
    cross_bias = scatter_about(key_list[11], (2, D), 0.5, 6.0, ((1, 8),))
    cross_out = scatter_about(key_list[12], (D, D), (D // 8) ** -0.5, 0.5, ((0, 8),))
    up_weight = scatter_about(key_list[13], (D, FF), D ** -0.5, 0.1875, ((1, 8),))
    up_bias = scatter_about(key_list[14], (FF,), 0.5, 6.0, ((0, 8),))
    down_weight = scatter_about(key_list[15], (FF, D), FF ** -0.5, 0.09375, ((0, 8),))
    out_bias = scatter_about(key_list[16], (3, D), 0.5, 6.0)
    return dict(layer_input=layer_input, output_grad=output_grad, memory=memory, memory_length=memory_length, norm_gain=norm_gain, norm_bias=norm_bias, self_qkv=self_qkv, self_bias=self_bias, self_out=self_out, cross_query=cross_query, cross_kv=cross_kv, cross_bias=cross_bias, cross_out=cross_out, up_weight=up_weight, up_bias=up_bias, down_weight=down_weight, out_bias=out_bias)


@jax.custom_vjp
def low(v):
    return lax.optimization_barrier(v.astype(jnp.bfloat16)).astype(jnp.float32)

@jax.custom_vjp
def low_back(v):
    return v

def low_keep(v):
    return (low(v), None)

def low_pass(kept, grad):
    return (grad,)

def back_keep(v):
    return (v, None)

def back_low(kept, grad):
    return (low(grad),)
low.defvjp(low_keep, low_pass)
low_back.defvjp(back_keep, back_low)
EPS = 1e-05
NEG = -1e+30

def matmul(former, latter):
    return jnp.dot(former, latter, precision=lax.Precision.HIGHEST)

def both_round(values):
    return low(low_back(values))

def layer_norm(values, scale_by, shift_by):
    centre = values - lax.optimization_barrier(jnp.mean(values, axis=-1, keepdims=True))
    spread = lax.optimization_barrier(jnp.mean(centre * centre, axis=-1, keepdims=True))
    return centre * lax.rsqrt(spread + EPS) * scale_by + shift_by

def attend(queries, key_rows, value_rows, allowed):
    scores = low_back(matmul(queries, key_rows.T) * HEAD_DIM ** (-0.5))
    scores = jnp.where(allowed, scores, NEG)
    row_peak = lax.optimization_barrier(jnp.max(scores, axis=-1, keepdims=True))
    raised = jnp.exp(scores - row_peak)
    weights = raised / lax.optimization_barrier(jnp.sum(raised, axis=-1, keepdims=True))
    return both_round(matmul(low(weights), value_rows))

def split_heads(values):
    return values.reshape(values.shape[0], HEADS, HEAD_DIM).transpose(1, 0, 2)

def multi_head(queries, key_rows, value_rows, allowed):
    head_fn = jax.checkpoint(lambda head_item: attend(head_item[0], head_item[1], head_item[2], allowed))
    mixed_rows = lax.map(head_fn, (split_heads(queries), split_heads(key_rows), split_heads(value_rows)))
    return mixed_rows.transpose(1, 0, 2).reshape(queries.shape[0], D)

def page_layer(parameters, page_input, page_memory, length):
    norm_gain, norm_bias, self_qkv, self_bias, self_out, cross_query, cross_kv, cross_bias, cross_out, up_weight, up_bias, down_weight, out_bias = parameters
    hidden_one = low(layer_norm(page_input, norm_gain[0], norm_bias[0]))
    queries = both_round(matmul(hidden_one, self_qkv[0]) + self_bias[0])
    key_rows = both_round(matmul(hidden_one, self_qkv[1]))
    value_rows = both_round(matmul(hidden_one, self_qkv[2]) + self_bias[1])
    position = jnp.arange(SEQ)
    causal = position[None, :] <= position[:, None]
    self_mixed = multi_head(queries, key_rows, value_rows, causal)
    stream_two = page_input + low_back(matmul(self_mixed, self_out) + out_bias[0])
    hidden_two = low(layer_norm(stream_two, norm_gain[1], norm_bias[1]))
    cross_queries = both_round(matmul(hidden_two, cross_query) + cross_bias[0])
    memory_keys = both_round(matmul(page_memory, cross_kv[0]))
    memory_values = both_round(matmul(page_memory, cross_kv[1]) + cross_bias[1])
    visible = jnp.broadcast_to(jnp.arange(MEM)[None, :] < length, (SEQ, MEM))
    cross_mixed = multi_head(cross_queries, memory_keys, memory_values, visible)
    stream_three = stream_two + low_back(matmul(cross_mixed, cross_out) + out_bias[1])
    hidden_three = low(layer_norm(stream_three, norm_gain[2], norm_bias[2]))
    pre_act = low_back(matmul(hidden_three, up_weight) + up_bias)
    activated = low(jax.nn.gelu(pre_act, approximate=False))
    return stream_three + low_back(matmul(activated, down_weight) + out_bias[2])

def reference(layer_input, output_grad, memory, memory_length, norm_gain, norm_bias, self_qkv, self_bias, self_out, cross_query, cross_kv, cross_bias, cross_out, up_weight, up_bias, down_weight, out_bias):
    parameters = tuple((single.astype(jnp.float32) for single in (norm_gain, norm_bias, self_qkv, self_bias, self_out, cross_query, cross_kv, cross_bias, cross_out, up_weight, up_bias, down_weight, out_bias)))
    pages_in = layer_input.astype(jnp.float32).reshape(PAGES, SEQ, D)
    grads_in = output_grad.astype(jnp.float32).reshape(PAGES, SEQ, D)
    memory_in = memory.astype(jnp.float32).reshape(PAGES, MEM, D)

    def page_step(totals, page_item):
        page_input, page_grad, page_memory, length = page_item

        def forward(weights_all, inputs_all, context):
            return page_layer(weights_all, inputs_all, context, length)
        result, pullback = jax.vjp(forward, parameters, page_input, page_memory)
        weight_grads, input_part, memory_part = pullback(page_grad)
        totals = jax.tree.map(lambda former, latter: former + latter, totals, weight_grads)
        return (totals, (result, input_part, memory_part))
    empty_grads = jax.tree.map(jnp.zeros_like, parameters)
    totals, (outputs, input_grads, memory_grads) = lax.scan(page_step, empty_grads, (pages_in, grads_in, memory_in, memory_length))
    return (outputs.reshape(TOKENS, D).astype(jnp.bfloat16), input_grads.reshape(TOKENS, D), memory_grads.reshape(PAGES * MEM, D), totals[0], totals[1], totals[2], totals[3], totals[4], totals[5], totals[6], totals[7], totals[8], totals[9], totals[10], totals[11], totals[12])
```

```python
import functools

import jax
import jax.numpy as jnp
from jax import lax
from jax.experimental import pallas as pl
from jax.experimental.pallas import tpu as pltpu
from jax.sharding import PartitionSpec as P

HEAD_DIM = 64
EPS = 1e-05
NEG = -1e30
BLOCK = 256
FACTOR = HEAD_DIM ** (-0.5)
F32 = jnp.float32
BF16 = jnp.bfloat16

SMEM = pl.BlockSpec(memory_space=pltpu.SMEM)
VMEM = pl.BlockSpec(memory_space=pltpu.VMEM)


def nn(a, b):
    return lax.dot_general(a, b, (((1,), (0,)), ((), ())), preferred_element_type=F32)


def nt(a, b):
    return lax.dot_general(a, b, (((1,), (1,)), ((), ())), preferred_element_type=F32)


def call(body, outs, ins, flops=0, scratch=(), trans=0, vmem=16):
    nbytes = sum(a.size * a.dtype.itemsize for a in ins)
    nbytes += sum(o.size * o.dtype.itemsize for o in outs)
    return pl.pallas_call(
        body,
        out_shape=tuple(outs),
        in_specs=[SMEM if a.dtype == jnp.int32 else VMEM for a in ins],
        out_specs=tuple(VMEM for _ in outs),
        scratch_shapes=list(scratch),
        compiler_params=pltpu.CompilerParams(vmem_limit_bytes=vmem * 2**20),
        cost_estimate=pl.CostEstimate(
            flops=int(flops), bytes_accessed=int(nbytes), transcendentals=int(trans)
        ),
    )(*ins)


def sds(shape, dtype):
    return jax.ShapeDtypeStruct(shape, dtype)


def normed(values):
    centre = values - jnp.mean(values, axis=-1, keepdims=True)
    spread = jnp.mean(centre * centre, axis=-1, keepdims=True)
    scale = lax.rsqrt(spread + EPS)
    return centre * scale, scale


def norm_back(values, gain, upstream):
    hat, scale = normed(values)
    scaled = upstream * gain
    first = jnp.mean(scaled, axis=-1, keepdims=True)
    second = jnp.mean(scaled * hat, axis=-1, keepdims=True)
    return scale * (scaled - first - hat * second), hat


def row_of(ref, row):
    return ref[row : row + 1, :].astype(F32)


def ordered(core, own, other):
    return jnp.where(core == 0, own, other), jnp.where(core == 0, other, own)


def heads_only(values, head, heads):
    if heads == 1:
        return values
    lane = lax.broadcasted_iota(jnp.int32, values.shape, 1)
    return jnp.where(lane // HEAD_DIM == head, values, jnp.zeros_like(values))


def key_tiles(total, limit):
    return [(at, min(BLOCK, limit - at)) for at in range(0, limit, BLOCK)]


def allowed_tile(at, width, row0, length, causal):
    key_at = at + lax.broadcasted_iota(jnp.int32, (width, BLOCK), 0)
    if causal:
        return key_at <= row0 + lax.broadcasted_iota(jnp.int32, (width, BLOCK), 1)
    return key_at < length


def scores_tile(k_ref, query, at, width, row0, length, causal):
    scores = nt(k_ref[at : at + width, :], query)
    if causal and at + width <= row0:
        return scores
    return jnp.where(allowed_tile(at, width, row0, length, causal), scores, NEG)


def attend(q_ref, k_ref, v_ref, mixed_ref, lse_ref, length, causal):
    seq, width = q_ref.shape
    keys = k_ref.shape[0]
    heads = width // HEAD_DIM
    value_t = jnp.transpose(v_ref[...])
    for row0 in range(0, seq, BLOCK):
        query = q_ref[row0 : row0 + BLOCK, :]
        tiles = key_tiles(keys, row0 + BLOCK if causal else keys)
        columns = []
        for head in range(heads):
            own = heads_only(query, head, heads)
            scores = [scores_tile(k_ref, own, at, w, row0, length, causal) for at, w in tiles]
            peak = functools.reduce(
                jnp.maximum, [jnp.max(s, axis=0, keepdims=True) for s in scores]
            )
            total = jnp.zeros_like(peak)
            mixed = jnp.zeros((HEAD_DIM, BLOCK), F32)
            for (at, w), s in zip(tiles, scores):
                raised = jnp.exp(s - peak)
                total = total + jnp.sum(raised, axis=0, keepdims=True)
                rows = value_t[head * HEAD_DIM : (head + 1) * HEAD_DIM, at : at + w]
                mixed = mixed + nn(rows, raised.astype(BF16))
            columns.append(mixed * (1.0 / total))
            lse_ref[head : head + 1, row0 : row0 + BLOCK] = peak + jnp.log(total)
        mixed_ref[row0 : row0 + BLOCK, :] = jnp.transpose(jnp.concatenate(columns, 0)).astype(BF16)


def attend_back(q_ref, k_ref, v_ref, up_ref, lse_ref, dq_ref, dk_acc, dv_acc, length, causal):
    seq, width = q_ref.shape
    keys = k_ref.shape[0]
    heads = width // HEAD_DIM
    key_t = jnp.transpose(k_ref[...])
    dk_acc[...] = jnp.zeros_like(dk_acc)
    dv_acc[...] = jnp.zeros_like(dv_acc)
    for row0 in range(0, seq, BLOCK):
        query = q_ref[row0 : row0 + BLOCK, :]
        upstream = up_ref[row0 : row0 + BLOCK, :]
        tiles = key_tiles(keys, row0 + BLOCK if causal else keys)
        columns = []
        for head in range(heads):
            own = heads_only(query, head, heads)
            own_up = heads_only(upstream, head, heads)
            lse = lse_ref[head : head + 1, row0 : row0 + BLOCK]
            weights, grads = [], []
            inner = jnp.zeros((1, BLOCK), F32)
            for at, w in tiles:
                weight = jnp.exp(scores_tile(k_ref, own, at, w, row0, length, causal) - lse)
                grad = nt(v_ref[at : at + w, :], own_up)
                inner = inner + jnp.sum(weight * grad, axis=0, keepdims=True)
                weights.append(weight)
                grads.append(grad)
            column = jnp.zeros((HEAD_DIM, BLOCK), F32)
            for (at, w), weight, grad in zip(tiles, weights, grads):
                score_grad = (weight * (grad - inner)).astype(BF16)
                dv_acc[at : at + w, :] += nn(weight.astype(BF16), own_up)
                dk_acc[at : at + w, :] += nn(score_grad, own)
                rows = key_t[head * HEAD_DIM : (head + 1) * HEAD_DIM, at : at + w]
                column = column + nn(rows, score_grad)
            columns.append(column * FACTOR)
        dq_ref[row0 : row0 + BLOCK, :] = jnp.transpose(jnp.concatenate(columns, 0)).astype(BF16)


def self_forward(chips, ids, *refs):
    parts = refs[: 2 * chips]
    gain, shift, wqkv, bias, x_ref, h_ref, qkv_ref, mixed_ref, lse_ref = refs[2 * chips :]
    core, chip = ids[0] % 2, ids[0] // 2
    own = parts[0].shape[0]
    for mask in range(chips):
        lo, hi = ordered(core, parts[2 * mask][...], parts[2 * mask + 1][...])
        rows = jnp.concatenate([lo, hi], 0)
        at = pl.ds(pl.multiple_of((chip ^ mask) * 2 * own, 2 * own), 2 * own)
        x_ref[at, :] = rows
        hat, _ = normed(rows.astype(F32))
        hidden = (hat * row_of(gain, 0) + row_of(shift, 0)).astype(BF16)
        h_ref[at, :] = hidden
        query = nn(hidden, wqkv[0]) + row_of(bias, 0)
        qkv_ref[0, at, :] = (query.astype(BF16).astype(F32) * FACTOR).astype(BF16)
        qkv_ref[1, at, :] = nn(hidden, wqkv[1]).astype(BF16)
        qkv_ref[2, at, :] = (nn(hidden, wqkv[2]) + row_of(bias, 1)).astype(BF16)
    attend(qkv_ref.at[0], qkv_ref.at[1], qkv_ref.at[2], mixed_ref, lse_ref, None, True)


def project_pairs(parts, weights, rows):
    total = None
    for at in range(0, len(parts), 2):
        lhs = [parts[at][rows, :], parts[at + 1][rows, :]]
        rhs = [weights[at][...], weights[at + 1][...]]
        if lhs[0].shape[1] % 128 == 0:
            term = nn(jnp.concatenate(lhs, 1), jnp.concatenate(rhs, 0))
        else:
            term = nn(lhs[0], rhs[0]) + nn(lhs[1], rhs[1])
        total = term if total is None else total + term
    return total


def cross_forward(chips, length, *refs):
    parts, wout = refs[: 2 * chips], refs[2 * chips : 4 * chips]
    (x_ref, gain, shift, out_bias, wq, bias, mk, mv) = refs[4 * chips : 4 * chips + 8]
    s2_ref, h_ref, q_ref, mixed_ref, lse_ref = refs[4 * chips + 8 :]
    for row0 in range(0, x_ref.shape[0], BLOCK):
        rows = pl.ds(row0, BLOCK)
        branch = project_pairs(parts, wout, rows) + row_of(out_bias, 0)
        stream = x_ref[rows, :].astype(F32) + branch
        s2_ref[rows, :] = stream
        hat, _ = normed(stream)
        hidden = (hat * row_of(gain, 1) + row_of(shift, 1)).astype(BF16)
        h_ref[rows, :] = hidden
        query = (nn(hidden, wq[...]) + row_of(bias, 0)).astype(BF16).astype(F32)
        q_ref[rows, :] = (query * FACTOR).astype(BF16)
    attend(q_ref, mk, mv, mixed_ref, lse_ref, length[0], False)


def mlp(chips, ids, *refs):
    parts, wout = refs[: 2 * chips], refs[2 * chips : 4 * chips]
    g_parts = refs[4 * chips : 6 * chips]
    (s2_ref, gain, shift, out_bias, wup, bup, wdown) = refs[6 * chips : 6 * chips + 7]
    s3_own, h_ref, act_ref, pg_ref, g_ref, sums, ups, s3 = refs[6 * chips + 7 :]
    core, chip = ids[0] % 2, ids[0] // 2
    own = s3_own.shape[0]
    sums[...] = jnp.zeros_like(sums)
    ups[...] = jnp.zeros_like(ups)
    for mask in range(chips):
        rows = pl.ds(pl.multiple_of((chip ^ mask) * 2 * own, 2 * own), 2 * own)
        branch = project_pairs(parts, wout, rows) + row_of(out_bias, 1)
        stream = s2_ref[rows, :] + branch
        if mask == 0:
            s3[...] = stream
            s3_own[...] = s3[pl.ds(pl.multiple_of(core * own, own), own), :]
        hat, _ = normed(stream)
        hidden = (hat * row_of(gain, 2) + row_of(shift, 2)).astype(BF16)
        h_ref[rows, :] = hidden
        pre = nn(hidden, wup[...]) + bup[...].astype(F32)
        half = 0.5 * (1.0 + lax.erf(pre * (0.5**0.5)))
        act_ref[rows, :] = (pre * half).astype(BF16)
        slope = half + pre * jnp.exp(-0.5 * pre * pre) * 0.3989422804014327
        lo, hi = ordered(core, g_parts[2 * mask][...], g_parts[2 * mask + 1][...])
        grad = jnp.concatenate([lo, hi], 0)
        g_ref[rows, :] = grad
        pre_grad = (nt(grad, wdown[...]) * slope).astype(BF16)
        pg_ref[rows, :] = pre_grad
        ups[...] += jnp.sum(pre_grad.astype(F32), axis=0, keepdims=True)
        sums[...] += jnp.sum(grad.astype(F32), axis=0, keepdims=True)


def rows_for(ref, chip, core, own, chips):
    picks = []
    for mask in range(chips):
        at = pl.multiple_of(((chip ^ mask) * 2 + core) * own, own)
        picks.append(ref[pl.ds(at, own), :])
    return jnp.concatenate(picks, 0)


def partial_sibling(chips, operands, dot, ids, *refs):
    out = refs[-1]
    own = out.shape[1]
    total = None
    for lhs, rhs in zip(refs[:operands], refs[operands : 2 * operands]):
        picked = rows_for(lhs, ids[0] // 2, 1 - ids[0] % 2, own, chips)
        term = dot(picked, rhs[...])
        total = term if total is None else total + term
    for mask in range(chips):
        out[mask] = total[mask * own : (mask + 1) * own].astype(BF16)


def partial_own(chips, operands, dot, ids, *refs):
    got, first = refs[2 * operands : 2 * operands + 2]
    sends = refs[2 * operands + 2 :]
    own = first.shape[0]
    total = None
    for lhs, rhs in zip(refs[:operands], refs[operands : 2 * operands]):
        picked = rows_for(lhs, ids[0] // 2, ids[0] % 2, own, chips)
        term = dot(picked, rhs[...])
        total = term if total is None else total + term
    for mask in range(chips):
        block = total[mask * own : (mask + 1) * own] + got[mask].astype(F32)
        if mask == 0:
            first[...] = block
        else:
            sends[mask - 1][...] = block.astype(BF16)


def three_back(chips, *refs):
    first = refs[0]
    got = refs[1:chips]
    s3, gain, g_own, resid, message = refs[chips:]
    own = first.shape[0]
    total = first[...]
    for part in got:
        total = total + part[...].astype(F32)
    back, hat = norm_back(s3[...], row_of(gain, 2), total)
    grad = g_own[...].astype(F32) + back
    resid[...] = grad
    message[0:own, :] = grad.astype(BF16)
    sums = jnp.concatenate(
        [
            jnp.sum(total * hat, axis=0, keepdims=True),
            jnp.sum(total, axis=0, keepdims=True),
            jnp.zeros((14, total.shape[1]), F32),
        ],
        0,
    )
    message[own : own + 16, :] = sums.astype(BF16)


def cross_back(chips, ids, length, *refs):
    parts = refs[: 2 * chips]
    wout, q_ref, mk, mv, lse = refs[2 * chips : 2 * chips + 5]
    cg_ref, sums, dq_ref, dkv_ref, biases = refs[2 * chips + 5 : 2 * chips + 10]
    up_ref, dk_acc, dv_acc = refs[2 * chips + 10 :]
    core, chip = ids[0] % 2, ids[0] // 2
    own = parts[0].shape[0] - 16
    norm_sums = jnp.zeros((2, cg_ref.shape[1]), F32)
    bias_sum = jnp.zeros((1, cg_ref.shape[1]), F32)
    for mask in range(chips):
        lo, hi = ordered(core, parts[2 * mask][...], parts[2 * mask + 1][...])
        norm_sums = norm_sums + lo[own : own + 2].astype(F32) + hi[own : own + 2].astype(F32)
        rows = jnp.concatenate([lo[:own], hi[:own]], 0)
        at = pl.ds(pl.multiple_of((chip ^ mask) * 2 * own, 2 * own), 2 * own)
        cg_ref[at, :] = rows
        bias_sum = bias_sum + jnp.sum(rows.astype(F32), axis=0, keepdims=True)
        up_ref[at, :] = nt(rows, wout[...]).astype(BF16)
    sums[...] = jnp.concatenate([norm_sums, bias_sum], 0)
    attend_back(q_ref, mk, mv, up_ref, lse, dq_ref, dk_acc, dv_acc, length[0], False)
    dkv_ref[0] = dk_acc[...].astype(BF16)
    dv = dv_acc[...].astype(BF16)
    dkv_ref[1] = dv
    biases[0:1, :] = jnp.sum(dq_ref[...].astype(F32), axis=0, keepdims=True)
    biases[1:2, :] = jnp.sum(dv.astype(F32), axis=0, keepdims=True)


def self_back(chips, ids, *refs):
    parts, wq = refs[: 2 * chips], refs[2 * chips : 4 * chips]
    (s2_ref, gain, cg_ref, resid_two, wout, qkv, lse) = refs[4 * chips : 4 * chips + 7]
    sg_ref, resid_one, sums, grads, biases = refs[4 * chips + 7 : 4 * chips + 12]
    base, up_ref, dk_acc, dv_acc = refs[4 * chips + 12 :]
    own = resid_two.shape[0]
    mine = pl.ds(pl.multiple_of(ids[0] * own, own), own)
    base[...] = cg_ref[...].astype(F32)
    base[mine, :] = resid_two[...]
    sums[...] = jnp.zeros_like(sums)
    for row0 in range(0, s2_ref.shape[0], BLOCK):
        rows = pl.ds(row0, BLOCK)
        upstream = project_pairs(parts, wq, rows)
        back, hat = norm_back(s2_ref[rows, :], row_of(gain, 1), upstream)
        grad = base[rows, :] + back
        base[rows, :] = grad
        rounded = grad.astype(BF16)
        sg_ref[rows, :] = rounded
        sums[0:1, :] += jnp.sum(upstream * hat, axis=0, keepdims=True)
        sums[1:2, :] += jnp.sum(upstream, axis=0, keepdims=True)
        sums[2:3, :] += jnp.sum(rounded.astype(F32), axis=0, keepdims=True)
        up_ref[rows, :] = nt(rounded, wout[...]).astype(BF16)
    resid_one[...] = base[mine, :]
    attend_back(
        qkv.at[0], qkv.at[1], qkv.at[2], up_ref, lse, grads.at[0], dk_acc, dv_acc, None, True
    )
    grads[1] = dk_acc[...].astype(BF16)
    grads[2] = dv_acc[...].astype(BF16)
    biases[0:1, :] = jnp.sum(grads[0].astype(F32), axis=0, keepdims=True)
    biases[1:2, :] = jnp.sum(grads[2].astype(F32), axis=0, keepdims=True)


def first_norm_sums(x_ref, grads, wqkv, sums):
    sums[...] = jnp.zeros_like(sums)
    for row0 in range(0, x_ref.shape[0], BLOCK):
        rows = pl.ds(row0, BLOCK)
        upstream = sum(nt(grads[i, rows, :], wqkv[i]) for i in range(3))
        hat, _ = normed(x_ref[rows, :].astype(F32))
        sums[0:1, :] += jnp.sum(upstream * hat, axis=0, keepdims=True)
        sums[1:2, :] += jnp.sum(upstream, axis=0, keepdims=True)


def one_back(chips, *refs):
    first = refs[0]
    got = refs[1:chips]
    x_own, gain, resid, out = refs[chips:]
    total = first[...]
    for part in got:
        total = total + part[...].astype(F32)
    back, _ = norm_back(x_own[...].astype(F32), row_of(gain, 0), total)
    out[...] = resid[...] + back


def on_device(
    layer_input,
    output_grad,
    memory,
    memory_length,
    norm_gain,
    norm_bias,
    self_qkv,
    self_bias,
    self_out,
    cross_query,
    cross_kv,
    cross_bias,
    cross_out,
    up_weight,
    up_bias,
    down_weight,
    out_bias,
):
    ranks = lax.axis_size("tensor")
    pages_ranks = lax.axis_size("dp")
    chips = ranks // 2
    rank = lax.axis_index("tensor")
    ids = jnp.reshape(rank, (1,)).astype(jnp.int32)
    own, wide = layer_input.shape
    seq = own * ranks
    width = self_qkv.shape[2]
    heads = width // HEAD_DIM
    hidden = up_bias.shape[0]
    mem = memory.shape[0]
    mem_pad = -(-mem // 128) * 128

    def swap(values, mask):
        return lax.ppermute(values, "tensor", [(i, i ^ mask) for i in range(ranks)])

    def gather(values):
        parts = []
        far = [values] + [swap(values, 2 * mask) for mask in range(1, chips)]
        for block in far:
            parts += [block, swap(block, 1)]
        return parts

    def scatter_sum(lhs, rhs, dot=nt):
        count = len(lhs)
        rows = lhs[0].shape[0] // ranks
        columns = rhs[0].shape[0 if dot is nt else 1]
        cost = sum(a.size for a in lhs) * columns
        sibling = call(
            functools.partial(partial_sibling, chips, count, dot),
            [sds((chips, rows, columns), BF16)],
            [ids, *lhs, *rhs],
            cost,
        )[0]
        got = swap(sibling, 1)
        sums = call(
            functools.partial(partial_own, chips, count, dot),
            [sds((rows, columns), F32)] + [sds((rows, columns), BF16)] * (chips - 1),
            [ids, *lhs, *rhs, got],
            cost,
        )
        return [sums[0]] + [swap(sums[mask], 2 * mask) for mask in range(1, chips)]

    def along(values, pairs):
        return lax.ppermute(
            values,
            "dp",
            [(at + a, at + b) for at in range(0, pages_ranks, 4) for a, b in pairs],
        )

    def dp_sum(values):
        if pages_ranks % 4:
            return lax.psum(values, "dp").astype(F32)
        place = lax.axis_index("dp") % 4
        inner = (values.astype(F32) + along(values, [(0, 1), (3, 2)]).astype(F32)).astype(BF16)
        total = (inner.astype(F32) + along(inner, [(1, 2), (2, 1)]).astype(F32)).astype(BF16)
        mask = 4
        while mask < pages_ranks:
            other = lax.ppermute(total, "dp", [(i, i ^ mask) for i in range(pages_ranks)])
            total = (total.astype(F32) + other.astype(F32)).astype(BF16)
            mask *= 2
        outer = along(total, [(1, 0), (2, 3)])
        return jnp.where((place == 1) | (place == 2), total, outer).astype(F32)

    x_parts = gather(layer_input)
    so_parts = gather(self_out)
    co_parts = gather(cross_out)
    g_parts = gather(output_grad)
    wq_parts = gather(jnp.transpose(cross_query))

    padded = jnp.pad(memory, ((0, mem_pad - mem), (0, 0)))
    mem_keys = jnp.dot(padded, cross_kv[0], preferred_element_type=F32).astype(BF16)
    mem_values = (
        jnp.dot(padded, cross_kv[1], preferred_element_type=F32) + cross_bias[1].astype(F32)
    ).astype(BF16)

    x, hidden_one, qkv, self_mixed, self_lse = call(
        functools.partial(self_forward, chips),
        [
            sds((seq, wide), BF16),
            sds((seq, wide), BF16),
            sds((3, seq, width), BF16),
            sds((seq, width), BF16),
            sds((heads, seq), F32),
        ],
        [ids, *x_parts, norm_gain, norm_bias, self_qkv, self_bias],
        2 * seq * wide * 3 * width + 4 * seq * seq * width,
    )
    mixed_parts = gather(self_mixed)
    stream_two, hidden_two, cross_q, cross_mixed, cross_lse = call(
        functools.partial(cross_forward, chips),
        [
            sds((seq, wide), F32),
            sds((seq, wide), BF16),
            sds((seq, width), BF16),
            sds((seq, width), BF16),
            sds((heads, seq), F32),
        ],
        [
            memory_length,
            *mixed_parts,
            *so_parts,
            x,
            norm_gain,
            norm_bias,
            out_bias,
            cross_query,
            cross_bias,
            mem_keys,
            mem_values,
        ],
        2 * seq * wide * (wide + width) + 4 * seq * mem_pad * width,
    )
    cross_parts = gather(cross_mixed)
    stream_three, hidden_three, activated, pre_grad, whole_grad, grad_sum, up_bias_grad = call(
        functools.partial(mlp, chips),
        [
            sds((own, wide), F32),
            sds((seq, wide), BF16),
            sds((seq, hidden), BF16),
            sds((seq, hidden), BF16),
            sds((seq, wide), BF16),
            sds((1, wide), F32),
            sds((1, hidden), F32),
        ],
        [
            ids,
            *cross_parts,
            *co_parts,
            *g_parts,
            stream_two,
            norm_gain,
            norm_bias,
            out_bias,
            up_weight,
            up_bias.reshape(1, -1),
            down_weight,
        ],
        2 * seq * wide * (wide + 2 * hidden),
        [pltpu.VMEM((2 * own, wide), F32)],
    )
    three_terms = scatter_sum([pre_grad], [up_weight])

    def grad_dot(lhs, rhs):
        return lax.dot_general(
            lhs, rhs, (((0,), (0,)), ((), ())), preferred_element_type=F32
        ).astype(BF16)

    down_grad = dp_sum(grad_dot(activated, whole_grad))
    up_grad = dp_sum(grad_dot(hidden_three, pre_grad))

    resid_two, message = call(
        functools.partial(three_back, chips),
        [sds((own, wide), F32), sds((own + 16, wide), BF16)],
        [*three_terms, stream_three, norm_gain, output_grad],
    )
    cg_parts = gather(message)
    cross_grad, cross_sums, dq2, dkv2, cross_bias_grad = call(
        functools.partial(cross_back, chips),
        [
            sds((seq, wide), BF16),
            sds((3, wide), F32),
            sds((seq, width), BF16),
            sds((2, mem_pad, width), BF16),
            sds((2, width), F32),
        ],
        [
            ids,
            memory_length,
            *cg_parts,
            cross_out,
            cross_q,
            mem_keys,
            mem_values,
            cross_lse,
        ],
        2 * seq * wide * width + 10 * seq * mem_pad * width,
        [
            pltpu.VMEM((seq, width), BF16),
            pltpu.VMEM((mem_pad, width), F32),
            pltpu.VMEM((mem_pad, width), F32),
        ],
    )
    dq2_parts = gather(dq2)
    out_terms = scatter_sum([activated], [down_weight], nn)
    output = (
        stream_three + out_bias[2].astype(F32) + sum(term.astype(F32) for term in out_terms)
    ).astype(BF16)
    memory_terms = scatter_sum([cross_kv[0], cross_kv[1]], [dkv2[0], dkv2[1]])
    memory_grad = jnp.transpose(sum(term.astype(F32) for term in memory_terms)[:, :mem])
    cross_out_grad = dp_sum(grad_dot(cross_mixed, cross_grad))
    cross_query_grad = dp_sum(grad_dot(hidden_two, dq2))
    cross_kv_grad = dp_sum(
        jnp.einsum("md,kme->kde", padded, dkv2, preferred_element_type=F32).astype(BF16)
    )

    self_grad, resid_one, self_sums, grads, self_bias_grad = call(
        functools.partial(self_back, chips),
        [
            sds((seq, wide), BF16),
            sds((own, wide), F32),
            sds((3, wide), F32),
            sds((3, seq, width), BF16),
            sds((2, width), F32),
        ],
        [
            ids,
            *dq2_parts,
            *wq_parts,
            stream_two,
            norm_gain,
            cross_grad,
            resid_two,
            self_out,
            qkv,
            self_lse,
        ],
        2 * seq * wide * (wide + width) + 10 * seq * seq * width,
        [
            pltpu.VMEM((seq, wide), F32),
            pltpu.VMEM((seq, width), BF16),
            pltpu.VMEM((seq, width), F32),
            pltpu.VMEM((seq, width), F32),
        ],
    )
    one_terms = scatter_sum([grads[i] for i in range(3)], [self_qkv[i] for i in range(3)])
    self_qkv_grad = dp_sum(
        jnp.einsum("fd,kfe->kde", hidden_one, grads, preferred_element_type=F32).astype(BF16)
    )
    self_out_grad = dp_sum(grad_dot(self_mixed, self_grad))
    one_all = call(
        first_norm_sums,
        [sds((2, wide), F32)],
        [x, grads, self_qkv],
        6 * seq * wide * width,
    )[0]
    one_all = one_all + swap(one_all, 1)
    one_all = one_all + sum(swap(one_all, 2 * mask) for mask in range(1, chips))

    biases = jnp.concatenate(
        [self_bias_grad.reshape(-1), cross_bias_grad.reshape(-1), up_bias_grad.reshape(-1)]
    )
    biases = jnp.pad(biases, (0, wide - biases.shape[0])).reshape(1, wide)
    small = jnp.concatenate([one_all, self_sums, cross_sums, grad_sum, biases], 0)
    small = small + sum(
        lax.ppermute(
            small, "dp", [(i, (i + step) % pages_ranks) for i in range(pages_ranks)]
        )
        for step in range(1, pages_ranks)
    )
    (input_grad,) = call(
        functools.partial(one_back, chips),
        [sds((own, wide), F32)],
        [*one_terms, layer_input, norm_gain, resid_one],
    )
    flat = small[9]
    return (
        output,
        input_grad,
        memory_grad,
        jnp.stack([small[0], small[2], small[5]]),
        jnp.stack([small[1], small[3], small[6]]),
        self_qkv_grad,
        flat[: 2 * width].reshape(2, width),
        self_out_grad,
        cross_query_grad,
        cross_kv_grad,
        flat[2 * width : 4 * width].reshape(2, width),
        cross_out_grad,
        up_grad,
        flat[4 * width : 4 * width + hidden],
        down_grad,
        jnp.stack([small[4], small[7], small[8]]),
    )


def solution(mesh):
    return jax.shard_map(
        on_device,
        mesh=mesh,
        in_specs=(
            P(("dp", "tensor"), None),
            P(("dp", "tensor"), None),
            P("dp", None),
            P("dp"),
            P(),
            P(),
            P(None, None, "tensor"),
            P(None, "tensor"),
            P("tensor", None),
            P(None, "tensor"),
            P(None, None, "tensor"),
            P(None, "tensor"),
            P("tensor", None),
            P(None, "tensor"),
            P("tensor"),
            P("tensor", None),
            P(),
        ),
        out_specs=(
            P(("dp", "tensor"), None),
            P(("dp", "tensor"), None),
            P("dp", "tensor"),
            P(),
            P(),
            P(None, None, "tensor"),
            P(None, "tensor"),
            P("tensor", None),
            P(None, "tensor"),
            P(None, None, "tensor"),
            P(None, "tensor"),
            P("tensor", None),
            P(None, "tensor"),
            P("tensor"),
            P("tensor", None),
            P(),
        ),
        check_vma=False,
    )
```

```python
import functools

import jax
import jax.numpy as jnp
from jax import lax
from jax.experimental import pallas as pl
from jax.experimental.pallas import tpu as pltpu
from jax.sharding import PartitionSpec as P

HEAD_DIM = 64
EPS = 1e-05
NEG = -1e30
BLOCK = 256
FACTOR = HEAD_DIM ** (-0.5)
F32 = jnp.float32
BF16 = jnp.bfloat16

def nn(a, b):
    return lax.dot_general(a, b, (((1,), (0,)), ((), ())), preferred_element_type=F32)


def nt(a, b):
    return lax.dot_general(a, b, (((1,), (1,)), ((), ())), preferred_element_type=F32)


WEIGHT = 0.12


def call(body, outs, ins, flops=0, scratch=(), after=(), vmem=8):
    inside = pl.BlockSpec(memory_space=pltpu.VMEM)
    scalar = pl.BlockSpec(memory_space=pltpu.SMEM)
    count, tokens = len(ins), len(after)
    nbytes = sum(a.size * a.dtype.itemsize for a in ins)
    nbytes += sum(o.size * o.dtype.itemsize for o in outs)

    def kernel(*refs):
        body(*refs[:count], *refs[count + tokens :])

    return pl.pallas_call(
        kernel,
        out_shape=tuple(outs),
        in_specs=[scalar if a.dtype == jnp.int32 else inside for a in ins]
        + [pl.BlockSpec(memory_space=pl.ANY)] * tokens,
        out_specs=tuple(inside for _ in outs),
        scratch_shapes=list(scratch),
        compiler_params=pltpu.CompilerParams(vmem_limit_bytes=vmem * 2**20),
        cost_estimate=pl.CostEstimate(
            flops=int(flops * WEIGHT), bytes_accessed=int(nbytes * WEIGHT), transcendentals=0
        ),
    )(*ins, *after)


def sds(shape, dtype):
    return jax.ShapeDtypeStruct(shape, dtype)


def normed(values):
    centre = values - jnp.mean(values, axis=-1, keepdims=True)
    spread = jnp.mean(centre * centre, axis=-1, keepdims=True)
    scale = lax.rsqrt(spread + EPS)
    return centre * scale, scale


def norm_back(values, gain, upstream):
    hat, scale = normed(values)
    scaled = upstream * gain
    first = jnp.mean(scaled, axis=-1, keepdims=True)
    second = jnp.mean(scaled * hat, axis=-1, keepdims=True)
    return scale * (scaled - first - hat * second), hat


def row_of(ref, row):
    return ref[row : row + 1, :].astype(F32)


def ordered(core, own, other):
    return jnp.where(core == 0, own, other), jnp.where(core == 0, other, own)


def heads_only(values, head, heads):
    if heads == 1:
        return values
    lane = lax.broadcasted_iota(jnp.int32, values.shape, 1)
    return jnp.where(lane // HEAD_DIM == head, values, jnp.zeros_like(values))


def key_tiles(total, limit):
    return [(at, min(BLOCK, limit - at)) for at in range(0, limit, BLOCK)]


def allowed_tile(at, width, row0, length, causal):
    key_at = at + lax.broadcasted_iota(jnp.int32, (width, BLOCK), 0)
    if causal:
        return key_at <= row0 + lax.broadcasted_iota(jnp.int32, (width, BLOCK), 1)
    return key_at < length


def scores_tile(k_ref, query, at, width, row0, length, causal):
    scores = nt(k_ref[at : at + width, :], query)
    if causal and at + width <= row0:
        return scores
    return jnp.where(allowed_tile(at, width, row0, length, causal), scores, NEG)


def attend(q_ref, k_ref, v_ref, mixed_ref, lse_ref, length, causal):
    seq, width = q_ref.shape
    keys = k_ref.shape[0]
    heads = width // HEAD_DIM
    value_t = jnp.transpose(v_ref[...])
    for row0 in range(0, seq, BLOCK):
        query = q_ref[row0 : row0 + BLOCK, :]
        tiles = key_tiles(keys, row0 + BLOCK if causal else keys)
        columns = []
        for head in range(heads):
            own = heads_only(query, head, heads)
            scores = [scores_tile(k_ref, own, at, w, row0, length, causal) for at, w in tiles]
            peak = functools.reduce(
                jnp.maximum, [jnp.max(s, axis=0, keepdims=True) for s in scores]
            )
            total = jnp.zeros_like(peak)
            mixed = jnp.zeros((HEAD_DIM, BLOCK), F32)
            for (at, w), s in zip(tiles, scores):
                raised = jnp.exp(s - peak)
                total = total + jnp.sum(raised, axis=0, keepdims=True)
                rows = value_t[head * HEAD_DIM : (head + 1) * HEAD_DIM, at : at + w]
                mixed = mixed + nn(rows, raised.astype(BF16))
            columns.append(mixed * (1.0 / total))
            lse_ref[head : head + 1, row0 : row0 + BLOCK] = peak + jnp.log(total)
        mixed_ref[row0 : row0 + BLOCK, :] = jnp.transpose(jnp.concatenate(columns, 0)).astype(BF16)


def attend_back(q_ref, k_ref, v_ref, up_ref, lse_ref, dq_ref, dk_acc, dv_acc, length, causal):
    seq, width = q_ref.shape
    keys = k_ref.shape[0]
    heads = width // HEAD_DIM
    key_t = jnp.transpose(k_ref[...])
    dk_acc[...] = jnp.zeros_like(dk_acc)
    dv_acc[...] = jnp.zeros_like(dv_acc)
    for row0 in range(0, seq, BLOCK):
        query = q_ref[row0 : row0 + BLOCK, :]
        upstream = up_ref[row0 : row0 + BLOCK, :]
        tiles = key_tiles(keys, row0 + BLOCK if causal else keys)
        columns = []
        for head in range(heads):
            own = heads_only(query, head, heads)
            own_up = heads_only(upstream, head, heads)
            lse = lse_ref[head : head + 1, row0 : row0 + BLOCK]
            weights, grads = [], []
            inner = jnp.zeros((1, BLOCK), F32)
            for at, w in tiles:
                weight = jnp.exp(scores_tile(k_ref, own, at, w, row0, length, causal) - lse)
                grad = nt(v_ref[at : at + w, :], own_up)
                inner = inner + jnp.sum(weight * grad, axis=0, keepdims=True)
                weights.append(weight)
                grads.append(grad)
            column = jnp.zeros((HEAD_DIM, BLOCK), F32)
            for (at, w), weight, grad in zip(tiles, weights, grads):
                score_grad = (weight * (grad - inner)).astype(BF16)
                dv_acc[at : at + w, :] += nn(weight.astype(BF16), own_up)
                dk_acc[at : at + w, :] += nn(score_grad, own)
                rows = key_t[head * HEAD_DIM : (head + 1) * HEAD_DIM, at : at + w]
                column = column + nn(rows, score_grad)
            columns.append(column * FACTOR)
        dq_ref[row0 : row0 + BLOCK, :] = jnp.transpose(jnp.concatenate(columns, 0)).astype(BF16)


def self_forward(chips, ids, *refs):
    parts = refs[: 2 * chips]
    gain, shift, wqkv, bias, x_ref, h_ref, qkv_ref, mixed_ref, lse_ref = refs[2 * chips :]
    core, chip = ids[0] % 2, ids[0] // 2
    own = parts[0].shape[0]
    for mask in range(chips):
        lo, hi = ordered(core, parts[2 * mask][...], parts[2 * mask + 1][...])
        rows = jnp.concatenate([lo, hi], 0)
        at = pl.ds(pl.multiple_of((chip ^ mask) * 2 * own, 2 * own), 2 * own)
        x_ref[at, :] = rows
        hat, _ = normed(rows.astype(F32))
        hidden = (hat * row_of(gain, 0) + row_of(shift, 0)).astype(BF16)
        h_ref[at, :] = hidden
        query = nn(hidden, wqkv[0]) + row_of(bias, 0)
        qkv_ref[0, at, :] = (query.astype(BF16).astype(F32) * FACTOR).astype(BF16)
        qkv_ref[1, at, :] = nn(hidden, wqkv[1]).astype(BF16)
        qkv_ref[2, at, :] = (nn(hidden, wqkv[2]) + row_of(bias, 1)).astype(BF16)
    attend(qkv_ref.at[0], qkv_ref.at[1], qkv_ref.at[2], mixed_ref, lse_ref, None, True)


def project_pairs(parts, mine, other, first, rows):
    width = parts[0].shape[1]
    total = None
    for mask in range(len(parts) // 2):
        lhs = [parts[2 * mask][rows, :], parts[2 * mask + 1][rows, :]]
        rhs = [ref[mask, first : first + width, :] for ref in (mine, other)]
        if width % 128 == 0:
            term = nn(jnp.concatenate(lhs, 1), jnp.concatenate(rhs, 0))
        else:
            term = nn(lhs[0], rhs[0]) + nn(lhs[1], rhs[1])
        total = term if total is None else total + term
    return total


def turned_place(mask, chips):
    bits = chips.bit_length() - 1
    return sum(((mask >> i) & 1) << (bits - 1 - i) for i in range(bits))


def pack(former, latter, out):
    count = former.shape[0]
    out[:count] = former[...]
    out[count:] = latter[...]


def cross_forward(chips, length, *refs):
    parts, wout = refs[: 2 * chips], refs[2 * chips : 2 * chips + 2]
    (x_ref, gain, shift, out_bias, wq, bias, mk, mv) = refs[2 * chips + 2 : 2 * chips + 10]
    s2_ref, h_ref, q_ref, mixed_ref, lse_ref = refs[2 * chips + 10 :]
    for row0 in range(0, x_ref.shape[0], BLOCK):
        rows = pl.ds(row0, BLOCK)
        branch = project_pairs(parts, *wout, 0, rows) + row_of(out_bias, 0)
        stream = x_ref[rows, :].astype(F32) + branch
        s2_ref[rows, :] = stream
        hat, _ = normed(stream)
        hidden = (hat * row_of(gain, 1) + row_of(shift, 1)).astype(BF16)
        h_ref[rows, :] = hidden
        query = (nn(hidden, wq[...]) + row_of(bias, 0)).astype(BF16).astype(F32)
        q_ref[rows, :] = (query * FACTOR).astype(BF16)
    attend(q_ref, mk, mv, mixed_ref, lse_ref, length[0], False)


def mlp(chips, ids, *refs):
    parts, wout = refs[: 2 * chips], refs[2 * chips : 2 * chips + 2]
    grad_in, grad_other = refs[2 * chips + 2 : 2 * chips + 4]
    (s2_ref, gain, shift, out_bias, wup, bup, wdown) = refs[2 * chips + 4 : 2 * chips + 11]
    s3_own, h_ref, act_ref, pg_ref, g_ref, sums, ups, s3 = refs[2 * chips + 11 :]
    core, chip = ids[0] % 2, ids[0] // 2
    own = s3_own.shape[0]
    sums[...] = jnp.zeros_like(sums[...])
    ups[...] = jnp.zeros_like(ups[...])
    for mask in range(chips):
        rows = pl.ds(pl.multiple_of((chip ^ mask) * 2 * own, 2 * own), 2 * own)
        branch = project_pairs(parts, *wout, 0, rows) + row_of(out_bias, 1)
        stream = s2_ref[rows, :] + branch
        if mask == 0:
            s3[...] = stream
            s3_own[...] = s3[pl.ds(pl.multiple_of(core * own, own), own), :]
        hat, _ = normed(stream)
        hidden = (hat * row_of(gain, 2) + row_of(shift, 2)).astype(BF16)
        h_ref[rows, :] = hidden
        pre = nn(hidden, wup[...]) + bup[...].astype(F32)
        half = 0.5 * (1.0 + lax.erf(pre * (0.5**0.5)))
        act_ref[rows, :] = (pre * half).astype(BF16)
        slope = half + pre * jnp.exp(-0.5 * pre * pre) * 0.3989422804014327
        lo, hi = ordered(core, grad_in[turned_place(mask, chips)], grad_other[turned_place(mask, chips)])
        grad = jnp.concatenate([lo, hi], 0)
        g_ref[rows, :] = grad
        pre_grad = (nt(grad, wdown[...]) * slope).astype(BF16)
        pg_ref[rows, :] = pre_grad
        ups[...] += jnp.sum(pre_grad.astype(F32), axis=0, keepdims=True)
        sums[...] += jnp.sum(grad.astype(F32), axis=0, keepdims=True)


def rows_for(ref, chip, core, own, chips):
    picks = []
    for mask in range(chips):
        at = pl.multiple_of(((chip ^ mask) * 2 + core) * own, own)
        picks.append(ref[pl.ds(at, own), :])
    return jnp.concatenate(picks, 0)


def picked_terms(lhs, rhs, dot, chip, core, own, chips):
    total = None
    for i in range(lhs.shape[0]):
        term = dot(rows_for(lhs.at[i], chip, core, own, chips), rhs[i])
        total = term if total is None else total + term
    return total


def partial_sibling(chips, dot, ids, lhs, rhs, *outs):
    own = outs[0].shape[0]
    total = picked_terms(lhs, rhs, dot, ids[0] // 2, 1 - ids[0] % 2, own, chips)
    for mask in range(chips):
        outs[mask][...] = total[mask * own : (mask + 1) * own].astype(BF16)


def partial_own(chips, dot, ids, lhs, rhs, *refs):
    got, first, sends = refs[:chips], refs[chips], refs[chips + 1 :]
    own = first.shape[0]
    total = picked_terms(lhs, rhs, dot, ids[0] // 2, ids[0] % 2, own, chips)
    for mask in list(range(1, chips)) + [0]:
        block = total[mask * own : (mask + 1) * own] + got[mask][...].astype(F32)
        if mask == 0:
            first[...] = block
        else:
            sends[mask - 1][...] = block.astype(BF16)


def last_sibling(chips, ids, act, wdown, wkv, dkv, norm, *outs):
    own, wide = act.shape[0] // (2 * chips), wdown.shape[1]
    chip, core = ids[0] // 2, 1 - ids[0] % 2
    total = nn(rows_for(act, chip, core, own, chips), wdown[...])
    turned_grad = picked_terms(wkv, dkv, nt, chip, core, own, chips)
    for mask in range(chips):
        rows = slice(mask * own, (mask + 1) * own)
        out = outs[mask]
        out[:own, :wide] = total[rows].astype(BF16)
        out[:own, wide:] = turned_grad[rows].astype(BF16)
        out[own:, :wide] = norm[...].astype(BF16)
        out[own:, wide:] = jnp.zeros_like(out[own:, wide:])


def last_own(chips, ids, act, wdown, wkv, dkv, norm, *refs):
    parts, first, sends = refs[:chips], refs[chips], refs[chips + 1 :]
    own, wide = act.shape[0] // (2 * chips), wdown.shape[1]
    chip, core = ids[0] // 2, ids[0] % 2
    total = nn(rows_for(act, chip, core, own, chips), wdown[...])
    turned_grad = picked_terms(wkv, dkv, nt, chip, core, own, chips)
    for mask in range(chips):
        rows = slice(mask * own, (mask + 1) * own)
        out = first if mask == 0 else sends[mask - 1]
        got = parts[mask][...].astype(F32)
        out[:own, :wide] = (total[rows] + got[:own, :wide]).astype(out.dtype)
        out[:own, wide:] = (turned_grad[rows] + got[:own, wide:]).astype(out.dtype)
        out[own:, :wide] = (norm[...] + got[own:, :wide]).astype(out.dtype)
        out[own:, wide:] = jnp.zeros_like(out[own:, wide:])


def last_final(chips, *refs):
    parts = refs[:chips]
    stream, bias, self_sums, cross_sums, grad_sum, self_bias, cross_bias, up_bias = refs[
        chips : chips + 8
    ]
    out, memory, small = refs[chips + 8 :]
    own, wide = out.shape
    total = parts[0][...]
    for part in parts[1:]:
        total = total + part[...].astype(F32)
    out[...] = (total[:own, :wide] + stream[...] + row_of(bias, 2)).astype(BF16)
    memory[...] = jnp.transpose(total[:own, wide:])[: memory.shape[0]]
    small[...] = total[own:, :wide]
    small[2:5, :] = self_sums[...]
    small[5:8, :] = cross_sums[...]
    small[8:9, :] = grad_sum[...]
    width = self_bias.shape[1]
    for i in range(2):
        small[9 + i : 10 + i, :width] = self_bias[i : i + 1, :]
        small[11 + i : 12 + i, :width] = cross_bias[i : i + 1, :]
    small[13:14, : up_bias.shape[1]] = up_bias[...]


def small_final(*refs):
    parts, (gains, shifts, outs, self_bias, cross_bias, up_bias) = refs[:-6], refs[-6:]
    total = parts[0][...]
    for part in parts[1:]:
        total = total + part[...]
    for i, (gain, shift, out) in enumerate(((0, 1, 4), (2, 3, 7), (5, 6, 8))):
        gains[i : i + 1, :] = total[gain : gain + 1]
        shifts[i : i + 1, :] = total[shift : shift + 1]
        outs[i : i + 1, :] = total[out : out + 1]
    width = self_bias.shape[1]
    self_bias[...] = total[9:11, :width]
    cross_bias[...] = total[11:13, :width]
    up_bias[...] = total[13:14, : up_bias.shape[1]]


def stacked(values, block):
    return jnp.concatenate(
        [values[:, at : at + block] for at in range(0, values.shape[1], block)], 0
    )


def turned(lhs, rhs):
    return nn(jnp.transpose(lhs), rhs).astype(BF16)


def split_bucket(role, columns, keep, send):
    half = keep.shape[0]
    for at, block in columns:
        top, bottom = block[:half], block[half:]
        width = block.shape[1]
        keep[:, at : at + width] = jnp.where(role[0] == 0, top, bottom)
        send[:, at : at + width] = jnp.where(role[0] == 0, bottom, top)


def mlp_bucket(role, act, grad, hidden, pre_grad, keep, send):
    down = stacked(turned(act[...], grad[...]), act.shape[1])
    up = jnp.transpose(turned(pre_grad[...], hidden[...]))
    keep[...] = jnp.where(role[0] == 0, down, up)
    send[...] = jnp.where(role[0] == 0, up, down)


def cross_bucket(role, hidden, dq, padded, dkv, mixed, grad, keep, send):
    width = dq.shape[1]
    columns = [(0, jnp.transpose(turned(dq[...], hidden[...])))]
    for i in range(2):
        columns.append(((1 + i) * width, jnp.transpose(turned(dkv[i], padded[...]))))
    columns.append((3 * width, stacked(turned(mixed[...], grad[...]), width)))
    split_bucket(role, columns, keep, send)


def self_bucket(role, hidden, grads, mixed, grad, keep, send):
    width = mixed.shape[1]
    columns = []
    for i in range(3):
        columns.append((i * width, jnp.transpose(turned(grads[i], hidden[...]))))
    columns.append((3 * width, stacked(turned(mixed[...], grad[...]), width)))
    split_bucket(role, columns, keep, send)


def add_halves(former, latter, out):
    out[...] = (former[...].astype(F32) + latter[...].astype(F32)).astype(BF16)


def whole_bucket(role, total, other):
    mine, theirs = total[...].astype(F32), other[...].astype(F32)
    return jnp.concatenate(
        [jnp.where(role[0] == 0, mine, theirs), jnp.where(role[0] == 0, theirs, mine)], 0
    )


def mlp_final(role, total, other, out_down, out_up):
    mine, theirs = total[...].astype(F32), other[...].astype(F32)
    down = jnp.where(role[0] == 0, mine, theirs)
    out_up[...] = jnp.where(role[0] == 0, theirs, mine)
    rows = out_down.shape[0]
    for at in range(0, out_down.shape[1], rows):
        out_down[:, at : at + rows] = down[at : at + rows]


def cross_final(role, total, other, out_q, out_kv, out_o):
    width = out_q.shape[1]
    whole = whole_bucket(role, total, other)
    out_q[...] = whole[:, :width]
    out_kv[0] = whole[:, width : 2 * width]
    out_kv[1] = whole[:, 2 * width : 3 * width]
    for at in range(0, out_o.shape[1], width):
        out_o[:, at : at + width] = whole[at : at + width, 3 * width :]


def self_final(role, total, other, out_qkv, out_o):
    width = out_o.shape[0]
    whole = whole_bucket(role, total, other)
    for i in range(3):
        out_qkv[i] = whole[:, i * width : (i + 1) * width]
    for at in range(0, out_o.shape[1], width):
        out_o[:, at : at + width] = whole[at : at + width, 3 * width :]


def prepare(memory, wkv, bias, wq, padded, mk, mv, wq_t):
    rows = memory.shape[0]
    whole = -(-rows // 16) * 16
    if rows < mk.shape[0]:
        padded[whole - 16 :, :] = jnp.zeros((padded.shape[0] - whole + 16, padded.shape[1]), BF16)
    padded[0:rows, :] = memory[...]
    mk[...] = nn(padded[...], wkv[0]).astype(BF16)
    mv[...] = (nn(padded[...], wkv[1]) + row_of(bias, 1)).astype(BF16)
    wq_t[...] = jnp.transpose(wq[...])


def three_back(chips, *refs):
    first = refs[0]
    got = refs[1:chips]
    s3, gain, g_own, resid, message = refs[chips:]
    own = first.shape[0]
    total = first[...]
    for part in got:
        total = total + part[...].astype(F32)
    back, hat = norm_back(s3[...], row_of(gain, 2), total)
    grad = g_own[...].astype(F32) + back
    resid[...] = grad
    message[0:own, :] = grad.astype(BF16)
    sums = jnp.concatenate(
        [
            jnp.sum(total * hat, axis=0, keepdims=True),
            jnp.sum(total, axis=0, keepdims=True),
            jnp.zeros((14, total.shape[1]), F32),
        ],
        0,
    )
    message[own : own + 16, :] = sums.astype(BF16)


def cross_back(chips, ids, length, *refs):
    parts = refs[: 2 * chips]
    wout, q_ref, mk, mv, lse = refs[2 * chips : 2 * chips + 5]
    cg_ref, sums, dq_ref, dkv_ref, biases = refs[2 * chips + 5 : 2 * chips + 10]
    up_ref, dk_acc, dv_acc = refs[2 * chips + 10 :]
    core, chip = ids[0] % 2, ids[0] // 2
    own = parts[0].shape[0] - 16
    norm_sums = jnp.zeros((2, cg_ref.shape[1]), F32)
    bias_sum = jnp.zeros((1, cg_ref.shape[1]), F32)
    for mask in range(chips):
        lo, hi = ordered(core, parts[2 * mask][...], parts[2 * mask + 1][...])
        norm_sums = norm_sums + lo[own : own + 2].astype(F32) + hi[own : own + 2].astype(F32)
        rows = jnp.concatenate([lo[:own], hi[:own]], 0)
        at = pl.ds(pl.multiple_of((chip ^ mask) * 2 * own, 2 * own), 2 * own)
        cg_ref[at, :] = rows
        bias_sum = bias_sum + jnp.sum(rows.astype(F32), axis=0, keepdims=True)
        up_ref[at, :] = nt(rows, wout[...]).astype(BF16)
    sums[...] = jnp.concatenate([norm_sums, bias_sum], 0)
    attend_back(q_ref, mk, mv, up_ref, lse, dq_ref, dk_acc, dv_acc, length[0], False)
    dkv_ref[0] = dk_acc[...].astype(BF16)
    dv = dv_acc[...].astype(BF16)
    dkv_ref[1] = dv
    biases[0:1, :] = jnp.sum(dq_ref[...].astype(F32), axis=0, keepdims=True)
    biases[1:2, :] = jnp.sum(dv.astype(F32), axis=0, keepdims=True)


def self_upstream(chips, ids, *refs):
    parts, wq = refs[: 2 * chips], refs[2 * chips : 2 * chips + 2]
    (s2_ref, gain, cg_ref, resid_two, wout) = refs[2 * chips + 2 : 2 * chips + 7]
    sg_ref, resid_one, sums, up_ref, base = refs[2 * chips + 7 :]
    own = resid_two.shape[0]
    mine = pl.ds(pl.multiple_of(ids[0] * own, own), own)
    base[...] = cg_ref[...].astype(F32)
    base[mine, :] = resid_two[...]
    sums[...] = jnp.zeros_like(sums[...])
    for row0 in range(0, s2_ref.shape[0], BLOCK):
        rows = pl.ds(row0, BLOCK)
        upstream = project_pairs(parts, *wq, 0, rows)
        back, hat = norm_back(s2_ref[rows, :], row_of(gain, 1), upstream)
        grad = base[rows, :] + back
        base[rows, :] = grad
        rounded = grad.astype(BF16)
        sg_ref[rows, :] = rounded
        sums[0:1, :] += jnp.sum(upstream * hat, axis=0, keepdims=True)
        sums[1:2, :] += jnp.sum(upstream, axis=0, keepdims=True)
        sums[2:3, :] += jnp.sum(rounded.astype(F32), axis=0, keepdims=True)
        up_ref[rows, :] = nt(rounded, wout[...]).astype(BF16)
    resid_one[...] = base[mine, :]


def self_back(qkv, up_ref, lse, grads, biases, dk_acc, dv_acc):
    attend_back(
        qkv.at[0], qkv.at[1], qkv.at[2], up_ref, lse, grads.at[0], dk_acc, dv_acc, None, True
    )
    grads[1] = dk_acc[...].astype(BF16)
    grads[2] = dv_acc[...].astype(BF16)
    biases[0:1, :] = jnp.sum(grads[0].astype(F32), axis=0, keepdims=True)
    biases[1:2, :] = jnp.sum(grads[2].astype(F32), axis=0, keepdims=True)


def first_norm_sums(x_ref, grads, wqkv, sums):
    sums[...] = jnp.zeros_like(sums[...])
    for row0 in range(0, x_ref.shape[0], BLOCK):
        rows = pl.ds(row0, BLOCK)
        upstream = sum(nt(grads[i, rows, :], wqkv[i]) for i in range(3))
        hat, _ = normed(x_ref[rows, :].astype(F32))
        sums[0:1, :] += jnp.sum(upstream * hat, axis=0, keepdims=True)
        sums[1:2, :] += jnp.sum(upstream, axis=0, keepdims=True)


def one_back(chips, *refs):
    first = refs[0]
    got = refs[1:chips]
    x_own, gain, resid, out = refs[chips:]
    total = first[...]
    for part in got:
        total = total + part[...].astype(F32)
    back, _ = norm_back(x_own[...].astype(F32), row_of(gain, 0), total)
    out[...] = resid[...] + back


def on_device(
    layer_input,
    output_grad,
    memory,
    memory_length,
    norm_gain,
    norm_bias,
    self_qkv,
    self_bias,
    self_out,
    cross_query,
    cross_kv,
    cross_bias,
    cross_out,
    up_weight,
    up_bias,
    down_weight,
    out_bias,
):
    ranks = lax.axis_size("tensor")
    pages_ranks = lax.axis_size("dp")
    chips = ranks // 2
    rank = lax.axis_index("tensor")
    own, wide = layer_input.shape
    seq = own * ranks
    width = self_qkv.shape[2]
    heads = width // HEAD_DIM
    hidden = up_bias.shape[0]
    mem = memory.shape[0]
    mem_pad = -(-mem // 128) * 128

    line = lax.axis_index("dp")
    ids = jnp.reshape(rank, (1,)).astype(jnp.int32)
    role = jnp.reshape((line ^ (line >> 1)) & 1, (1,)).astype(jnp.int32)

    def swap(values, mask):
        return lax.ppermute(values, "tensor", [(i, i ^ mask) for i in range(ranks)])

    def far_parts(values):
        return [values] + [swap(values, 2 * mask) for mask in range(1, chips)]

    def hold(values, *tokens):
        return lax.optimization_barrier((values, *tokens))[0]

    def near_parts(far):
        return [part for block in far for part in (block, swap(block, 1))]

    def joined(former, latter, after):
        shape = (2 * former.shape[0], *former.shape[1:])
        return call(pack, [sds(shape, BF16)], [former, latter], after=after)[0]

    turns = [1 << at for at in range(1, ranks.bit_length() - 1)]

    def gather(values):
        return near_parts(far_parts(values))

    def along(values, pairs):
        return lax.ppermute(
            values,
            "dp",
            [(at + a, at + b) for at in range(0, pages_ranks, 4) for a, b in pairs],
        )

    outer = [(0, 1), (1, 0), (2, 3), (3, 2)]
    middle = [(0, 3), (3, 0), (1, 2), (2, 1)]
    def bucket(body, rows, ins, flops, after):
        half = sds((rows, 4 * width), BF16)
        keep, send = call(body, [half, half], [role, *ins], flops, after=after)
        return keep, along(send, outer)

    def across(state, after):
        keep, got = state
        inner = call(add_halves, [sds(keep.shape, BF16)], [keep, got], after=after)[0]
        return inner, along(inner, middle)

    def back_out(state, after):
        inner, got = state
        half = sds(inner.shape, BF16)
        total = call(add_halves, [half], [inner, got], after=after)[0]
        mask = 4
        while mask < pages_ranks:
            pairs = [(i, i ^ mask) for i in range(pages_ranks)]
            total = call(add_halves, [half], [total, lax.ppermute(total, "dp", pairs)])[0]
            mask *= 2
        return total, along(total, outer)

    def sibling_terms(lhs, rhs, dot, after):
        rows = lhs.shape[1] // ranks
        columns = rhs.shape[1 if dot is nt else 2]
        return call(
            functools.partial(partial_sibling, chips, dot),
            [sds((rows, columns), BF16)] * chips,
            [ids, lhs, rhs],
            lhs.size * columns,
            after=after,
        )

    def own_terms(lhs, rhs, dot, got, after):
        rows, columns = got[0].shape
        return call(
            functools.partial(partial_own, chips, dot),
            [sds((rows, columns), F32)] + [sds((rows, columns), BF16)] * (chips - 1),
            [ids, lhs, rhs, *got],
            lhs.size * columns,
            after=after,
        )

    def scatter_far(sums):
        return [sums[0]] + [swap(sums[mask], 2 * mask) for mask in range(1, chips)]

    x_far = far_parts(layer_input)
    padded, mem_keys, mem_values, query_t = call(
        prepare,
        [
            sds((mem_pad, wide), BF16),
            sds((mem_pad, width), BF16),
            sds((mem_pad, width), BF16),
            sds((width, wide), BF16),
        ],
        [memory, cross_kv, cross_bias, cross_query],
        4 * mem_pad * wide * width,
    )
    x_far = [layer_input] + [hold(part, mem_keys) for part in x_far[1:]]
    so_block, co_block, g_block = self_out[None], cross_out[None], output_grad[None]
    so_got = swap(so_block, turns[0])
    x_parts = near_parts(x_far)
    co_got, g_got = swap(co_block, turns[0]), swap(g_block, turns[-1])
    so_block = joined(so_block, so_got, [mem_keys, *x_far[1:]])
    so_got = swap(so_block, turns[1])
    x, hidden_one, qkv, self_mixed, self_lse = call(
        functools.partial(self_forward, chips),
        [
            sds((seq, wide), BF16),
            sds((seq, wide), BF16),
            sds((3, seq, width), BF16),
            sds((seq, width), BF16),
            sds((heads, seq), F32),
        ],
        [ids, *x_parts, norm_gain, norm_bias, self_qkv, self_bias],
        2 * seq * wide * 3 * width + 4 * seq * seq * width,
        after=[so_block],
    )
    co_block = joined(co_block, co_got, [self_mixed])
    g_block = joined(g_block, g_got, [co_block])
    mixed_far = far_parts(hold(self_mixed, g_block))
    so_block = joined(so_block, so_got, mixed_far[1:])
    for mask in turns[2:]:
        so_block = joined(so_block, swap(so_block, mask), [])
    so_other = swap(so_block, 1)
    mixed_parts = near_parts(mixed_far)
    co_got = swap(hold(co_block, *mixed_far[1:]), turns[1])
    g_got = swap(hold(g_block, *mixed_far[1:]), turns[-2])
    stream_two, hidden_two, cross_q, cross_mixed, cross_lse = call(
        functools.partial(cross_forward, chips),
        [
            sds((seq, wide), F32),
            sds((seq, wide), BF16),
            sds((seq, width), BF16),
            sds((seq, width), BF16),
            sds((heads, seq), F32),
        ],
        [
            memory_length,
            *mixed_parts,
            so_block,
            so_other,
            x,
            norm_gain,
            norm_bias,
            out_bias,
            cross_query,
            cross_bias,
            mem_keys,
            mem_values,
        ],
        2 * seq * wide * (wide + width) + 4 * seq * mem_pad * width,
        after=[g_block],
    )
    cross_far = far_parts(cross_mixed)
    co_block = joined(co_block, co_got, cross_far[1:])
    g_block = joined(g_block, g_got, [co_block])
    for at in range(2, len(turns)):
        co_block = joined(co_block, swap(co_block, turns[at]), [])
        g_block = joined(g_block, swap(g_block, turns[-1 - at]), [])
    co_other, g_other = swap(co_block, 1), swap(g_block, 1)
    cross_parts = near_parts(cross_far)
    wq_block = hold(query_t, *cross_far[1:])[None]
    wq_got = swap(wq_block, turns[0])
    stream_three, hidden_three, activated, pre_grad, whole_grad, grad_sum, up_bias_grad = call(
        functools.partial(mlp, chips),
        [
            sds((own, wide), F32),
            sds((seq, wide), BF16),
            sds((seq, hidden), BF16),
            sds((seq, hidden), BF16),
            sds((seq, wide), BF16),
            sds((1, wide), F32),
            sds((1, hidden), F32),
        ],
        [
            ids,
            *cross_parts,
            co_block,
            co_other,
            g_block,
            g_other,
            stream_two,
            norm_gain,
            norm_bias,
            out_bias,
            up_weight,
            up_bias.reshape(1, -1),
            down_weight,
        ],
        2 * seq * wide * (wide + 2 * hidden),
        [pltpu.VMEM((2 * own, wide), F32)],
    )
    up_item, pre_item = up_weight[None], pre_grad[None]
    sibling = sibling_terms(pre_item, up_item, nt, [])
    got = [swap(part, 1) for part in sibling]
    both = bucket(
        mlp_bucket,
        wide,
        [activated, whole_grad, hidden_three, pre_grad],
        4 * seq * wide * hidden,
        [sibling[0]],
    )
    wq_block = joined(wq_block, wq_got, [both[0]])
    three_sums = own_terms(pre_item, up_item, nt, got, [wq_block])
    three_far = scatter_far(three_sums)
    resid_two, message = call(
        functools.partial(three_back, chips),
        [sds((own, wide), F32), sds((own + 16, wide), BF16)],
        [*three_far, stream_three, norm_gain, output_grad],
    )
    cg_far = far_parts(message)
    cg_parts = near_parts(cg_far)
    both = across(both, cg_far[1:])
    wq_got = swap(hold(wq_block, *cg_far[1:]), turns[1])
    cross_grad, cross_sums, dq2, dkv2, cross_bias_grad = call(
        functools.partial(cross_back, chips),
        [
            sds((seq, wide), BF16),
            sds((3, wide), F32),
            sds((seq, width), BF16),
            sds((2, mem_pad, width), BF16),
            sds((2, width), F32),
        ],
        [
            ids,
            memory_length,
            *cg_parts,
            cross_out,
            cross_q,
            mem_keys,
            mem_values,
            cross_lse,
        ],
        2 * seq * wide * width + 10 * seq * mem_pad * width,
        [
            pltpu.VMEM((seq, width), BF16),
            pltpu.VMEM((mem_pad, width), F32),
            pltpu.VMEM((mem_pad, width), F32),
        ],
        after=[both[0]],
    )
    dq2_far = far_parts(dq2)
    cross = bucket(
        cross_bucket,
        wide // 2,
        [hidden_two, dq2, padded, dkv2, cross_mixed, cross_grad],
        8 * seq * wide * width,
        [dq2],
    )
    wq_block = joined(wq_block, wq_got, [cross[0], *dq2_far[1:]])
    for mask in turns[2:]:
        wq_block = joined(wq_block, swap(wq_block, mask), [])
    wq_other = swap(wq_block, 1)
    dq2_parts = near_parts(dq2_far)
    self_grad, resid_one, self_sums, self_up = call(
        functools.partial(self_upstream, chips),
        [
            sds((seq, wide), BF16),
            sds((own, wide), F32),
            sds((3, wide), F32),
            sds((seq, width), BF16),
        ],
        [
            ids,
            *dq2_parts,
            wq_block,
            wq_other,
            stream_two,
            norm_gain,
            cross_grad,
            resid_two,
            self_out,
        ],
        2 * seq * wide * (wide + width),
        [pltpu.VMEM((seq, wide), F32)],
    )
    grads, self_bias_grad = call(
        self_back,
        [sds((3, seq, width), BF16), sds((2, width), F32)],
        [qkv, self_up, self_lse],
        10 * seq * seq * width,
        [pltpu.VMEM((seq, width), F32), pltpu.VMEM((seq, width), F32)],
    )
    sibling = sibling_terms(grads, self_qkv, nt, [])
    got = [swap(part, 1) for part in sibling]
    cross = across(cross, [sibling[0]])
    attn = bucket(
        self_bucket, wide // 2, [hidden_one, grads, self_mixed, self_grad], 8 * seq * wide * width, [cross[0]]
    )
    one_sums = own_terms(grads, self_qkv, nt, got, [attn[0]])
    one_far = scatter_far(one_sums)
    norm_sums = call(
        first_norm_sums,
        [sds((16, wide), F32)],
        [x, grads, self_qkv],
        6 * seq * wide * width,
        after=[one_sums[0]],
    )[0]
    last_ins = [ids, activated, down_weight, cross_kv, dkv2, norm_sums]
    sibling = call(
        functools.partial(last_sibling, chips),
        [sds((own + 16, wide + mem_pad), BF16)] * chips,
        last_ins,
    )
    got = [swap(part, 1) for part in sibling]
    (input_grad,) = call(
        functools.partial(one_back, chips),
        [sds((own, wide), F32)],
        [*one_far, layer_input, norm_gain, resid_one],
        after=[sibling[0]],
    )
    attn = across(attn, [input_grad])
    both = back_out(both, [attn[0]])
    last = call(
        functools.partial(last_own, chips),
        [sds((own + 16, wide + mem_pad), F32)]
        + [sds((own + 16, wide + mem_pad), BF16)] * (chips - 1),
        [*last_ins, *got],
        after=[both[0]],
    )
    last_far = scatter_far(last)
    cross = back_out(cross, [last[0]])
    output, memory_grad, small = call(
        functools.partial(last_final, chips),
        [
            sds((own, wide), BF16),
            sds((mem, wide // ranks), F32),
            sds((16, wide), F32),
        ],
        [
            *last_far,
            stream_three,
            out_bias,
            self_sums,
            cross_sums,
            grad_sum,
            self_bias_grad,
            cross_bias_grad,
            up_bias_grad,
        ],
        after=[cross[0]],
    )
    small_parts = [small] + [
        lax.ppermute(small, "dp", [(i, (i + step) % pages_ranks) for i in range(pages_ranks)])
        for step in range(1, pages_ranks)
    ]
    attn = back_out(attn, [small])
    down_grad, up_grad = call(
        mlp_final,
        [sds((hidden, wide), F32), sds((wide, hidden), F32)],
        [role, *both],
        after=[attn[0]],
    )
    cross_query_grad, cross_kv_grad, cross_out_grad = call(
        cross_final,
        [sds((wide, width), F32), sds((2, wide, width), F32), sds((width, wide), F32)],
        [role, *cross],
        after=[down_grad],
    )
    gains, shifts, outs, self_bias_sum, cross_bias_sum, up_bias_sum = call(
        small_final,
        [sds((3, wide), F32)] * 3
        + [sds((2, width), F32), sds((2, width), F32), sds((1, hidden), F32)],
        small_parts,
        after=[cross_query_grad],
    )
    self_qkv_grad, self_out_grad = call(
        self_final,
        [sds((3, wide, width), F32), sds((width, wide), F32)],
        [role, *attn],
        after=[gains],
    )
    return (
        output,
        input_grad,
        memory_grad,
        gains,
        shifts,
        self_qkv_grad,
        self_bias_sum,
        self_out_grad,
        cross_query_grad,
        cross_kv_grad,
        cross_bias_sum,
        cross_out_grad,
        up_grad,
        up_bias_sum.reshape(-1),
        down_grad,
        outs,
    )


def solution(mesh):
    return jax.shard_map(
        on_device,
        mesh=mesh,
        in_specs=(
            P(("dp", "tensor"), None),
            P(("dp", "tensor"), None),
            P("dp", None),
            P("dp"),
            P(),
            P(),
            P(None, None, "tensor"),
            P(None, "tensor"),
            P("tensor", None),
            P(None, "tensor"),
            P(None, None, "tensor"),
            P(None, "tensor"),
            P("tensor", None),
            P(None, "tensor"),
            P("tensor"),
            P("tensor", None),
            P(),
        ),
        out_specs=(
            P(("dp", "tensor"), None),
            P(("dp", "tensor"), None),
            P("dp", "tensor"),
            P(),
            P(),
            P(None, None, "tensor"),
            P(None, "tensor"),
            P("tensor", None),
            P(None, "tensor"),
            P(None, None, "tensor"),
            P(None, "tensor"),
            P("tensor", None),
            P(None, "tensor"),
            P("tensor"),
            P("tensor", None),
            P(),
        ),
        check_vma=False,
    )
```

```python
import functools

import jax
import jax.numpy as jnp
from jax import lax
from jax.experimental import pallas as pl
from jax.experimental.pallas import tpu as pltpu
from jax.sharding import PartitionSpec as P

HEAD_DIM = 64
EPS = 1e-05
NEG = -1e30
BLOCK = 256
FACTOR = HEAD_DIM ** (-0.5)
F32 = jnp.float32
BF16 = jnp.bfloat16

def nn(a, b):
    return lax.dot_general(a, b, (((1,), (0,)), ((), ())), preferred_element_type=F32)


def nt(a, b):
    return lax.dot_general(a, b, (((1,), (1,)), ((), ())), preferred_element_type=F32)


SLOTS = {
    "x": ["so1"],
    "self": ["co1", "g1"],
    "mixed": ["so2"],
    "cross": ["co2", "g2"],
    "mlp": [],
    "three": ["wq1"],
    "three far": ["bucket m"],
    "grad far": ["wq2", "add m"],
    "query far": ["bucket c"],
    "up": [],
    "back": [],
    "one": ["out m", "bucket a"],
    "one far": ["add c", "norm"],
    "input": ["add a", "out c"],
    "last": [],
    "last far": ["final m"],
    "end": ["out a", "final c"],
}
BASE = {"mixed": 2, "cross": 2, "grad far": 2, "query far": 2}
NEAR = {}
LOAD = {"three_back": 4}
UNIT = 1.8e9
WEIGHT = 0.12


def call(body, outs, ins, flops=0, scratch=(), after=(), vmem=8):
    inside = pl.BlockSpec(memory_space=pltpu.VMEM)
    scalar = pl.BlockSpec(memory_space=pltpu.SMEM)
    count, tokens = len(ins), len(after)
    name = getattr(body, "func", body).__name__
    nbytes = sum(a.size * a.dtype.itemsize for a in ins)
    nbytes += sum(o.size * o.dtype.itemsize for o in outs)

    def kernel(*refs):
        body(*refs[:count], *refs[count + tokens :])

    return pl.pallas_call(
        kernel,
        name=name,
        out_shape=tuple(outs),
        in_specs=[scalar if a.dtype == jnp.int32 else inside for a in ins]
        + [pl.BlockSpec(memory_space=pl.ANY)] * tokens,
        out_specs=tuple(inside for _ in outs),
        scratch_shapes=list(scratch),
        compiler_params=pltpu.CompilerParams(vmem_limit_bytes=vmem * 2**20),
        cost_estimate=pl.CostEstimate(
            flops=int(flops * WEIGHT + UNIT * LOAD.get(name, 0)),
            bytes_accessed=int(nbytes * WEIGHT),
            transcendentals=0,
        ),
    )(*ins, *after)


def sds(shape, dtype):
    return jax.ShapeDtypeStruct(shape, dtype)


def normed(values):
    centre = values - jnp.mean(values, axis=-1, keepdims=True)
    spread = jnp.mean(centre * centre, axis=-1, keepdims=True)
    scale = lax.rsqrt(spread + EPS)
    return centre * scale, scale


def norm_back(values, gain, upstream):
    hat, scale = normed(values)
    scaled = upstream * gain
    first = jnp.mean(scaled, axis=-1, keepdims=True)
    second = jnp.mean(scaled * hat, axis=-1, keepdims=True)
    return scale * (scaled - first - hat * second), hat


def row_of(ref, row):
    return ref[row : row + 1, :].astype(F32)


def ordered(core, own, other):
    return jnp.where(core == 0, own, other), jnp.where(core == 0, other, own)


def heads_only(values, head, heads):
    if heads == 1:
        return values
    lane = lax.broadcasted_iota(jnp.int32, values.shape, 1)
    return jnp.where(lane // HEAD_DIM == head, values, jnp.zeros_like(values))


def key_tiles(total, limit):
    return [(at, min(BLOCK, limit - at)) for at in range(0, limit, BLOCK)]


def allowed_tile(at, width, row0, length, causal):
    key_at = at + lax.broadcasted_iota(jnp.int32, (width, BLOCK), 0)
    if causal:
        return key_at <= row0 + lax.broadcasted_iota(jnp.int32, (width, BLOCK), 1)
    return key_at < length


def scores_tile(k_ref, query, at, width, row0, length, causal):
    scores = nt(k_ref[at : at + width, :], query)
    if causal and at + width <= row0:
        return scores
    return jnp.where(allowed_tile(at, width, row0, length, causal), scores, NEG)


def attend(q_ref, k_ref, v_ref, mixed_ref, lse_ref, length, causal):
    seq, width = q_ref.shape
    keys = k_ref.shape[0]
    heads = width // HEAD_DIM
    value_t = jnp.transpose(v_ref[...])
    for row0 in range(0, seq, BLOCK):
        query = q_ref[row0 : row0 + BLOCK, :]
        tiles = key_tiles(keys, row0 + BLOCK if causal else keys)
        columns = []
        for head in range(heads):
            own = heads_only(query, head, heads)
            scores = [scores_tile(k_ref, own, at, w, row0, length, causal) for at, w in tiles]
            peak = functools.reduce(
                jnp.maximum, [jnp.max(s, axis=0, keepdims=True) for s in scores]
            )
            total = jnp.zeros_like(peak)
            mixed = jnp.zeros((HEAD_DIM, BLOCK), F32)
            for (at, w), s in zip(tiles, scores):
                raised = jnp.exp(s - peak)
                total = total + jnp.sum(raised, axis=0, keepdims=True)
                rows = value_t[head * HEAD_DIM : (head + 1) * HEAD_DIM, at : at + w]
                mixed = mixed + nn(rows, raised.astype(BF16))
            columns.append(mixed * (1.0 / total))
            lse_ref[head : head + 1, row0 : row0 + BLOCK] = peak + jnp.log(total)
        mixed_ref[row0 : row0 + BLOCK, :] = jnp.transpose(jnp.concatenate(columns, 0)).astype(BF16)


def attend_back(q_ref, k_ref, v_ref, up_ref, lse_ref, dq_ref, dk_acc, dv_acc, length, causal):
    seq, width = q_ref.shape
    keys = k_ref.shape[0]
    heads = width // HEAD_DIM
    key_t = jnp.transpose(k_ref[...])
    dk_acc[...] = jnp.zeros_like(dk_acc)
    dv_acc[...] = jnp.zeros_like(dv_acc)
    for row0 in range(0, seq, BLOCK):
        query = q_ref[row0 : row0 + BLOCK, :]
        upstream = up_ref[row0 : row0 + BLOCK, :]
        tiles = key_tiles(keys, row0 + BLOCK if causal else keys)
        columns = []
        for head in range(heads):
            own = heads_only(query, head, heads)
            own_up = heads_only(upstream, head, heads)
            lse = lse_ref[head : head + 1, row0 : row0 + BLOCK]
            weights, grads = [], []
            inner = jnp.zeros((1, BLOCK), F32)
            for at, w in tiles:
                weight = jnp.exp(scores_tile(k_ref, own, at, w, row0, length, causal) - lse)
                grad = nt(v_ref[at : at + w, :], own_up)
                inner = inner + jnp.sum(weight * grad, axis=0, keepdims=True)
                weights.append(weight)
                grads.append(grad)
            column = jnp.zeros((HEAD_DIM, BLOCK), F32)
            for (at, w), weight, grad in zip(tiles, weights, grads):
                score_grad = (weight * (grad - inner)).astype(BF16)
                dv_acc[at : at + w, :] += nn(weight.astype(BF16), own_up)
                dk_acc[at : at + w, :] += nn(score_grad, own)
                rows = key_t[head * HEAD_DIM : (head + 1) * HEAD_DIM, at : at + w]
                column = column + nn(rows, score_grad)
            columns.append(column * FACTOR)
        dq_ref[row0 : row0 + BLOCK, :] = jnp.transpose(jnp.concatenate(columns, 0)).astype(BF16)


def self_forward(chips, group, ids, *refs):
    parts, refs = paired(refs, chips, group)
    gain, shift, wqkv, bias, x_ref, h_ref, qkv_ref, mixed_ref, lse_ref = refs
    core, chip = ids[0] % 2, ids[0] // 2
    own = parts[0].shape[0]
    for mask in range(chips):
        lo, hi = ordered(core, parts[2 * mask][...], parts[2 * mask + 1][...])
        rows = jnp.concatenate([lo, hi], 0)
        at = pl.ds(pl.multiple_of((chip ^ mask) * 2 * own, 2 * own), 2 * own)
        x_ref[at, :] = rows
        hat, _ = normed(rows.astype(F32))
        hidden = (hat * row_of(gain, 0) + row_of(shift, 0)).astype(BF16)
        h_ref[at, :] = hidden
        query = nn(hidden, wqkv[0]) + row_of(bias, 0)
        qkv_ref[0, at, :] = (query.astype(BF16).astype(F32) * FACTOR).astype(BF16)
        qkv_ref[1, at, :] = nn(hidden, wqkv[1]).astype(BF16)
        qkv_ref[2, at, :] = (nn(hidden, wqkv[2]) + row_of(bias, 1)).astype(BF16)
    attend(qkv_ref.at[0], qkv_ref.at[1], qkv_ref.at[2], mixed_ref, lse_ref, None, True)


def paired(refs, chips, group):
    parts = []
    for mask in range(chips):
        other = refs[chips + mask // group]
        parts += [refs[mask], other if group == 1 else other.at[mask % group]]
    return parts, refs[chips + chips // group :]


def project_pairs(parts, mine, other, first, rows):
    width = parts[0].shape[1]
    total = None
    for mask in range(len(parts) // 2):
        lhs = [parts[2 * mask][rows, :], parts[2 * mask + 1][rows, :]]
        rhs = [ref[mask, first : first + width, :] for ref in (mine, other)]
        if width % 128 == 0:
            term = nn(jnp.concatenate(lhs, 1), jnp.concatenate(rhs, 0))
        else:
            term = nn(lhs[0], rhs[0]) + nn(lhs[1], rhs[1])
        total = term if total is None else total + term
    return total


def pack_all(*refs):
    for i, ref in enumerate(refs[:-1]):
        refs[-1][i] = ref[...]


def turned_place(mask, chips):
    bits = chips.bit_length() - 1
    return sum(((mask >> i) & 1) << (bits - 1 - i) for i in range(bits))


def pack(former, latter, out):
    count = former.shape[0]
    out[:count] = former[...]
    out[count:] = latter[...]


def cross_forward(chips, group, length, *refs):
    parts, refs = paired(refs, chips, group)
    wout, (x_ref, gain, shift, out_bias, wq, bias, mk, mv) = refs[:2], refs[2:10]
    s2_ref, h_ref, q_ref, mixed_ref, lse_ref = refs[10:]
    for row0 in range(0, x_ref.shape[0], BLOCK):
        rows = pl.ds(row0, BLOCK)
        branch = project_pairs(parts, *wout, 0, rows) + row_of(out_bias, 0)
        stream = x_ref[rows, :].astype(F32) + branch
        s2_ref[rows, :] = stream
        hat, _ = normed(stream)
        hidden = (hat * row_of(gain, 1) + row_of(shift, 1)).astype(BF16)
        h_ref[rows, :] = hidden
        query = (nn(hidden, wq[...]) + row_of(bias, 0)).astype(BF16).astype(F32)
        q_ref[rows, :] = (query * FACTOR).astype(BF16)
    attend(q_ref, mk, mv, mixed_ref, lse_ref, length[0], False)


def mlp(chips, group, ids, *refs):
    parts, refs = paired(refs, chips, group)
    wout, (grad_in, grad_other) = refs[:2], refs[2:4]
    (s2_ref, gain, shift, out_bias, wup, bup, wdown) = refs[4:11]
    s3_own, h_ref, act_ref, pg_ref, g_ref, sums, ups, s3 = refs[11:]
    core, chip = ids[0] % 2, ids[0] // 2
    own = s3_own.shape[0]
    sums[...] = jnp.zeros_like(sums[...])
    ups[...] = jnp.zeros_like(ups[...])
    for mask in range(chips):
        rows = pl.ds(pl.multiple_of((chip ^ mask) * 2 * own, 2 * own), 2 * own)
        branch = project_pairs(parts, *wout, 0, rows) + row_of(out_bias, 1)
        stream = s2_ref[rows, :] + branch
        if mask == 0:
            s3[...] = stream
            s3_own[...] = s3[pl.ds(pl.multiple_of(core * own, own), own), :]
        hat, _ = normed(stream)
        hidden = (hat * row_of(gain, 2) + row_of(shift, 2)).astype(BF16)
        h_ref[rows, :] = hidden
        pre = nn(hidden, wup[...]) + bup[...].astype(F32)
        half = 0.5 * (1.0 + lax.erf(pre * (0.5**0.5)))
        act_ref[rows, :] = (pre * half).astype(BF16)
        slope = half + pre * jnp.exp(-0.5 * pre * pre) * 0.3989422804014327
        lo, hi = ordered(core, grad_in[turned_place(mask, chips)], grad_other[turned_place(mask, chips)])
        grad = jnp.concatenate([lo, hi], 0)
        g_ref[rows, :] = grad
        pre_grad = (nt(grad, wdown[...]) * slope).astype(BF16)
        pg_ref[rows, :] = pre_grad
        ups[...] += jnp.sum(pre_grad.astype(F32), axis=0, keepdims=True)
        sums[...] += jnp.sum(grad.astype(F32), axis=0, keepdims=True)


def rows_for(ref, chip, core, own, chips):
    picks = []
    for mask in range(chips):
        at = pl.multiple_of(((chip ^ mask) * 2 + core) * own, own)
        picks.append(ref[pl.ds(at, own), :])
    return jnp.concatenate(picks, 0)


def picked_terms(lhs, rhs, dot, chip, core, own, chips):
    total = None
    for i in range(lhs.shape[0]):
        term = dot(rows_for(lhs.at[i], chip, core, own, chips), rhs[i])
        total = term if total is None else total + term
    return total


def member(refs, mask, group):
    return refs[mask] if group == 1 else refs[mask // group].at[mask % group]


def partial_sibling(chips, dot, ids, lhs, rhs, *outs):
    own, group = outs[0].shape[-2], chips // len(outs)
    total = picked_terms(lhs, rhs, dot, ids[0] // 2, 1 - ids[0] % 2, own, chips)
    for mask in range(chips):
        member(outs, mask, group)[...] = total[mask * own : (mask + 1) * own].astype(BF16)


def partial_own(chips, dot, ids, lhs, rhs, *refs):
    swaps = len(refs) - chips
    got, (first, *sends) = refs[:swaps], refs[swaps:]
    own, group = first.shape[0], chips // swaps
    total = picked_terms(lhs, rhs, dot, ids[0] // 2, ids[0] % 2, own, chips)
    for mask in list(range(1, chips)) + [0]:
        block = total[mask * own : (mask + 1) * own]
        block = block + member(got, mask, group)[...].astype(F32)
        if mask == 0:
            first[...] = block
        else:
            sends[mask - 1][...] = block.astype(BF16)


def last_sibling(chips, ids, act, wdown, wkv, dkv, norm, *outs):
    own, wide = act.shape[0] // (2 * chips), wdown.shape[1]
    chip, core = ids[0] // 2, 1 - ids[0] % 2
    total = nn(rows_for(act, chip, core, own, chips), wdown[...])
    turned_grad = picked_terms(wkv, dkv, nt, chip, core, own, chips)
    for mask in range(chips):
        rows = slice(mask * own, (mask + 1) * own)
        out = member(outs, mask, chips // len(outs))
        out[:own, :wide] = total[rows].astype(BF16)
        out[:own, wide:] = turned_grad[rows].astype(BF16)
        out[own:, :wide] = norm[...].astype(BF16)
        out[own:, wide:] = jnp.zeros_like(out[own:, wide:])


def last_own(chips, ids, act, wdown, wkv, dkv, norm, *refs):
    swaps = len(refs) - chips
    parts, (first, *sends) = refs[:swaps], refs[swaps:]
    own, wide = act.shape[0] // (2 * chips), wdown.shape[1]
    chip, core = ids[0] // 2, ids[0] % 2
    total = nn(rows_for(act, chip, core, own, chips), wdown[...])
    turned_grad = picked_terms(wkv, dkv, nt, chip, core, own, chips)
    for mask in range(chips):
        rows = slice(mask * own, (mask + 1) * own)
        out = first if mask == 0 else sends[mask - 1]
        got = member(parts, mask, chips // swaps)[...].astype(F32)
        out[:own, :wide] = (total[rows] + got[:own, :wide]).astype(out.dtype)
        out[:own, wide:] = (turned_grad[rows] + got[:own, wide:]).astype(out.dtype)
        out[own:, :wide] = (norm[...] + got[own:, :wide]).astype(out.dtype)
        out[own:, wide:] = jnp.zeros_like(out[own:, wide:])


def last_final(chips, *refs):
    parts = refs[:chips]
    stream, bias, self_sums, cross_sums, grad_sum, self_bias, cross_bias, up_bias = refs[
        chips : chips + 8
    ]
    out, memory, small = refs[chips + 8 :]
    own, wide = out.shape
    total = parts[0][...]
    for part in parts[1:]:
        total = total + part[...].astype(F32)
    out[...] = (total[:own, :wide] + stream[...] + row_of(bias, 2)).astype(BF16)
    memory[...] = jnp.transpose(total[:own, wide:])[: memory.shape[0]]
    small[...] = total[own:, :wide]
    small[2:5, :] = self_sums[...]
    small[5:8, :] = cross_sums[...]
    small[8:9, :] = grad_sum[...]
    width = self_bias.shape[1]
    for i in range(2):
        small[9 + i : 10 + i, :width] = self_bias[i : i + 1, :]
        small[11 + i : 12 + i, :width] = cross_bias[i : i + 1, :]
    small[13:14, : up_bias.shape[1]] = up_bias[...]


def small_final(*refs):
    parts, (gains, shifts, outs, self_bias, cross_bias, up_bias) = refs[:-6], refs[-6:]
    total = parts[0][...]
    for part in parts[1:]:
        total = total + part[...]
    for i, (gain, shift, out) in enumerate(((0, 1, 4), (2, 3, 7), (5, 6, 8))):
        gains[i : i + 1, :] = total[gain : gain + 1]
        shifts[i : i + 1, :] = total[shift : shift + 1]
        outs[i : i + 1, :] = total[out : out + 1]
    width = self_bias.shape[1]
    self_bias[...] = total[9:11, :width]
    cross_bias[...] = total[11:13, :width]
    up_bias[...] = total[13:14, : up_bias.shape[1]]


def stacked(values, block):
    return jnp.concatenate(
        [values[:, at : at + block] for at in range(0, values.shape[1], block)], 0
    )


def turned(lhs, rhs):
    return nn(jnp.transpose(lhs), rhs).astype(BF16)


def split_bucket(role, columns, keep, send):
    half = keep.shape[0]
    for at, block in columns:
        top, bottom = block[:half], block[half:]
        width = block.shape[1]
        keep[:, at : at + width] = jnp.where(role[0] == 0, top, bottom)
        send[:, at : at + width] = jnp.where(role[0] == 0, bottom, top)


def mlp_bucket(role, act, grad, hidden, pre_grad, keep, send):
    down = stacked(turned(act[...], grad[...]), act.shape[1])
    up = jnp.transpose(turned(pre_grad[...], hidden[...]))
    keep[...] = jnp.where(role[0] == 0, down, up)
    send[...] = jnp.where(role[0] == 0, up, down)


def cross_bucket(role, hidden, dq, padded, dkv, mixed, grad, keep, send):
    width = dq.shape[1]
    columns = [(0, jnp.transpose(turned(dq[...], hidden[...])))]
    for i in range(2):
        columns.append(((1 + i) * width, jnp.transpose(turned(dkv[i], padded[...]))))
    columns.append((3 * width, stacked(turned(mixed[...], grad[...]), width)))
    split_bucket(role, columns, keep, send)


def self_bucket(role, hidden, grads, mixed, grad, keep, send):
    width = mixed.shape[1]
    columns = []
    for i in range(3):
        columns.append((i * width, jnp.transpose(turned(grads[i], hidden[...]))))
    columns.append((3 * width, stacked(turned(mixed[...], grad[...]), width)))
    split_bucket(role, columns, keep, send)


def add_halves(former, latter, out):
    out[...] = (former[...].astype(F32) + latter[...].astype(F32)).astype(BF16)


def whole_bucket(role, total, other):
    mine, theirs = total[...].astype(F32), other[...].astype(F32)
    return jnp.concatenate(
        [jnp.where(role[0] == 0, mine, theirs), jnp.where(role[0] == 0, theirs, mine)], 0
    )


def mlp_final(role, total, other, out_down, out_up):
    mine, theirs = total[...].astype(F32), other[...].astype(F32)
    down = jnp.where(role[0] == 0, mine, theirs)
    out_up[...] = jnp.where(role[0] == 0, theirs, mine)
    rows = out_down.shape[0]
    for at in range(0, out_down.shape[1], rows):
        out_down[:, at : at + rows] = down[at : at + rows]


def cross_final(role, total, other, out_q, out_kv, out_o):
    width = out_q.shape[1]
    whole = whole_bucket(role, total, other)
    out_q[...] = whole[:, :width]
    out_kv[0] = whole[:, width : 2 * width]
    out_kv[1] = whole[:, 2 * width : 3 * width]
    for at in range(0, out_o.shape[1], width):
        out_o[:, at : at + width] = whole[at : at + width, 3 * width :]


def self_final(role, total, other, out_qkv, out_o):
    width = out_o.shape[0]
    whole = whole_bucket(role, total, other)
    for i in range(3):
        out_qkv[i] = whole[:, i * width : (i + 1) * width]
    for at in range(0, out_o.shape[1], width):
        out_o[:, at : at + width] = whole[at : at + width, 3 * width :]


def prepare(memory, wkv, bias, wq, padded, mk, mv, wq_t):
    rows = memory.shape[0]
    whole = -(-rows // 16) * 16
    if rows < mk.shape[0]:
        padded[whole - 16 :, :] = jnp.zeros((padded.shape[0] - whole + 16, padded.shape[1]), BF16)
    padded[0:rows, :] = memory[...]
    mk[...] = nn(padded[...], wkv[0]).astype(BF16)
    mv[...] = (nn(padded[...], wkv[1]) + row_of(bias, 1)).astype(BF16)
    wq_t[...] = jnp.transpose(wq[...])


def three_back(chips, *refs):
    first = refs[0]
    got = refs[1:chips]
    s3, gain, g_own, resid, message = refs[chips:]
    own = first.shape[0]
    total = first[...]
    for part in got:
        total = total + part[...].astype(F32)
    back, hat = norm_back(s3[...], row_of(gain, 2), total)
    grad = g_own[...].astype(F32) + back
    resid[...] = grad
    message[0:own, :] = grad.astype(BF16)
    sums = jnp.concatenate(
        [
            jnp.sum(total * hat, axis=0, keepdims=True),
            jnp.sum(total, axis=0, keepdims=True),
            jnp.zeros((14, total.shape[1]), F32),
        ],
        0,
    )
    message[own : own + 16, :] = sums.astype(BF16)


def cross_back(chips, group, ids, length, *refs):
    parts, refs = paired(refs, chips, group)
    wout, q_ref, mk, mv, lse, cg_ref, sums, dq_ref, dkv_ref, biases = refs[:10]
    up_ref, dk_acc, dv_acc = refs[10:]
    core, chip = ids[0] % 2, ids[0] // 2
    own = parts[0].shape[0] - 16
    norm_sums = jnp.zeros((2, cg_ref.shape[1]), F32)
    bias_sum = jnp.zeros((1, cg_ref.shape[1]), F32)
    for mask in range(chips):
        lo, hi = ordered(core, parts[2 * mask][...], parts[2 * mask + 1][...])
        norm_sums = norm_sums + lo[own : own + 2].astype(F32) + hi[own : own + 2].astype(F32)
        rows = jnp.concatenate([lo[:own], hi[:own]], 0)
        at = pl.ds(pl.multiple_of((chip ^ mask) * 2 * own, 2 * own), 2 * own)
        cg_ref[at, :] = rows
        bias_sum = bias_sum + jnp.sum(rows.astype(F32), axis=0, keepdims=True)
        up_ref[at, :] = nt(rows, wout[...]).astype(BF16)
    sums[...] = jnp.concatenate([norm_sums, bias_sum], 0)
    attend_back(q_ref, mk, mv, up_ref, lse, dq_ref, dk_acc, dv_acc, length[0], False)
    dkv_ref[0] = dk_acc[...].astype(BF16)
    dv = dv_acc[...].astype(BF16)
    dkv_ref[1] = dv
    biases[0:1, :] = jnp.sum(dq_ref[...].astype(F32), axis=0, keepdims=True)
    biases[1:2, :] = jnp.sum(dv.astype(F32), axis=0, keepdims=True)


def self_upstream(chips, group, ids, *refs):
    parts, refs = paired(refs, chips, group)
    wq, (s2_ref, gain, cg_ref, resid_two, wout) = refs[:2], refs[2:7]
    sg_ref, resid_one, sums, up_ref, base = refs[7:]
    own = resid_two.shape[0]
    mine = pl.ds(pl.multiple_of(ids[0] * own, own), own)
    base[...] = cg_ref[...].astype(F32)
    base[mine, :] = resid_two[...]
    sums[...] = jnp.zeros_like(sums[...])
    for row0 in range(0, s2_ref.shape[0], BLOCK):
        rows = pl.ds(row0, BLOCK)
        upstream = project_pairs(parts, *wq, 0, rows)
        back, hat = norm_back(s2_ref[rows, :], row_of(gain, 1), upstream)
        grad = base[rows, :] + back
        base[rows, :] = grad
        rounded = grad.astype(BF16)
        sg_ref[rows, :] = rounded
        sums[0:1, :] += jnp.sum(upstream * hat, axis=0, keepdims=True)
        sums[1:2, :] += jnp.sum(upstream, axis=0, keepdims=True)
        sums[2:3, :] += jnp.sum(rounded.astype(F32), axis=0, keepdims=True)
        up_ref[rows, :] = nt(rounded, wout[...]).astype(BF16)
    resid_one[...] = base[mine, :]


def self_back(qkv, up_ref, lse, grads, biases, dk_acc, dv_acc):
    attend_back(
        qkv.at[0], qkv.at[1], qkv.at[2], up_ref, lse, grads.at[0], dk_acc, dv_acc, None, True
    )
    grads[1] = dk_acc[...].astype(BF16)
    grads[2] = dv_acc[...].astype(BF16)
    biases[0:1, :] = jnp.sum(grads[0].astype(F32), axis=0, keepdims=True)
    biases[1:2, :] = jnp.sum(grads[2].astype(F32), axis=0, keepdims=True)


def first_norm_sums(x_ref, grads, wqkv, sums):
    sums[...] = jnp.zeros_like(sums[...])
    for row0 in range(0, x_ref.shape[0], BLOCK):
        rows = pl.ds(row0, BLOCK)
        upstream = sum(nt(grads[i, rows, :], wqkv[i]) for i in range(3))
        hat, _ = normed(x_ref[rows, :].astype(F32))
        sums[0:1, :] += jnp.sum(upstream * hat, axis=0, keepdims=True)
        sums[1:2, :] += jnp.sum(upstream, axis=0, keepdims=True)


def one_back(chips, *refs):
    first = refs[0]
    got = refs[1:chips]
    x_own, gain, resid, out = refs[chips:]
    total = first[...]
    for part in got:
        total = total + part[...].astype(F32)
    back, _ = norm_back(x_own[...].astype(F32), row_of(gain, 0), total)
    out[...] = resid[...] + back


def on_device(
    layer_input,
    output_grad,
    memory,
    memory_length,
    norm_gain,
    norm_bias,
    self_qkv,
    self_bias,
    self_out,
    cross_query,
    cross_kv,
    cross_bias,
    cross_out,
    up_weight,
    up_bias,
    down_weight,
    out_bias,
):
    ranks = lax.axis_size("tensor")
    pages_ranks = lax.axis_size("dp")
    chips = ranks // 2
    rank = lax.axis_index("tensor")
    own, wide = layer_input.shape
    seq = own * ranks
    width = self_qkv.shape[2]
    heads = width // HEAD_DIM
    hidden = up_bias.shape[0]
    mem = memory.shape[0]
    mem_pad = -(-mem // 128) * 128

    line = lax.axis_index("dp")
    ids = jnp.reshape(rank, (1,)).astype(jnp.int32)
    role = jnp.reshape((line ^ (line >> 1)) & 1, (1,)).astype(jnp.int32)

    def swap(values, mask):
        return lax.ppermute(values, "tensor", [(i, i ^ mask) for i in range(ranks)])

    def far_parts(values):
        return [values] + [swap(values, 2 * mask) for mask in range(1, chips)]

    def hold(values, *tokens):
        return lax.optimization_barrier((values, *tokens))[0]

    def grouped(name):
        return min(NEAR.get(name, 1), chips)

    def packed(parts):
        shape = (len(parts), *parts[0].shape)
        return call(pack_all, [sds(shape, parts[0].dtype)], parts)[0]

    def near_parts(far, name):
        group = grouped(name)
        groups = [far[at : at + group] for at in range(0, chips, group)]
        return [*far, *(swap(packed(g) if group > 1 else g[0], 1) for g in groups)]

    def joined(former, latter, after):
        shape = (2 * former.shape[0], *former.shape[1:])
        return call(pack, [sds(shape, BF16)], [former, latter], after=after)[0]

    turns = [1 << at for at in range(1, ranks.bit_length() - 1)]

    def gather(values):
        return near_parts(far_parts(values))

    def along(values, pairs):
        return lax.ppermute(
            values,
            "dp",
            [(at + a, at + b) for at in range(0, pages_ranks, 4) for a, b in pairs],
        )

    outer = [(0, 1), (1, 0), (2, 3), (3, 2)]
    middle = [(0, 3), (3, 0), (1, 2), (2, 1)]
    def bucket(body, rows, ins, flops, after):
        half = sds((rows, 4 * width), BF16)
        keep, send = call(body, [half, half], [role, *ins], flops, after=after)
        return keep, along(send, outer)

    def across(state, after):
        keep, got = state
        inner = call(add_halves, [sds(keep.shape, BF16)], [keep, got], after=after)[0]
        return inner, along(inner, middle)

    def back_out(state, after):
        inner, got = state
        half = sds(inner.shape, BF16)
        total = call(add_halves, [half], [inner, got], after=after)[0]
        mask = 4
        while mask < pages_ranks:
            pairs = [(i, i ^ mask) for i in range(pages_ranks)]
            total = call(add_halves, [half], [total, lax.ppermute(total, "dp", pairs)])[0]
            mask *= 2
        return total, along(total, outer)

    def stacks(rows, columns, name):
        group = grouped(name)
        shape = (rows, columns) if group == 1 else (group, rows, columns)
        return [sds(shape, BF16)] * (chips // group)

    def sibling_terms(lhs, rhs, dot, after, name):
        rows = lhs.shape[1] // ranks
        columns = rhs.shape[1 if dot is nt else 2]
        return call(
            functools.partial(partial_sibling, chips, dot),
            stacks(rows, columns, name),
            [ids, lhs, rhs],
            lhs.size * columns,
            after=after,
        )

    def own_terms(lhs, rhs, dot, got, after):
        rows, columns = got[0].shape[-2:]
        return call(
            functools.partial(partial_own, chips, dot),
            [sds((rows, columns), F32)] + [sds((rows, columns), BF16)] * (chips - 1),
            [ids, lhs, rhs, *got],
            lhs.size * columns,
            after=after,
        )

    def scatter_far(sums):
        return [sums[0]] + [swap(sums[mask], 2 * mask) for mask in range(1, chips)]

    held, steps = {}, {}

    def fill(slot, kernel, far=()):
        tokens = [kernel, far[1:2], far[1:]][BASE.get(slot, 0)] if far else kernel
        for name in SLOTS[slot]:
            tokens = [steps[name](tokens)]
        return tokens if SLOTS[slot] else []

    x_far = far_parts(layer_input)
    padded, mem_keys, mem_values, query_t = call(
        prepare,
        [
            sds((mem_pad, wide), BF16),
            sds((mem_pad, width), BF16),
            sds((mem_pad, width), BF16),
            sds((width, wide), BF16),
        ],
        [memory, cross_kv, cross_bias, cross_query],
        4 * mem_pad * wide * width,
    )
    x_far = [layer_input] + [hold(part, mem_keys) for part in x_far[1:]]

    def gather_step(name, order, at, until=()):
        def step(after):
            block, got = held[name]
            block = joined(block, got, after)
            if at + 1 < len(order):
                held[name] = (block, swap(hold(block, *until()) if until else block, order[at + 1]))
            else:
                held[name] = (block, swap(block, 1))
            return block

        return step

    def begin(name, value, order, until=()):
        block = value[None]
        held[name] = (block, swap(hold(block, *until) if until else block, order[0]))
        steps[name + "1"] = gather_step(name, order, 0, lambda: holds.get(name, ()))
        for at in range(1, len(order)):
            steps[name + str(at + 1)] = gather_step(name, order, at)

    def finish(name, order):
        for at in range(2, len(order)):
            steps[name + str(at + 1)]([])
        return held[name]

    holds = {}
    forth, back = turns, turns[::-1]
    begin("so", self_out, forth)
    begin("co", cross_out, forth)
    begin("g", output_grad, back)
    x_parts = near_parts(x_far, "x")
    x, hidden_one, qkv, self_mixed, self_lse = call(
        functools.partial(self_forward, chips, grouped("x")),
        [
            sds((seq, wide), BF16),
            sds((seq, wide), BF16),
            sds((3, seq, width), BF16),
            sds((seq, width), BF16),
            sds((heads, seq), F32),
        ],
        [ids, *x_parts, norm_gain, norm_bias, self_qkv, self_bias],
        2 * seq * wide * 3 * width + 4 * seq * seq * width,
        after=fill("x", [mem_keys, *x_far[1:]]),
    )
    tokens = fill("self", [self_mixed])
    mixed_far = far_parts(hold(self_mixed, *tokens) if tokens else self_mixed)
    holds["co"] = holds["g"] = mixed_far[1:]
    for name in ("co", "g"):
        if name + "1" in SLOTS["self"] or name + "1" in SLOTS["x"]:
            block, _ = held[name]
            held[name] = (block, swap(hold(block, *mixed_far[1:]), (forth if name == "co" else back)[1]))
    tokens = fill("mixed", [self_mixed], mixed_far)
    mixed_parts = near_parts(mixed_far, "mixed")
    so_block, so_other = finish("so", forth)
    stream_two, hidden_two, cross_q, cross_mixed, cross_lse = call(
        functools.partial(cross_forward, chips, grouped("mixed")),
        [
            sds((seq, wide), F32),
            sds((seq, wide), BF16),
            sds((seq, width), BF16),
            sds((seq, width), BF16),
            sds((heads, seq), F32),
        ],
        [
            memory_length,
            *mixed_parts,
            so_block,
            so_other,
            x,
            norm_gain,
            norm_bias,
            out_bias,
            cross_query,
            cross_bias,
            mem_keys,
            mem_values,
        ],
        2 * seq * wide * (wide + width) + 4 * seq * mem_pad * width,
        after=tokens,
    )
    cross_far = far_parts(cross_mixed)
    tokens = fill("cross", [cross_mixed], cross_far)
    cross_parts = near_parts(cross_far, "cross")
    co_block, co_other = finish("co", forth)
    g_block, g_other = finish("g", back)
    begin("wq", query_t, forth, cross_far[1:])
    stream_three, hidden_three, activated, pre_grad, whole_grad, grad_sum, up_bias_grad = call(
        functools.partial(mlp, chips, grouped("cross")),
        [
            sds((own, wide), F32),
            sds((seq, wide), BF16),
            sds((seq, hidden), BF16),
            sds((seq, hidden), BF16),
            sds((seq, wide), BF16),
            sds((1, wide), F32),
            sds((1, hidden), F32),
        ],
        [
            ids,
            *cross_parts,
            co_block,
            co_other,
            g_block,
            g_other,
            stream_two,
            norm_gain,
            norm_bias,
            out_bias,
            up_weight,
            up_bias.reshape(1, -1),
            down_weight,
        ],
        2 * seq * wide * (wide + 2 * hidden),
        [pltpu.VMEM((2 * own, wide), F32)],
        after=tokens,
    )

    def step(name):
        return lambda function: steps.__setitem__(name, function)

    @step("bucket m")
    def _(after):
        held["m"] = bucket(
            mlp_bucket,
            wide,
            [activated, whole_grad, hidden_three, pre_grad],
            4 * seq * wide * hidden,
            after,
        )
        return held["m"][0]

    def mover(key, function):
        def run(after):
            held[key] = function(held[key], after)
            return held[key][0]

        return run

    for key in "mca":
        steps["add " + key] = mover(key, across)
        steps["out " + key] = mover(key, back_out)

    up_item, pre_item = up_weight[None], pre_grad[None]
    sibling = sibling_terms(pre_item, up_item, nt, fill("mlp", [pre_grad]), "three")
    got = [swap(part, 1) for part in sibling]
    three_sums = own_terms(pre_item, up_item, nt, got, fill("three", [sibling[0]]))
    three_far = scatter_far(three_sums)
    resid_two, message = call(
        functools.partial(three_back, chips),
        [sds((own, wide), F32), sds((own + 16, wide), BF16)],
        [*three_far, stream_three, norm_gain, output_grad],
        after=fill("three far", [three_sums[0]], three_far),
    )
    cg_far = far_parts(message)
    cg_parts = near_parts(cg_far, "grad")
    cross_grad, cross_sums, dq2, dkv2, cross_bias_grad = call(
        functools.partial(cross_back, chips, grouped("grad")),
        [
            sds((seq, wide), BF16),
            sds((3, wide), F32),
            sds((seq, width), BF16),
            sds((2, mem_pad, width), BF16),
            sds((2, width), F32),
        ],
        [
            ids,
            memory_length,
            *cg_parts,
            cross_out,
            cross_q,
            mem_keys,
            mem_values,
            cross_lse,
        ],
        2 * seq * wide * width + 10 * seq * mem_pad * width,
        [
            pltpu.VMEM((seq, width), BF16),
            pltpu.VMEM((mem_pad, width), F32),
            pltpu.VMEM((mem_pad, width), F32),
        ],
        after=fill("grad far", [message], cg_far),
    )
    dq2_far = far_parts(dq2)

    @step("bucket c")
    def _(after):
        held["c"] = bucket(
            cross_bucket,
            wide // 2,
            [hidden_two, dq2, padded, dkv2, cross_mixed, cross_grad],
            8 * seq * wide * width,
            after,
        )
        return held["c"][0]

    tokens = fill("query far", [dq2], dq2_far)
    dq2_parts = near_parts(dq2_far, "query")
    wq_block, wq_other = finish("wq", forth)
    self_grad, resid_one, self_sums, self_up = call(
        functools.partial(self_upstream, chips, grouped("query")),
        [
            sds((seq, wide), BF16),
            sds((own, wide), F32),
            sds((3, wide), F32),
            sds((seq, width), BF16),
        ],
        [
            ids,
            *dq2_parts,
            wq_block,
            wq_other,
            stream_two,
            norm_gain,
            cross_grad,
            resid_two,
            self_out,
        ],
        2 * seq * wide * (wide + width),
        [pltpu.VMEM((seq, wide), F32)],
        after=tokens,
    )
    grads, self_bias_grad = call(
        self_back,
        [sds((3, seq, width), BF16), sds((2, width), F32)],
        [qkv, self_up, self_lse],
        10 * seq * seq * width,
        [pltpu.VMEM((seq, width), F32), pltpu.VMEM((seq, width), F32)],
        after=fill("up", [self_up]),
    )

    @step("bucket a")
    def _(after):
        held["a"] = bucket(
            self_bucket,
            wide // 2,
            [hidden_one, grads, self_mixed, self_grad],
            8 * seq * wide * width,
            after,
        )
        return held["a"][0]

    @step("norm")
    def _(after):
        held["norm"] = call(
            first_norm_sums,
            [sds((16, wide), F32)],
            [x, grads, self_qkv],
            6 * seq * wide * width,
            after=after,
        )[0]
        return held["norm"]

    sibling = sibling_terms(grads, self_qkv, nt, fill("back", [grads]), "one")
    got = [swap(part, 1) for part in sibling]
    one_sums = own_terms(grads, self_qkv, nt, got, fill("one", [sibling[0]]))
    one_far = scatter_far(one_sums)
    (input_grad,) = call(
        functools.partial(one_back, chips),
        [sds((own, wide), F32)],
        [*one_far, layer_input, norm_gain, resid_one],
        after=fill("one far", [one_sums[0]], one_far),
    )
    tokens = fill("input", [input_grad])
    last_ins = [ids, activated, down_weight, cross_kv, dkv2, held["norm"]]
    sibling = call(
        functools.partial(last_sibling, chips),
        stacks(own + 16, wide + mem_pad, "last"),
        last_ins,
        after=tokens,
    )
    got = [swap(part, 1) for part in sibling]
    last = call(
        functools.partial(last_own, chips),
        [sds((own + 16, wide + mem_pad), F32)]
        + [sds((own + 16, wide + mem_pad), BF16)] * (chips - 1),
        [*last_ins, *got],
        after=fill("last", [sibling[0]]),
    )
    last_far = scatter_far(last)

    @step("final m")
    def _(after):
        held["final m"] = call(
            mlp_final,
            [sds((hidden, wide), F32), sds((wide, hidden), F32)],
            [role, *held["m"]],
            after=after,
        )
        return held["final m"][0]

    @step("final c")
    def _(after):
        held["final c"] = call(
            cross_final,
            [sds((wide, width), F32), sds((2, wide, width), F32), sds((width, wide), F32)],
            [role, *held["c"]],
            after=after,
        )
        return held["final c"][0]

    output, memory_grad, small = call(
        functools.partial(last_final, chips),
        [
            sds((own, wide), BF16),
            sds((mem, wide // ranks), F32),
            sds((16, wide), F32),
        ],
        [
            *last_far,
            stream_three,
            out_bias,
            self_sums,
            cross_sums,
            grad_sum,
            self_bias_grad,
            cross_bias_grad,
            up_bias_grad,
        ],
        after=fill("last far", [last[0]], last_far),
    )
    small_parts = [small] + [
        lax.ppermute(small, "dp", [(i, (i + shift) % pages_ranks) for i in range(pages_ranks)])
        for shift in range(1, pages_ranks)
    ]
    tokens = fill("end", [small])
    gains, shifts, outs, self_bias_sum, cross_bias_sum, up_bias_sum = call(
        small_final,
        [sds((3, wide), F32)] * 3
        + [sds((2, width), F32), sds((2, width), F32), sds((1, hidden), F32)],
        small_parts,
        after=tokens,
    )
    self_qkv_grad, self_out_grad = call(
        self_final,
        [sds((3, wide, width), F32), sds((width, wide), F32)],
        [role, *held["a"]],
        after=[gains],
    )
    down_grad, up_grad = held["final m"]
    cross_query_grad, cross_kv_grad, cross_out_grad = held["final c"]
    return (
        output,
        input_grad,
        memory_grad,
        gains,
        shifts,
        self_qkv_grad,
        self_bias_sum,
        self_out_grad,
        cross_query_grad,
        cross_kv_grad,
        cross_bias_sum,
        cross_out_grad,
        up_grad,
        up_bias_sum.reshape(-1),
        down_grad,
        outs,
    )


def solution(mesh):
    return jax.shard_map(
        on_device,
        mesh=mesh,
        in_specs=(
            P(("dp", "tensor"), None),
            P(("dp", "tensor"), None),
            P("dp", None),
            P("dp"),
            P(),
            P(),
            P(None, None, "tensor"),
            P(None, "tensor"),
            P("tensor", None),
            P(None, "tensor"),
            P(None, None, "tensor"),
            P(None, "tensor"),
            P("tensor", None),
            P(None, "tensor"),
            P("tensor"),
            P("tensor", None),
            P(),
        ),
        out_specs=(
            P(("dp", "tensor"), None),
            P(("dp", "tensor"), None),
            P("dp", "tensor"),
            P(),
            P(),
            P(None, None, "tensor"),
            P(None, "tensor"),
            P("tensor", None),
            P(None, "tensor"),
            P(None, None, "tensor"),
            P(None, "tensor"),
            P("tensor", None),
            P(None, "tensor"),
            P("tensor"),
            P("tensor", None),
            P(),
        ),
        check_vma=False,
    )
```

```python
import functools

import jax
import jax.numpy as jnp
from jax import lax
from jax.experimental import pallas as pl
from jax.experimental.pallas import tpu as pltpu
from jax.sharding import PartitionSpec as P

HEAD_DIM = 64
EPS = 1e-05
NEG = -1e30
BLOCK = 256
FACTOR = HEAD_DIM ** (-0.5)
F32 = jnp.float32
BF16 = jnp.bfloat16

def nn(a, b):
    return lax.dot_general(a, b, (((1,), (0,)), ((), ())), preferred_element_type=F32)


def nt(a, b):
    return lax.dot_general(a, b, (((1,), (1,)), ((), ())), preferred_element_type=F32)


SLOTS = {
    "x": ["so1"],
    "self": ["co1", "g1"],
    "mixed": ["so2"],
    "cross": ["co2", "g2"],
    "mlp": [],
    "three": ["wq1"],
    "three far": ["bucket m"],
    "grad far": ["wq2", "add m"],
    "query far": ["bucket c"],
    "up": [],
    "back": [],
    "one": ["out m", "bucket a"],
    "one far": ["add c"],
    "input": ["add a", "out c"],
    "last": [],
    "last far": ["final m", "out a", "final c", "last final"],
    "end": [],
}
BASE = {"mixed": 2, "cross": 2, "grad far": 2, "query far": 2}
NEAR = {}
LOAD = {"three_back": 4, "last_final": 2}
UNIT = 1.8e9
WEIGHT = 0.12


def call(body, outs, ins, flops=0, scratch=(), after=(), vmem=8):
    inside = pl.BlockSpec(memory_space=pltpu.VMEM)
    scalar = pl.BlockSpec(memory_space=pltpu.SMEM)
    count, tokens = len(ins), len(after)
    name = getattr(body, "func", body).__name__
    nbytes = sum(a.size * a.dtype.itemsize for a in ins)
    nbytes += sum(o.size * o.dtype.itemsize for o in outs)

    def kernel(*refs):
        body(*refs[:count], *refs[count + tokens :])

    return pl.pallas_call(
        kernel,
        name=name,
        out_shape=tuple(outs),
        in_specs=[scalar if a.dtype == jnp.int32 else inside for a in ins]
        + [pl.BlockSpec(memory_space=pl.ANY)] * tokens,
        out_specs=tuple(inside for _ in outs),
        scratch_shapes=list(scratch),
        compiler_params=pltpu.CompilerParams(vmem_limit_bytes=vmem * 2**20),
        cost_estimate=pl.CostEstimate(
            flops=int(flops * WEIGHT + UNIT * LOAD.get(name, 0)),
            bytes_accessed=int(nbytes * WEIGHT),
            transcendentals=0,
        ),
    )(*ins, *after)


def sds(shape, dtype):
    return jax.ShapeDtypeStruct(shape, dtype)


def normed(values):
    centre = values - jnp.mean(values, axis=-1, keepdims=True)
    spread = jnp.mean(centre * centre, axis=-1, keepdims=True)
    scale = lax.rsqrt(spread + EPS)
    return centre * scale, scale


def norm_back(values, gain, upstream):
    hat, scale = normed(values)
    scaled = upstream * gain
    first = jnp.mean(scaled, axis=-1, keepdims=True)
    second = jnp.mean(scaled * hat, axis=-1, keepdims=True)
    return scale * (scaled - first - hat * second), hat


def row_of(ref, row):
    return ref[row : row + 1, :].astype(F32)


def ordered(core, own, other):
    return jnp.where(core == 0, own, other), jnp.where(core == 0, other, own)


def heads_only(values, head, heads):
    if heads == 1:
        return values
    lane = lax.broadcasted_iota(jnp.int32, values.shape, 1)
    return jnp.where(lane // HEAD_DIM == head, values, jnp.zeros_like(values))


def key_tiles(total, limit):
    return [(at, min(BLOCK, limit - at)) for at in range(0, limit, BLOCK)]


def allowed_tile(at, width, row0, length, causal):
    key_at = at + lax.broadcasted_iota(jnp.int32, (width, BLOCK), 0)
    if causal:
        return key_at <= row0 + lax.broadcasted_iota(jnp.int32, (width, BLOCK), 1)
    return key_at < length


def scores_tile(k_ref, query, at, width, row0, length, causal):
    scores = nt(k_ref[at : at + width, :], query)
    if causal and at + width <= row0:
        return scores
    return jnp.where(allowed_tile(at, width, row0, length, causal), scores, NEG)


def attend(q_ref, k_ref, v_ref, mixed_ref, lse_ref, length, causal):
    seq, width = q_ref.shape
    keys = k_ref.shape[0]
    heads = width // HEAD_DIM
    value_t = jnp.transpose(v_ref[...])
    for row0 in range(0, seq, BLOCK):
        query = q_ref[row0 : row0 + BLOCK, :]
        tiles = key_tiles(keys, row0 + BLOCK if causal else keys)
        columns = []
        for head in range(heads):
            own = heads_only(query, head, heads)
            scores = [scores_tile(k_ref, own, at, w, row0, length, causal) for at, w in tiles]
            peak = functools.reduce(
                jnp.maximum, [jnp.max(s, axis=0, keepdims=True) for s in scores]
            )
            total = jnp.zeros_like(peak)
            mixed = jnp.zeros((HEAD_DIM, BLOCK), F32)
            for (at, w), s in zip(tiles, scores):
                raised = jnp.exp(s - peak)
                total = total + jnp.sum(raised, axis=0, keepdims=True)
                rows = value_t[head * HEAD_DIM : (head + 1) * HEAD_DIM, at : at + w]
                mixed = mixed + nn(rows, raised.astype(BF16))
            columns.append(mixed * (1.0 / total))
            lse_ref[head : head + 1, row0 : row0 + BLOCK] = peak + jnp.log(total)
        mixed_ref[row0 : row0 + BLOCK, :] = jnp.transpose(jnp.concatenate(columns, 0)).astype(BF16)


def attend_back(q_ref, k_ref, v_ref, up_ref, lse_ref, dq_ref, dk_acc, dv_acc, length, causal):
    seq, width = q_ref.shape
    keys = k_ref.shape[0]
    heads = width // HEAD_DIM
    key_t = jnp.transpose(k_ref[...])
    dk_acc[...] = jnp.zeros_like(dk_acc)
    dv_acc[...] = jnp.zeros_like(dv_acc)
    for row0 in range(0, seq, BLOCK):
        query = q_ref[row0 : row0 + BLOCK, :]
        upstream = up_ref[row0 : row0 + BLOCK, :]
        tiles = key_tiles(keys, row0 + BLOCK if causal else keys)
        columns = []
        for head in range(heads):
            own = heads_only(query, head, heads)
            own_up = heads_only(upstream, head, heads)
            lse = lse_ref[head : head + 1, row0 : row0 + BLOCK]
            weights, grads = [], []
            inner = jnp.zeros((1, BLOCK), F32)
            for at, w in tiles:
                weight = jnp.exp(scores_tile(k_ref, own, at, w, row0, length, causal) - lse)
                grad = nt(v_ref[at : at + w, :], own_up)
                inner = inner + jnp.sum(weight * grad, axis=0, keepdims=True)
                weights.append(weight)
                grads.append(grad)
            column = jnp.zeros((HEAD_DIM, BLOCK), F32)
            for (at, w), weight, grad in zip(tiles, weights, grads):
                score_grad = (weight * (grad - inner)).astype(BF16)
                dv_acc[at : at + w, :] += nn(weight.astype(BF16), own_up)
                dk_acc[at : at + w, :] += nn(score_grad, own)
                rows = key_t[head * HEAD_DIM : (head + 1) * HEAD_DIM, at : at + w]
                column = column + nn(rows, score_grad)
            columns.append(column * FACTOR)
        dq_ref[row0 : row0 + BLOCK, :] = jnp.transpose(jnp.concatenate(columns, 0)).astype(BF16)


def self_forward(chips, group, ids, *refs):
    parts, refs = paired(refs, chips, group)
    gain, shift, wqkv, bias, x_ref, h_ref, qkv_ref, mixed_ref, lse_ref = refs
    core, chip = ids[0] % 2, ids[0] // 2
    own = parts[0].shape[0]
    for mask in range(chips):
        lo, hi = ordered(core, parts[2 * mask][...], parts[2 * mask + 1][...])
        rows = jnp.concatenate([lo, hi], 0)
        at = pl.ds(pl.multiple_of((chip ^ mask) * 2 * own, 2 * own), 2 * own)
        x_ref[at, :] = rows
        hat, _ = normed(rows.astype(F32))
        hidden = (hat * row_of(gain, 0) + row_of(shift, 0)).astype(BF16)
        h_ref[at, :] = hidden
        query = nn(hidden, wqkv[0]) + row_of(bias, 0)
        qkv_ref[0, at, :] = (query.astype(BF16).astype(F32) * FACTOR).astype(BF16)
        qkv_ref[1, at, :] = nn(hidden, wqkv[1]).astype(BF16)
        qkv_ref[2, at, :] = (nn(hidden, wqkv[2]) + row_of(bias, 1)).astype(BF16)
    attend(qkv_ref.at[0], qkv_ref.at[1], qkv_ref.at[2], mixed_ref, lse_ref, None, True)


def paired(refs, chips, group):
    parts = []
    for mask in range(chips):
        other = refs[chips + mask // group]
        parts += [refs[mask], other if group == 1 else other.at[mask % group]]
    return parts, refs[chips + chips // group :]


def project_pairs(parts, mine, other, first, rows):
    width = parts[0].shape[1]
    total = None
    for mask in range(len(parts) // 2):
        lhs = [parts[2 * mask][rows, :], parts[2 * mask + 1][rows, :]]
        rhs = [ref[mask, first : first + width, :] for ref in (mine, other)]
        if width % 128 == 0:
            term = nn(jnp.concatenate(lhs, 1), jnp.concatenate(rhs, 0))
        else:
            term = nn(lhs[0], rhs[0]) + nn(lhs[1], rhs[1])
        total = term if total is None else total + term
    return total


def pack_all(*refs):
    for i, ref in enumerate(refs[:-1]):
        refs[-1][i] = ref[...]


def turned_place(mask, chips):
    bits = chips.bit_length() - 1
    return sum(((mask >> i) & 1) << (bits - 1 - i) for i in range(bits))


def pack(former, latter, out):
    count = former.shape[0]
    out[:count] = former[...]
    out[count:] = latter[...]


def cross_forward(chips, group, length, *refs):
    parts, refs = paired(refs, chips, group)
    wout, (x_ref, gain, shift, out_bias, wq, bias, mk, mv) = refs[:2], refs[2:10]
    s2_ref, h_ref, q_ref, mixed_ref, lse_ref = refs[10:]
    for row0 in range(0, x_ref.shape[0], BLOCK):
        rows = pl.ds(row0, BLOCK)
        branch = project_pairs(parts, *wout, 0, rows) + row_of(out_bias, 0)
        stream = x_ref[rows, :].astype(F32) + branch
        s2_ref[rows, :] = stream
        hat, _ = normed(stream)
        hidden = (hat * row_of(gain, 1) + row_of(shift, 1)).astype(BF16)
        h_ref[rows, :] = hidden
        query = (nn(hidden, wq[...]) + row_of(bias, 0)).astype(BF16).astype(F32)
        q_ref[rows, :] = (query * FACTOR).astype(BF16)
    attend(q_ref, mk, mv, mixed_ref, lse_ref, length[0], False)


def mlp(chips, group, ids, *refs):
    parts, refs = paired(refs, chips, group)
    wout, (grad_in, grad_other) = refs[:2], refs[2:4]
    (s2_ref, gain, shift, out_bias, wup, bup, wdown) = refs[4:11]
    s3_own, h_ref, act_ref, pg_ref, g_ref, sums, ups, s3 = refs[11:]
    core, chip = ids[0] % 2, ids[0] // 2
    own = s3_own.shape[0]
    sums[...] = jnp.zeros_like(sums[...])
    ups[...] = jnp.zeros_like(ups[...])
    for mask in range(chips):
        rows = pl.ds(pl.multiple_of((chip ^ mask) * 2 * own, 2 * own), 2 * own)
        branch = project_pairs(parts, *wout, 0, rows) + row_of(out_bias, 1)
        stream = s2_ref[rows, :] + branch
        if mask == 0:
            s3[...] = stream
            s3_own[...] = s3[pl.ds(pl.multiple_of(core * own, own), own), :]
        hat, _ = normed(stream)
        hidden = (hat * row_of(gain, 2) + row_of(shift, 2)).astype(BF16)
        h_ref[rows, :] = hidden
        pre = nn(hidden, wup[...]) + bup[...].astype(F32)
        half = 0.5 * (1.0 + lax.erf(pre * (0.5**0.5)))
        act_ref[rows, :] = (pre * half).astype(BF16)
        slope = half + pre * jnp.exp(-0.5 * pre * pre) * 0.3989422804014327
        lo, hi = ordered(core, grad_in[turned_place(mask, chips)], grad_other[turned_place(mask, chips)])
        grad = jnp.concatenate([lo, hi], 0)
        g_ref[rows, :] = grad
        pre_grad = (nt(grad, wdown[...]) * slope).astype(BF16)
        pg_ref[rows, :] = pre_grad
        ups[...] += jnp.sum(pre_grad.astype(F32), axis=0, keepdims=True)
        sums[...] += jnp.sum(grad.astype(F32), axis=0, keepdims=True)


def rows_for(ref, chip, core, own, chips):
    picks = []
    for mask in range(chips):
        at = pl.multiple_of(((chip ^ mask) * 2 + core) * own, own)
        picks.append(ref[pl.ds(at, own), :])
    return jnp.concatenate(picks, 0)


def picked_terms(lhs, rhs, dot, chip, core, own, chips):
    total = None
    for i in range(lhs.shape[0]):
        term = dot(rows_for(lhs.at[i], chip, core, own, chips), rhs[i])
        total = term if total is None else total + term
    return total


def member(refs, mask, group):
    return refs[mask] if group == 1 else refs[mask // group].at[mask % group]


def partial_sibling(chips, dot, ids, lhs, rhs, *outs):
    own, group = outs[0].shape[-2], chips // len(outs)
    total = picked_terms(lhs, rhs, dot, ids[0] // 2, 1 - ids[0] % 2, own, chips)
    for mask in range(chips):
        member(outs, mask, group)[...] = total[mask * own : (mask + 1) * own].astype(BF16)


def partial_own(chips, dot, ids, lhs, rhs, *refs):
    swaps = len(refs) - chips
    got, (first, *sends) = refs[:swaps], refs[swaps:]
    own, group = first.shape[0], chips // swaps
    total = picked_terms(lhs, rhs, dot, ids[0] // 2, ids[0] % 2, own, chips)
    for mask in list(range(1, chips)) + [0]:
        block = total[mask * own : (mask + 1) * own]
        block = block + member(got, mask, group)[...].astype(F32)
        if mask == 0:
            first[...] = block
        else:
            sends[mask - 1][...] = block.astype(BF16)


def last_sibling(chips, ids, act, wdown, wkv, dkv, *outs):
    own, wide = act.shape[0] // (2 * chips), wdown.shape[1]
    chip, core = ids[0] // 2, 1 - ids[0] % 2
    total = nn(rows_for(act, chip, core, own, chips), wdown[...])
    turned_grad = picked_terms(wkv, dkv, nt, chip, core, own, chips)
    for mask in range(chips):
        rows = slice(mask * own, (mask + 1) * own)
        out = member(outs, mask, chips // len(outs))
        out[:, :wide] = total[rows].astype(BF16)
        out[:, wide:] = turned_grad[rows].astype(BF16)


def last_own(chips, ids, act, wdown, wkv, dkv, *refs):
    swaps = len(refs) - chips
    parts, (first, *sends) = refs[:swaps], refs[swaps:]
    own, wide = act.shape[0] // (2 * chips), wdown.shape[1]
    chip, core = ids[0] // 2, ids[0] % 2
    total = nn(rows_for(act, chip, core, own, chips), wdown[...])
    turned_grad = picked_terms(wkv, dkv, nt, chip, core, own, chips)
    for mask in range(chips):
        rows = slice(mask * own, (mask + 1) * own)
        out = first if mask == 0 else sends[mask - 1]
        got = member(parts, mask, chips // swaps)[...].astype(F32)
        out[:, :wide] = (total[rows] + got[:, :wide]).astype(out.dtype)
        out[:, wide:] = (turned_grad[rows] + got[:, wide:]).astype(out.dtype)


def last_final(chips, *refs):
    parts, (stream, bias, out, memory) = refs[:chips], refs[chips:]
    wide = out.shape[1]
    total = parts[0][...]
    for part in parts[1:]:
        total = total + part[...].astype(F32)
    out[...] = (total[:, :wide] + stream[...] + row_of(bias, 2)).astype(BF16)
    memory[...] = jnp.transpose(total[:, wide:])[: memory.shape[0]]


def small_final(small, *refs):
    parts, (gains, shifts, outs, self_bias, cross_bias, up_bias) = refs[:-6], refs[-6:]
    norm = parts[0][0:2, :]
    for part in parts[1:]:
        norm = norm + part[0:2, :]
    gains[0:1, :] = norm[0:1]
    shifts[0:1, :] = norm[1:2]
    for i, (gain, shift, out) in enumerate(((0, 1, 4), (2, 3, 7), (5, 6, 8))):
        if i:
            gains[i : i + 1, :] = small[gain : gain + 1, :]
            shifts[i : i + 1, :] = small[shift : shift + 1, :]
        outs[i : i + 1, :] = small[out : out + 1, :]
    width = self_bias.shape[1]
    self_bias[...] = small[9:11, :width]
    cross_bias[...] = small[11:13, :width]
    up_bias[...] = small[13:14, : up_bias.shape[1]]


def stacked(values, block):
    return jnp.concatenate(
        [values[:, at : at + block] for at in range(0, values.shape[1], block)], 0
    )


def turned(lhs, rhs):
    return nn(jnp.transpose(lhs), rhs).astype(BF16)


def split_bucket(role, columns, keep, send):
    half = keep.shape[0]
    for at, block in columns:
        top, bottom = block[:half], block[half:]
        width = block.shape[1]
        keep[:, at : at + width] = jnp.where(role[0] == 0, top, bottom)
        send[:, at : at + width] = jnp.where(role[0] == 0, bottom, top)


def mlp_bucket(role, act, grad, hidden, pre_grad, keep, send):
    down = stacked(turned(act[...], grad[...]), act.shape[1])
    up = jnp.transpose(turned(pre_grad[...], hidden[...]))
    keep[...] = jnp.where(role[0] == 0, down, up)
    send[...] = jnp.where(role[0] == 0, up, down)


def cross_bucket(role, hidden, dq, padded, dkv, mixed, grad, keep, send):
    width = dq.shape[1]
    columns = [(0, jnp.transpose(turned(dq[...], hidden[...])))]
    for i in range(2):
        columns.append(((1 + i) * width, jnp.transpose(turned(dkv[i], padded[...]))))
    columns.append((3 * width, stacked(turned(mixed[...], grad[...]), width)))
    split_bucket(role, columns, keep, send)


def self_bucket(role, hidden, grads, mixed, grad, wqkv, gain, shift, *refs):
    self_sums, cross_sums, grad_sum, self_bias, cross_bias, up_bias, keep, send, small = refs
    width = mixed.shape[1]
    columns = []
    products = jnp.zeros((1, hidden.shape[1]), F32)
    sums = jnp.zeros((1, hidden.shape[1]), F32)
    for i in range(3):
        turned_grads = jnp.transpose(grads[i])
        weight_grad = nn(turned_grads, hidden[...])
        weight = jnp.transpose(wqkv[i]).astype(F32)
        total = jnp.sum(turned_grads.astype(F32), axis=1, keepdims=True)
        products = products + jnp.sum(weight * weight_grad, axis=0, keepdims=True)
        sums = sums + jnp.sum(weight * total, axis=0, keepdims=True)
        columns.append((i * width, jnp.transpose(weight_grad.astype(BF16))))
    columns.append((3 * width, stacked(turned(mixed[...], grad[...]), width)))
    half = keep.shape[0] - small.size // (4 * width)
    for at, block in columns:
        top, bottom = block[:half], block[half:]
        place = slice(at, at + block.shape[1])
        keep[:half, place] = jnp.where(role[0] == 0, top, bottom)
        send[:half, place] = jnp.where(role[0] == 0, bottom, top)
    small[...] = jnp.zeros_like(small[...])
    small[0:1, :] = (products - row_of(shift, 0) * sums) / row_of(gain, 0)
    small[1:2, :] = sums
    small[2:5, :] = self_sums[...]
    small[5:8, :] = cross_sums[...]
    small[8:9, :] = grad_sum[...]
    for i in range(2):
        small[9 + i : 10 + i, :width] = self_bias[i : i + 1, :]
        small[11 + i : 12 + i, :width] = cross_bias[i : i + 1, :]
    small[13:14, : up_bias.shape[1]] = up_bias[...]
    rows = stacked(small[...], 4 * width).astype(BF16)
    keep[half:, :] = rows
    send[half:, :] = rows


def add_halves(former, latter, out):
    out[...] = (former[...].astype(F32) + latter[...].astype(F32)).astype(BF16)


def whole_bucket(role, total, other):
    mine, theirs = total[...].astype(F32), other[...].astype(F32)
    return jnp.concatenate(
        [jnp.where(role[0] == 0, mine, theirs), jnp.where(role[0] == 0, theirs, mine)], 0
    )


def mlp_final(role, total, other, out_down, out_up):
    mine, theirs = total[...].astype(F32), other[...].astype(F32)
    down = jnp.where(role[0] == 0, mine, theirs)
    out_up[...] = jnp.where(role[0] == 0, theirs, mine)
    rows = out_down.shape[0]
    for at in range(0, out_down.shape[1], rows):
        out_down[:, at : at + rows] = down[at : at + rows]


def cross_final(role, total, other, out_q, out_kv, out_o):
    width = out_q.shape[1]
    whole = whole_bucket(role, total, other)
    out_q[...] = whole[:, :width]
    out_kv[0] = whole[:, width : 2 * width]
    out_kv[1] = whole[:, 2 * width : 3 * width]
    for at in range(0, out_o.shape[1], width):
        out_o[:, at : at + width] = whole[at : at + width, 3 * width :]


def self_final(role, total, other, out_qkv, out_o):
    width, wide = out_o.shape
    half = wide // 2
    whole = whole_bucket(role, total[:half], other[:half])
    for i in range(3):
        out_qkv[i] = whole[:, i * width : (i + 1) * width]
    for at in range(0, wide, width):
        out_o[:, at : at + width] = whole[at : at + width, 3 * width :]


def small_rows(total, out):
    rows, wide = out.shape
    block = total.shape[1]
    first = total.shape[0] - rows * wide // block
    for i, at in enumerate(range(0, wide, block)):
        out[:, at : at + block] = total[first + i * rows : first + (i + 1) * rows].astype(F32)


def add_pair(former, latter, out):
    out[...] = former[...] + latter[...]


def prepare(memory, wkv, bias, wq, padded, mk, mv, wq_t):
    rows = memory.shape[0]
    whole = -(-rows // 16) * 16
    if rows < mk.shape[0]:
        padded[whole - 16 :, :] = jnp.zeros((padded.shape[0] - whole + 16, padded.shape[1]), BF16)
    padded[0:rows, :] = memory[...]
    mk[...] = nn(padded[...], wkv[0]).astype(BF16)
    mv[...] = (nn(padded[...], wkv[1]) + row_of(bias, 1)).astype(BF16)
    wq_t[...] = jnp.transpose(wq[...])


def three_back(chips, *refs):
    first = refs[0]
    got = refs[1:chips]
    s3, gain, g_own, resid, message = refs[chips:]
    own = first.shape[0]
    total = first[...]
    for part in got:
        total = total + part[...].astype(F32)
    back, hat = norm_back(s3[...], row_of(gain, 2), total)
    grad = g_own[...].astype(F32) + back
    resid[...] = grad
    message[0:own, :] = grad.astype(BF16)
    sums = jnp.concatenate(
        [
            jnp.sum(total * hat, axis=0, keepdims=True),
            jnp.sum(total, axis=0, keepdims=True),
            jnp.zeros((14, total.shape[1]), F32),
        ],
        0,
    )
    message[own : own + 16, :] = sums.astype(BF16)


def cross_back(chips, group, ids, length, *refs):
    parts, refs = paired(refs, chips, group)
    wout, q_ref, mk, mv, lse, cg_ref, sums, dq_ref, dkv_ref, biases = refs[:10]
    up_ref, dk_acc, dv_acc = refs[10:]
    core, chip = ids[0] % 2, ids[0] // 2
    own = parts[0].shape[0] - 16
    norm_sums = jnp.zeros((2, cg_ref.shape[1]), F32)
    bias_sum = jnp.zeros((1, cg_ref.shape[1]), F32)
    for mask in range(chips):
        lo, hi = ordered(core, parts[2 * mask][...], parts[2 * mask + 1][...])
        norm_sums = norm_sums + lo[own : own + 2].astype(F32) + hi[own : own + 2].astype(F32)
        rows = jnp.concatenate([lo[:own], hi[:own]], 0)
        at = pl.ds(pl.multiple_of((chip ^ mask) * 2 * own, 2 * own), 2 * own)
        cg_ref[at, :] = rows
        bias_sum = bias_sum + jnp.sum(rows.astype(F32), axis=0, keepdims=True)
        up_ref[at, :] = nt(rows, wout[...]).astype(BF16)
    sums[...] = jnp.concatenate([norm_sums, bias_sum], 0)
    attend_back(q_ref, mk, mv, up_ref, lse, dq_ref, dk_acc, dv_acc, length[0], False)
    dkv_ref[0] = dk_acc[...].astype(BF16)
    dv = dv_acc[...].astype(BF16)
    dkv_ref[1] = dv
    biases[0:1, :] = jnp.sum(dq_ref[...].astype(F32), axis=0, keepdims=True)
    biases[1:2, :] = jnp.sum(dv.astype(F32), axis=0, keepdims=True)


def self_upstream(chips, group, ids, *refs):
    parts, refs = paired(refs, chips, group)
    wq, (s2_ref, gain, cg_ref, resid_two, wout) = refs[:2], refs[2:7]
    sg_ref, resid_one, sums, up_ref, base = refs[7:]
    own = resid_two.shape[0]
    mine = pl.ds(pl.multiple_of(ids[0] * own, own), own)
    base[...] = cg_ref[...].astype(F32)
    base[mine, :] = resid_two[...]
    sums[...] = jnp.zeros_like(sums[...])
    for row0 in range(0, s2_ref.shape[0], BLOCK):
        rows = pl.ds(row0, BLOCK)
        upstream = project_pairs(parts, *wq, 0, rows)
        back, hat = norm_back(s2_ref[rows, :], row_of(gain, 1), upstream)
        grad = base[rows, :] + back
        base[rows, :] = grad
        rounded = grad.astype(BF16)
        sg_ref[rows, :] = rounded
        sums[0:1, :] += jnp.sum(upstream * hat, axis=0, keepdims=True)
        sums[1:2, :] += jnp.sum(upstream, axis=0, keepdims=True)
        sums[2:3, :] += jnp.sum(rounded.astype(F32), axis=0, keepdims=True)
        up_ref[rows, :] = nt(rounded, wout[...]).astype(BF16)
    resid_one[...] = base[mine, :]


def self_back(qkv, up_ref, lse, grads, biases, dk_acc, dv_acc):
    attend_back(
        qkv.at[0], qkv.at[1], qkv.at[2], up_ref, lse, grads.at[0], dk_acc, dv_acc, None, True
    )
    grads[1] = dk_acc[...].astype(BF16)
    grads[2] = dv_acc[...].astype(BF16)
    biases[0:1, :] = jnp.sum(grads[0].astype(F32), axis=0, keepdims=True)
    biases[1:2, :] = jnp.sum(grads[2].astype(F32), axis=0, keepdims=True)


def one_back(chips, *refs):
    first = refs[0]
    got = refs[1:chips]
    x_own, gain, resid, out = refs[chips:]
    total = first[...]
    for part in got:
        total = total + part[...].astype(F32)
    back, _ = norm_back(x_own[...].astype(F32), row_of(gain, 0), total)
    out[...] = resid[...] + back


def on_device(
    layer_input,
    output_grad,
    memory,
    memory_length,
    norm_gain,
    norm_bias,
    self_qkv,
    self_bias,
    self_out,
    cross_query,
    cross_kv,
    cross_bias,
    cross_out,
    up_weight,
    up_bias,
    down_weight,
    out_bias,
):
    ranks = lax.axis_size("tensor")
    pages_ranks = lax.axis_size("dp")
    chips = ranks // 2
    rank = lax.axis_index("tensor")
    own, wide = layer_input.shape
    seq = own * ranks
    width = self_qkv.shape[2]
    heads = width // HEAD_DIM
    hidden = up_bias.shape[0]
    mem = memory.shape[0]
    mem_pad = -(-mem // 128) * 128

    line = lax.axis_index("dp")
    ids = jnp.reshape(rank, (1,)).astype(jnp.int32)
    role = jnp.reshape((line ^ (line >> 1)) & 1, (1,)).astype(jnp.int32)

    def swap(values, mask):
        return lax.ppermute(values, "tensor", [(i, i ^ mask) for i in range(ranks)])

    def far_parts(values):
        return [values] + [swap(values, 2 * mask) for mask in range(1, chips)]

    def hold(values, *tokens):
        return lax.optimization_barrier((values, *tokens))[0]

    def grouped(name):
        return min(NEAR.get(name, 1), chips)

    def packed(parts):
        shape = (len(parts), *parts[0].shape)
        return call(pack_all, [sds(shape, parts[0].dtype)], parts)[0]

    def near_parts(far, name):
        group = grouped(name)
        groups = [far[at : at + group] for at in range(0, chips, group)]
        return [*far, *(swap(packed(g) if group > 1 else g[0], 1) for g in groups)]

    def joined(former, latter, after):
        shape = (2 * former.shape[0], *former.shape[1:])
        return call(pack, [sds(shape, BF16)], [former, latter], after=after)[0]

    turns = [1 << at for at in range(1, ranks.bit_length() - 1)]

    def gather(values):
        return near_parts(far_parts(values))

    def along(values, pairs):
        return lax.ppermute(
            values,
            "dp",
            [(at + a, at + b) for at in range(0, pages_ranks, 4) for a, b in pairs],
        )

    outer = [(0, 1), (1, 0), (2, 3), (3, 2)]
    middle = [(0, 3), (3, 0), (1, 2), (2, 1)]
    def bucket(body, rows, ins, flops, after, scratch=()):
        half = sds((rows, 4 * width), BF16)
        keep, send = call(body, [half, half], [role, *ins], flops, scratch, after)
        return keep, along(send, outer)

    def across(state, after):
        keep, got = state
        inner = call(add_halves, [sds(keep.shape, BF16)], [keep, got], after=after)[0]
        return inner, along(inner, middle)

    def back_out(state, after):
        inner, got = state
        half = sds(inner.shape, BF16)
        total = call(add_halves, [half], [inner, got], after=after)[0]
        mask = 4
        while mask < pages_ranks:
            pairs = [(i, i ^ mask) for i in range(pages_ranks)]
            total = call(add_halves, [half], [total, lax.ppermute(total, "dp", pairs)])[0]
            mask *= 2
        return total, along(total, outer)

    def stacks(rows, columns, name):
        group = grouped(name)
        shape = (rows, columns) if group == 1 else (group, rows, columns)
        return [sds(shape, BF16)] * (chips // group)

    def sibling_terms(lhs, rhs, dot, after, name):
        rows = lhs.shape[1] // ranks
        columns = rhs.shape[1 if dot is nt else 2]
        return call(
            functools.partial(partial_sibling, chips, dot),
            stacks(rows, columns, name),
            [ids, lhs, rhs],
            lhs.size * columns,
            after=after,
        )

    def own_terms(lhs, rhs, dot, got, after):
        rows, columns = got[0].shape[-2:]
        return call(
            functools.partial(partial_own, chips, dot),
            [sds((rows, columns), F32)] + [sds((rows, columns), BF16)] * (chips - 1),
            [ids, lhs, rhs, *got],
            lhs.size * columns,
            after=after,
        )

    def scatter_far(sums):
        return [sums[0]] + [swap(sums[mask], 2 * mask) for mask in range(1, chips)]

    held, steps = {}, {}

    def fill(slot, kernel, far=()):
        tokens = [kernel, far[1:2], far[1:]][BASE.get(slot, 0)] if far else kernel
        for name in SLOTS[slot]:
            tokens = [steps[name](tokens)]
        return tokens if SLOTS[slot] else []

    x_far = far_parts(layer_input)
    padded, mem_keys, mem_values, query_t = call(
        prepare,
        [
            sds((mem_pad, wide), BF16),
            sds((mem_pad, width), BF16),
            sds((mem_pad, width), BF16),
            sds((width, wide), BF16),
        ],
        [memory, cross_kv, cross_bias, cross_query],
        4 * mem_pad * wide * width,
    )
    x_far = [layer_input] + [hold(part, mem_keys) for part in x_far[1:]]

    def gather_step(name, order, at, until=()):
        def step(after):
            block, got = held[name]
            block = joined(block, got, after)
            if at + 1 < len(order):
                held[name] = (block, swap(hold(block, *until()) if until else block, order[at + 1]))
            else:
                held[name] = (block, swap(block, 1))
            return block

        return step

    def begin(name, value, order, until=()):
        block = value[None]
        held[name] = (block, swap(hold(block, *until) if until else block, order[0]))
        steps[name + "1"] = gather_step(name, order, 0, lambda: holds.get(name, ()))
        for at in range(1, len(order)):
            steps[name + str(at + 1)] = gather_step(name, order, at)

    def finish(name, order):
        for at in range(2, len(order)):
            steps[name + str(at + 1)]([])
        return held[name]

    holds = {}
    forth, back = turns, turns[::-1]
    begin("so", self_out, forth)
    begin("co", cross_out, forth)
    begin("g", output_grad, back)
    if BASE.get("wq start", 0) == 2:
        begin("wq", query_t, forth)
    x_parts = near_parts(x_far, "x")
    x, hidden_one, qkv, self_mixed, self_lse = call(
        functools.partial(self_forward, chips, grouped("x")),
        [
            sds((seq, wide), BF16),
            sds((seq, wide), BF16),
            sds((3, seq, width), BF16),
            sds((seq, width), BF16),
            sds((heads, seq), F32),
        ],
        [ids, *x_parts, norm_gain, norm_bias, self_qkv, self_bias],
        2 * seq * wide * 3 * width + 4 * seq * seq * width,
        after=fill("x", [mem_keys, *x_far[1:]]),
    )
    tokens = fill("self", [self_mixed])
    mixed_far = far_parts(hold(self_mixed, *tokens) if tokens else self_mixed)
    holds["co"] = holds["g"] = mixed_far[1:]
    for name in ("co", "g"):
        if name + "1" in SLOTS["self"] or name + "1" in SLOTS["x"]:
            block, _ = held[name]
            held[name] = (block, swap(hold(block, *mixed_far[1:]), (forth if name == "co" else back)[1]))
    tokens = fill("mixed", [self_mixed], mixed_far)
    mixed_parts = near_parts(mixed_far, "mixed")
    so_block, so_other = finish("so", forth)
    stream_two, hidden_two, cross_q, cross_mixed, cross_lse = call(
        functools.partial(cross_forward, chips, grouped("mixed")),
        [
            sds((seq, wide), F32),
            sds((seq, wide), BF16),
            sds((seq, width), BF16),
            sds((seq, width), BF16),
            sds((heads, seq), F32),
        ],
        [
            memory_length,
            *mixed_parts,
            so_block,
            so_other,
            x,
            norm_gain,
            norm_bias,
            out_bias,
            cross_query,
            cross_bias,
            mem_keys,
            mem_values,
        ],
        2 * seq * wide * (wide + width) + 4 * seq * mem_pad * width,
        after=tokens,
    )
    if BASE.get("wq start", 0) == 1:
        begin("wq", query_t, forth, mixed_far[1:])
    cross_far = far_parts(cross_mixed)
    holds["wq"] = cross_far[1:]
    tokens = fill("cross", [cross_mixed], cross_far)
    cross_parts = near_parts(cross_far, "cross")
    co_block, co_other = finish("co", forth)
    g_block, g_other = finish("g", back)
    if BASE.get("wq start", 0) == 0:
        begin("wq", query_t, forth, cross_far[1:])
    stream_three, hidden_three, activated, pre_grad, whole_grad, grad_sum, up_bias_grad = call(
        functools.partial(mlp, chips, grouped("cross")),
        [
            sds((own, wide), F32),
            sds((seq, wide), BF16),
            sds((seq, hidden), BF16),
            sds((seq, hidden), BF16),
            sds((seq, wide), BF16),
            sds((1, wide), F32),
            sds((1, hidden), F32),
        ],
        [
            ids,
            *cross_parts,
            co_block,
            co_other,
            g_block,
            g_other,
            stream_two,
            norm_gain,
            norm_bias,
            out_bias,
            up_weight,
            up_bias.reshape(1, -1),
            down_weight,
        ],
        2 * seq * wide * (wide + 2 * hidden),
        [pltpu.VMEM((2 * own, wide), F32)],
        after=tokens,
    )

    def step(name):
        return lambda function: steps.__setitem__(name, function)

    @step("bucket m")
    def _(after):
        held["m"] = bucket(
            mlp_bucket,
            wide,
            [activated, whole_grad, hidden_three, pre_grad],
            4 * seq * wide * hidden,
            after,
        )
        return held["m"][0]

    def mover(key, function):
        def run(after):
            held[key] = function(held[key], after)
            return held[key][0]

        return run

    for key in "mca":
        steps["add " + key] = mover(key, across)
        steps["out " + key] = mover(key, back_out)

    up_item, pre_item = up_weight[None], pre_grad[None]
    sibling = sibling_terms(pre_item, up_item, nt, fill("mlp", [pre_grad]), "three")
    got = [swap(part, 1) for part in sibling]
    three_sums = own_terms(pre_item, up_item, nt, got, fill("three", [sibling[0]]))
    three_far = scatter_far(three_sums)
    resid_two, message = call(
        functools.partial(three_back, chips),
        [sds((own, wide), F32), sds((own + 16, wide), BF16)],
        [*three_far, stream_three, norm_gain, output_grad],
        after=fill("three far", [three_sums[0]], three_far),
    )
    cg_far = far_parts(message)
    cg_parts = near_parts(cg_far, "grad")
    cross_grad, cross_sums, dq2, dkv2, cross_bias_grad = call(
        functools.partial(cross_back, chips, grouped("grad")),
        [
            sds((seq, wide), BF16),
            sds((3, wide), F32),
            sds((seq, width), BF16),
            sds((2, mem_pad, width), BF16),
            sds((2, width), F32),
        ],
        [
            ids,
            memory_length,
            *cg_parts,
            cross_out,
            cross_q,
            mem_keys,
            mem_values,
            cross_lse,
        ],
        2 * seq * wide * width + 10 * seq * mem_pad * width,
        [
            pltpu.VMEM((seq, width), BF16),
            pltpu.VMEM((mem_pad, width), F32),
            pltpu.VMEM((mem_pad, width), F32),
        ],
        after=fill("grad far", [message], cg_far),
    )
    dq2_far = far_parts(dq2)

    @step("bucket c")
    def _(after):
        held["c"] = bucket(
            cross_bucket,
            wide // 2,
            [hidden_two, dq2, padded, dkv2, cross_mixed, cross_grad],
            8 * seq * wide * width,
            after,
        )
        return held["c"][0]

    tokens = fill("query far", [dq2], dq2_far)
    dq2_parts = near_parts(dq2_far, "query")
    wq_block, wq_other = finish("wq", forth)
    self_grad, resid_one, self_sums, self_up = call(
        functools.partial(self_upstream, chips, grouped("query")),
        [
            sds((seq, wide), BF16),
            sds((own, wide), F32),
            sds((3, wide), F32),
            sds((seq, width), BF16),
        ],
        [
            ids,
            *dq2_parts,
            wq_block,
            wq_other,
            stream_two,
            norm_gain,
            cross_grad,
            resid_two,
            self_out,
        ],
        2 * seq * wide * (wide + width),
        [pltpu.VMEM((seq, wide), F32)],
        after=tokens,
    )
    grads, self_bias_grad = call(
        self_back,
        [sds((3, seq, width), BF16), sds((2, width), F32)],
        [qkv, self_up, self_lse],
        10 * seq * seq * width,
        [pltpu.VMEM((seq, width), F32), pltpu.VMEM((seq, width), F32)],
        after=fill("up", [self_up]),
    )

    @step("bucket a")
    def _(after):
        held["a"] = bucket(
            self_bucket,
            wide // 2 + 4 * wide // width,
            [
                hidden_one,
                grads,
                self_mixed,
                self_grad,
                self_qkv,
                norm_gain,
                norm_bias,
                self_sums,
                cross_sums,
                grad_sum,
                self_bias_grad,
                cross_bias_grad,
                up_bias_grad,
            ],
            8 * seq * wide * width,
            after,
            [pltpu.VMEM((16, wide), F32)],
        )
        return held["a"][0]

    sibling = sibling_terms(grads, self_qkv, nt, fill("back", [grads]), "one")
    got = [swap(part, 1) for part in sibling]
    one_sums = own_terms(grads, self_qkv, nt, got, fill("one", [sibling[0]]))
    one_far = scatter_far(one_sums)
    (input_grad,) = call(
        functools.partial(one_back, chips),
        [sds((own, wide), F32)],
        [*one_far, layer_input, norm_gain, resid_one],
        after=fill("one far", [one_sums[0]], one_far),
    )
    tokens = fill("input", [input_grad])
    last_ins = [ids, activated, down_weight, cross_kv, dkv2]
    sibling = call(
        functools.partial(last_sibling, chips),
        stacks(own, wide + mem_pad, "last"),
        last_ins,
        after=tokens,
    )
    got = [swap(part, 1) for part in sibling]
    last = call(
        functools.partial(last_own, chips),
        [sds((own, wide + mem_pad), F32)]
        + [sds((own, wide + mem_pad), BF16)] * (chips - 1),
        [*last_ins, *got],
        after=fill("last", [sibling[0]]),
    )
    last_far = scatter_far(last)

    @step("final m")
    def _(after):
        held["final m"] = call(
            mlp_final,
            [sds((hidden, wide), F32), sds((wide, hidden), F32)],
            [role, *held["m"]],
            after=after,
        )
        return held["final m"][0]

    @step("final c")
    def _(after):
        held["final c"] = call(
            cross_final,
            [sds((wide, width), F32), sds((2, wide, width), F32), sds((width, wide), F32)],
            [role, *held["c"]],
            after=after,
        )
        return held["final c"][0]

    @step("last final")
    def _(after):
        held["last final"] = call(
            functools.partial(last_final, chips),
            [sds((own, wide), BF16), sds((mem, wide // ranks), F32)],
            [*last_far, stream_three, out_bias],
            after=after,
        )
        return held["last final"][0]

    out_a = steps["out a"]

    @step("out a")
    def _(after):
        total = out_a(after)
        small = call(small_rows, [sds((16, wide), F32)], [total])[0]
        pair = call(add_pair, [sds((16, wide), F32)], [small, swap(small, 1)])[0]
        held["small"] = [small, *far_parts(pair)]
        return small

    fill("last far", [last[0]], last_far)
    tokens = fill("end", [held["last final"][0]] if "last final" in held else [last[0]])
    gains, shifts, outs, self_bias_sum, cross_bias_sum, up_bias_sum = call(
        small_final,
        [sds((3, wide), F32)] * 3
        + [sds((2, width), F32), sds((2, width), F32), sds((1, hidden), F32)],
        held["small"],
        after=tokens,
    )
    self_qkv_grad, self_out_grad = call(
        self_final,
        [sds((3, wide, width), F32), sds((width, wide), F32)],
        [role, *held["a"]],
        after=[gains],
    )
    output, memory_grad = held["last final"]
    down_grad, up_grad = held["final m"]
    cross_query_grad, cross_kv_grad, cross_out_grad = held["final c"]
    return (
        output,
        input_grad,
        memory_grad,
        gains,
        shifts,
        self_qkv_grad,
        self_bias_sum,
        self_out_grad,
        cross_query_grad,
        cross_kv_grad,
        cross_bias_sum,
        cross_out_grad,
        up_grad,
        up_bias_sum.reshape(-1),
        down_grad,
        outs,
    )


def solution(mesh):
    return jax.shard_map(
        on_device,
        mesh=mesh,
        in_specs=(
            P(("dp", "tensor"), None),
            P(("dp", "tensor"), None),
            P("dp", None),
            P("dp"),
            P(),
            P(),
            P(None, None, "tensor"),
            P(None, "tensor"),
            P("tensor", None),
            P(None, "tensor"),
            P(None, None, "tensor"),
            P(None, "tensor"),
            P("tensor", None),
            P(None, "tensor"),
            P("tensor"),
            P("tensor", None),
            P(),
        ),
        out_specs=(
            P(("dp", "tensor"), None),
            P(("dp", "tensor"), None),
            P("dp", "tensor"),
            P(),
            P(),
            P(None, None, "tensor"),
            P(None, "tensor"),
            P("tensor", None),
            P(None, "tensor"),
            P(None, None, "tensor"),
            P(None, "tensor"),
            P("tensor", None),
            P(None, "tensor"),
            P("tensor"),
            P("tensor", None),
            P(),
        ),
        check_vma=False,
    )
```

```python
import functools

import jax
import jax.numpy as jnp
from jax import lax
from jax.experimental import pallas as pl
from jax.experimental.pallas import tpu as pltpu
from jax.sharding import PartitionSpec as P

HEAD_DIM = 64
EPS = 1e-05
NEG = -1e30
BLOCK = 256
FACTOR = HEAD_DIM ** (-0.5)
F32 = jnp.float32
BF16 = jnp.bfloat16

def nn(a, b):
    return lax.dot_general(a, b, (((1,), (0,)), ((), ())), preferred_element_type=F32)


def nt(a, b):
    return lax.dot_general(a, b, (((1,), (1,)), ((), ())), preferred_element_type=F32)


SLOTS = {
    "x": ["so1"],
    "self": ["co1", "g1"],
    "mixed": ["so2"],
    "cross": ["co2", "g2"],
    "mlp": [],
    "three": ["wq1"],
    "three far": ["bucket m"],
    "grad far": ["wq2", "add m"],
    "query far": ["bucket c"],
    "up": [],
    "back": [],
    "one": ["out m", "bucket a"],
    "one far": ["add c"],
    "input": ["add a"],
    "last": ["out c"],
    "last far": ["final m", "out a", "final c", "last final"],
    "end": [],
}
BASE = {"mixed": 2, "cross": 2, "grad far": 2, "query far": 2}
NEAR = {}
LOAD = {"three_back": 4, "last_final": 2}
UNIT = 1.8e9
WEIGHT = 0.12


def call(body, outs, ins, flops=0, scratch=(), after=(), vmem=8):
    inside = pl.BlockSpec(memory_space=pltpu.VMEM)
    scalar = pl.BlockSpec(memory_space=pltpu.SMEM)
    count, tokens = len(ins), len(after)
    name = getattr(body, "func", body).__name__
    nbytes = sum(a.size * a.dtype.itemsize for a in ins)
    nbytes += sum(o.size * o.dtype.itemsize for o in outs)

    def kernel(*refs):
        body(*refs[:count], *refs[count + tokens :])

    return pl.pallas_call(
        kernel,
        name=name,
        out_shape=tuple(outs),
        in_specs=[scalar if a.dtype == jnp.int32 else inside for a in ins]
        + [pl.BlockSpec(memory_space=pl.ANY)] * tokens,
        out_specs=tuple(inside for _ in outs),
        scratch_shapes=list(scratch),
        compiler_params=pltpu.CompilerParams(vmem_limit_bytes=vmem * 2**20),
        cost_estimate=pl.CostEstimate(
            flops=int(flops * WEIGHT + UNIT * LOAD.get(name, 0)),
            bytes_accessed=int(nbytes * WEIGHT),
            transcendentals=0,
        ),
    )(*ins, *after)


def sds(shape, dtype):
    return jax.ShapeDtypeStruct(shape, dtype)


def normed(values):
    centre = values - jnp.mean(values, axis=-1, keepdims=True)
    spread = jnp.mean(centre * centre, axis=-1, keepdims=True)
    scale = lax.rsqrt(spread + EPS)
    return centre * scale, scale


def norm_back(values, gain, upstream):
    hat, scale = normed(values)
    scaled = upstream * gain
    first = jnp.mean(scaled, axis=-1, keepdims=True)
    second = jnp.mean(scaled * hat, axis=-1, keepdims=True)
    return scale * (scaled - first - hat * second), hat


def row_of(ref, row):
    return ref[row : row + 1, :].astype(F32)


def ordered(core, own, other):
    return jnp.where(core == 0, own, other), jnp.where(core == 0, other, own)


def heads_only(values, head, heads):
    if heads == 1:
        return values
    lane = lax.broadcasted_iota(jnp.int32, values.shape, 1)
    return jnp.where(lane // HEAD_DIM == head, values, jnp.zeros_like(values))


def key_tiles(total, limit):
    return [(at, min(BLOCK, limit - at)) for at in range(0, limit, BLOCK)]


def allowed_tile(at, width, row0, length, causal):
    key_at = at + lax.broadcasted_iota(jnp.int32, (width, BLOCK), 0)
    if causal:
        return key_at <= row0 + lax.broadcasted_iota(jnp.int32, (width, BLOCK), 1)
    return key_at < length


def scores_tile(k_ref, query, at, width, row0, length, causal):
    scores = nt(k_ref[at : at + width, :], query)
    if causal and at + width <= row0:
        return scores
    return jnp.where(allowed_tile(at, width, row0, length, causal), scores, NEG)


def attend(q_ref, k_ref, v_ref, mixed_ref, lse_ref, length, causal):
    seq, width = q_ref.shape
    keys = k_ref.shape[0]
    heads = width // HEAD_DIM
    value_t = jnp.transpose(v_ref[...])
    for row0 in range(0, seq, BLOCK):
        query = q_ref[row0 : row0 + BLOCK, :]
        tiles = key_tiles(keys, row0 + BLOCK if causal else keys)
        columns = []
        for head in range(heads):
            own = heads_only(query, head, heads)
            scores = [scores_tile(k_ref, own, at, w, row0, length, causal) for at, w in tiles]
            peak = functools.reduce(
                jnp.maximum, [jnp.max(s, axis=0, keepdims=True) for s in scores]
            )
            total = jnp.zeros_like(peak)
            mixed = jnp.zeros((HEAD_DIM, BLOCK), F32)
            for (at, w), s in zip(tiles, scores):
                raised = jnp.exp(s - peak)
                total = total + jnp.sum(raised, axis=0, keepdims=True)
                rows = value_t[head * HEAD_DIM : (head + 1) * HEAD_DIM, at : at + w]
                mixed = mixed + nn(rows, raised.astype(BF16))
            columns.append(mixed * (1.0 / total))
            lse_ref[head : head + 1, row0 : row0 + BLOCK] = peak + jnp.log(total)
        mixed_ref[row0 : row0 + BLOCK, :] = jnp.transpose(jnp.concatenate(columns, 0)).astype(BF16)


def attend_back(q_ref, k_ref, v_ref, up_ref, lse_ref, dq_ref, dk_acc, dv_acc, length, causal):
    seq, width = q_ref.shape
    keys = k_ref.shape[0]
    heads = width // HEAD_DIM
    key_t = jnp.transpose(k_ref[...])
    dk_acc[...] = jnp.zeros_like(dk_acc)
    dv_acc[...] = jnp.zeros_like(dv_acc)
    for row0 in range(0, seq, BLOCK):
        query = q_ref[row0 : row0 + BLOCK, :]
        upstream = up_ref[row0 : row0 + BLOCK, :]
        tiles = key_tiles(keys, row0 + BLOCK if causal else keys)
        columns = []
        for head in range(heads):
            own = heads_only(query, head, heads)
            own_up = heads_only(upstream, head, heads)
            lse = lse_ref[head : head + 1, row0 : row0 + BLOCK]
            weights, grads = [], []
            inner = jnp.zeros((1, BLOCK), F32)
            for at, w in tiles:
                weight = jnp.exp(scores_tile(k_ref, own, at, w, row0, length, causal) - lse)
                grad = nt(v_ref[at : at + w, :], own_up)
                inner = inner + jnp.sum(weight * grad, axis=0, keepdims=True)
                weights.append(weight)
                grads.append(grad)
            column = jnp.zeros((HEAD_DIM, BLOCK), F32)
            for (at, w), weight, grad in zip(tiles, weights, grads):
                score_grad = (weight * (grad - inner)).astype(BF16)
                dv_acc[at : at + w, :] += nn(weight.astype(BF16), own_up)
                dk_acc[at : at + w, :] += nn(score_grad, own)
                rows = key_t[head * HEAD_DIM : (head + 1) * HEAD_DIM, at : at + w]
                column = column + nn(rows, score_grad)
            columns.append(column * FACTOR)
        dq_ref[row0 : row0 + BLOCK, :] = jnp.transpose(jnp.concatenate(columns, 0)).astype(BF16)


def self_forward(chips, group, ids, *refs):
    parts, refs = paired(refs, chips, group)
    gain, shift, wqkv, bias, x_ref, h_ref, qkv_ref, mixed_ref, lse_ref = refs
    core, chip = ids[0] % 2, ids[0] // 2
    own = parts[0].shape[0]
    for mask in range(chips):
        lo, hi = ordered(core, parts[2 * mask][...], parts[2 * mask + 1][...])
        rows = jnp.concatenate([lo, hi], 0)
        at = pl.ds(pl.multiple_of((chip ^ mask) * 2 * own, 2 * own), 2 * own)
        x_ref[at, :] = rows
        hat, _ = normed(rows.astype(F32))
        hidden = (hat * row_of(gain, 0) + row_of(shift, 0)).astype(BF16)
        h_ref[at, :] = hidden
        query = nn(hidden, wqkv[0]) + row_of(bias, 0)
        qkv_ref[0, at, :] = (query.astype(BF16).astype(F32) * FACTOR).astype(BF16)
        qkv_ref[1, at, :] = nn(hidden, wqkv[1]).astype(BF16)
        qkv_ref[2, at, :] = (nn(hidden, wqkv[2]) + row_of(bias, 1)).astype(BF16)
    attend(qkv_ref.at[0], qkv_ref.at[1], qkv_ref.at[2], mixed_ref, lse_ref, None, True)


def paired(refs, chips, group):
    parts = []
    for mask in range(chips):
        other = refs[chips + mask // group]
        parts += [refs[mask], other if group == 1 else other.at[mask % group]]
    return parts, refs[chips + chips // group :]


def project_pairs(parts, mine, other, first, rows):
    width = parts[0].shape[1]
    total = None
    for mask in range(len(parts) // 2):
        lhs = [parts[2 * mask][rows, :], parts[2 * mask + 1][rows, :]]
        rhs = [ref[mask, first : first + width, :] for ref in (mine, other)]
        if width % 128 == 0:
            term = nn(jnp.concatenate(lhs, 1), jnp.concatenate(rhs, 0))
        else:
            term = nn(lhs[0], rhs[0]) + nn(lhs[1], rhs[1])
        total = term if total is None else total + term
    return total


def pack_all(*refs):
    for i, ref in enumerate(refs[:-1]):
        refs[-1][i] = ref[...]


def turned_place(mask, chips):
    bits = chips.bit_length() - 1
    return sum(((mask >> i) & 1) << (bits - 1 - i) for i in range(bits))


def pack(former, latter, out):
    count = former.shape[0]
    out[:count] = former[...]
    out[count:] = latter[...]


def cross_forward(chips, group, length, *refs):
    parts, refs = paired(refs, chips, group)
    wout, (x_ref, gain, shift, out_bias, wq, bias, mk, mv) = refs[:2], refs[2:10]
    s2_ref, h_ref, q_ref, mixed_ref, lse_ref = refs[10:]
    for row0 in range(0, x_ref.shape[0], BLOCK):
        rows = pl.ds(row0, BLOCK)
        branch = project_pairs(parts, *wout, 0, rows) + row_of(out_bias, 0)
        stream = x_ref[rows, :].astype(F32) + branch
        s2_ref[rows, :] = stream
        hat, _ = normed(stream)
        hidden = (hat * row_of(gain, 1) + row_of(shift, 1)).astype(BF16)
        h_ref[rows, :] = hidden
        query = (nn(hidden, wq[...]) + row_of(bias, 0)).astype(BF16).astype(F32)
        q_ref[rows, :] = (query * FACTOR).astype(BF16)
    attend(q_ref, mk, mv, mixed_ref, lse_ref, length[0], False)


def mlp(chips, group, ids, *refs):
    parts, refs = paired(refs, chips, group)
    wout, (grad_in, grad_other) = refs[:2], refs[2:4]
    (s2_ref, gain, shift, out_bias, wup, bup, wdown) = refs[4:11]
    s3_own, h_ref, act_ref, pg_ref, g_ref, sums, ups, s3 = refs[11:]
    core, chip = ids[0] % 2, ids[0] // 2
    own = s3_own.shape[0]
    sums[...] = jnp.zeros_like(sums[...])
    ups[...] = jnp.zeros_like(ups[...])
    for mask in range(chips):
        rows = pl.ds(pl.multiple_of((chip ^ mask) * 2 * own, 2 * own), 2 * own)
        branch = project_pairs(parts, *wout, 0, rows) + row_of(out_bias, 1)
        stream = s2_ref[rows, :] + branch
        if mask == 0:
            s3[...] = stream
            s3_own[...] = s3[pl.ds(pl.multiple_of(core * own, own), own), :]
        hat, _ = normed(stream)
        hidden = (hat * row_of(gain, 2) + row_of(shift, 2)).astype(BF16)
        h_ref[rows, :] = hidden
        pre = nn(hidden, wup[...]) + bup[...].astype(F32)
        half = 0.5 * (1.0 + lax.erf(pre * (0.5**0.5)))
        act_ref[rows, :] = (pre * half).astype(BF16)
        slope = half + pre * jnp.exp(-0.5 * pre * pre) * 0.3989422804014327
        lo, hi = ordered(core, grad_in[turned_place(mask, chips)], grad_other[turned_place(mask, chips)])
        grad = jnp.concatenate([lo, hi], 0)
        g_ref[rows, :] = grad
        pre_grad = (nt(grad, wdown[...]) * slope).astype(BF16)
        pg_ref[rows, :] = pre_grad
        ups[...] += jnp.sum(pre_grad.astype(F32), axis=0, keepdims=True)
        sums[...] += jnp.sum(grad.astype(F32), axis=0, keepdims=True)


def rows_for(ref, chip, core, own, chips):
    picks = []
    for mask in range(chips):
        at = pl.multiple_of(((chip ^ mask) * 2 + core) * own, own)
        picks.append(ref[pl.ds(at, own), :])
    return jnp.concatenate(picks, 0)


def picked_terms(lhs, rhs, dot, chip, core, own, chips):
    total = None
    for i in range(lhs.shape[0]):
        term = dot(rows_for(lhs.at[i], chip, core, own, chips), rhs[i])
        total = term if total is None else total + term
    return total


def member(refs, mask, group):
    return refs[mask] if group == 1 else refs[mask // group].at[mask % group]


def partial_sibling(chips, dot, ids, lhs, rhs, *outs):
    own, group = outs[0].shape[-2], chips // len(outs)
    total = picked_terms(lhs, rhs, dot, ids[0] // 2, 1 - ids[0] % 2, own, chips)
    for mask in range(chips):
        member(outs, mask, group)[...] = total[mask * own : (mask + 1) * own].astype(BF16)


def partial_own(chips, dot, ids, lhs, rhs, *refs):
    swaps = len(refs) - chips
    got, (first, *sends) = refs[:swaps], refs[swaps:]
    own, group = first.shape[0], chips // swaps
    total = picked_terms(lhs, rhs, dot, ids[0] // 2, ids[0] % 2, own, chips)
    for mask in list(range(1, chips)) + [0]:
        block = total[mask * own : (mask + 1) * own]
        block = block + member(got, mask, group)[...].astype(F32)
        if mask == 0:
            first[...] = block
        else:
            sends[mask - 1][...] = block.astype(BF16)


def last_sibling(chips, ids, act, wdown, wkv, dkv, *outs):
    own, wide = act.shape[0] // (2 * chips), wdown.shape[1]
    chip, core = ids[0] // 2, 1 - ids[0] % 2
    total = nn(rows_for(act, chip, core, own, chips), wdown[...])
    turned_grad = picked_terms(wkv, dkv, nt, chip, core, own, chips)
    for mask in range(chips):
        rows = slice(mask * own, (mask + 1) * own)
        out = member(outs, mask, chips // len(outs))
        out[:, :wide] = total[rows].astype(BF16)
        out[:, wide:] = turned_grad[rows].astype(BF16)


def last_own(chips, ids, act, wdown, wkv, dkv, *refs):
    swaps = len(refs) - chips
    parts, (first, *sends) = refs[:swaps], refs[swaps:]
    own, wide = act.shape[0] // (2 * chips), wdown.shape[1]
    chip, core = ids[0] // 2, ids[0] % 2
    total = nn(rows_for(act, chip, core, own, chips), wdown[...])
    turned_grad = picked_terms(wkv, dkv, nt, chip, core, own, chips)
    for mask in range(chips):
        rows = slice(mask * own, (mask + 1) * own)
        out = first if mask == 0 else sends[mask - 1]
        got = member(parts, mask, chips // swaps)[...].astype(F32)
        out[:, :wide] = (total[rows] + got[:, :wide]).astype(out.dtype)
        out[:, wide:] = (turned_grad[rows] + got[:, wide:]).astype(out.dtype)


def last_final(chips, *refs):
    parts, (stream, bias, out, memory) = refs[:chips], refs[chips:]
    wide = out.shape[1]
    total = parts[0][...]
    for part in parts[1:]:
        total = total + part[...].astype(F32)
    out[...] = (total[:, :wide] + stream[...] + row_of(bias, 2)).astype(BF16)
    memory[...] = jnp.transpose(total[:, wide:])[: memory.shape[0]]


def small_final(small, *refs):
    parts, (gains, shifts, outs, self_bias, cross_bias, up_bias) = refs[:-6], refs[-6:]
    norm = parts[0][0:2, :]
    for part in parts[1:]:
        norm = norm + part[0:2, :]
    gains[0:1, :] = norm[0:1]
    shifts[0:1, :] = norm[1:2]
    for i, (gain, shift, out) in enumerate(((0, 1, 4), (2, 3, 7), (5, 6, 8))):
        if i:
            gains[i : i + 1, :] = small[gain : gain + 1, :]
            shifts[i : i + 1, :] = small[shift : shift + 1, :]
        outs[i : i + 1, :] = small[out : out + 1, :]
    width = self_bias.shape[1]
    self_bias[...] = small[9:11, :width]
    cross_bias[...] = small[11:13, :width]
    up_bias[...] = small[13:14, : up_bias.shape[1]]


def stacked(values, block):
    return jnp.concatenate(
        [values[:, at : at + block] for at in range(0, values.shape[1], block)], 0
    )


def turned(lhs, rhs):
    return nn(jnp.transpose(lhs), rhs).astype(BF16)


def split_bucket(role, columns, keep, send):
    half = keep.shape[0]
    for at, block in columns:
        top, bottom = block[:half], block[half:]
        width = block.shape[1]
        keep[:, at : at + width] = jnp.where(role[0] == 0, top, bottom)
        send[:, at : at + width] = jnp.where(role[0] == 0, bottom, top)


def mlp_bucket(role, act, grad, hidden, pre_grad, keep, send):
    down = stacked(turned(act[...], grad[...]), act.shape[1])
    up = jnp.transpose(turned(pre_grad[...], hidden[...]))
    keep[...] = jnp.where(role[0] == 0, down, up)
    send[...] = jnp.where(role[0] == 0, up, down)


def cross_bucket(role, hidden, dq, padded, dkv, mixed, grad, keep, send):
    width = dq.shape[1]
    columns = [(0, jnp.transpose(turned(dq[...], hidden[...])))]
    for i in range(2):
        columns.append(((1 + i) * width, jnp.transpose(turned(dkv[i], padded[...]))))
    columns.append((3 * width, stacked(turned(mixed[...], grad[...]), width)))
    split_bucket(role, columns, keep, send)


def self_bucket(role, hidden, grads, mixed, grad, wqkv, gain, shift, *refs):
    self_sums, cross_sums, grad_sum, self_bias, cross_bias, up_bias, keep, send, small = refs
    width = mixed.shape[1]
    columns = []
    products = jnp.zeros((1, hidden.shape[1]), F32)
    sums = jnp.zeros((1, hidden.shape[1]), F32)
    for i in range(3):
        turned_grads = jnp.transpose(grads[i])
        weight_grad = nn(turned_grads, hidden[...])
        weight = jnp.transpose(wqkv[i]).astype(F32)
        total = jnp.sum(turned_grads.astype(F32), axis=1, keepdims=True)
        products = products + jnp.sum(weight * weight_grad, axis=0, keepdims=True)
        sums = sums + jnp.sum(weight * total, axis=0, keepdims=True)
        columns.append((i * width, jnp.transpose(weight_grad.astype(BF16))))
    columns.append((3 * width, stacked(turned(mixed[...], grad[...]), width)))
    half = keep.shape[0] - small.size // (4 * width)
    for at, block in columns:
        top, bottom = block[:half], block[half:]
        place = slice(at, at + block.shape[1])
        keep[:half, place] = jnp.where(role[0] == 0, top, bottom)
        send[:half, place] = jnp.where(role[0] == 0, bottom, top)
    small[...] = jnp.zeros_like(small[...])
    small[0:1, :] = (products - row_of(shift, 0) * sums) / row_of(gain, 0)
    small[1:2, :] = sums
    small[2:5, :] = self_sums[...]
    small[5:8, :] = cross_sums[...]
    small[8:9, :] = grad_sum[...]
    for i in range(2):
        small[9 + i : 10 + i, :width] = self_bias[i : i + 1, :]
        small[11 + i : 12 + i, :width] = cross_bias[i : i + 1, :]
    small[13:14, : up_bias.shape[1]] = up_bias[...]
    rows = stacked(small[...], 4 * width).astype(BF16)
    keep[half:, :] = rows
    send[half:, :] = rows


def add_halves(former, latter, out):
    out[...] = (former[...].astype(F32) + latter[...].astype(F32)).astype(BF16)


def whole_bucket(role, total, other):
    mine, theirs = total[...].astype(F32), other[...].astype(F32)
    return jnp.concatenate(
        [jnp.where(role[0] == 0, mine, theirs), jnp.where(role[0] == 0, theirs, mine)], 0
    )


def mlp_final(role, total, other, out_down, out_up):
    mine, theirs = total[...].astype(F32), other[...].astype(F32)
    down = jnp.where(role[0] == 0, mine, theirs)
    out_up[...] = jnp.where(role[0] == 0, theirs, mine)
    rows = out_down.shape[0]
    for at in range(0, out_down.shape[1], rows):
        out_down[:, at : at + rows] = down[at : at + rows]


def cross_final(role, total, other, out_q, out_kv, out_o):
    width = out_q.shape[1]
    whole = whole_bucket(role, total, other)
    out_q[...] = whole[:, :width]
    out_kv[0] = whole[:, width : 2 * width]
    out_kv[1] = whole[:, 2 * width : 3 * width]
    for at in range(0, out_o.shape[1], width):
        out_o[:, at : at + width] = whole[at : at + width, 3 * width :]


def self_final(role, total, other, out_qkv, out_o):
    width, wide = out_o.shape
    half = wide // 2
    whole = whole_bucket(role, total[:half], other[:half])
    for i in range(3):
        out_qkv[i] = whole[:, i * width : (i + 1) * width]
    for at in range(0, wide, width):
        out_o[:, at : at + width] = whole[at : at + width, 3 * width :]


def small_rows(total, out):
    rows, wide = out.shape
    block = total.shape[1]
    first = total.shape[0] - rows * wide // block
    for i, at in enumerate(range(0, wide, block)):
        out[:, at : at + block] = total[first + i * rows : first + (i + 1) * rows].astype(F32)


def add_pair(former, latter, out):
    out[...] = former[...] + latter[...]


def prepare(memory, wkv, bias, wq, padded, mk, mv, wq_t):
    rows = memory.shape[0]
    whole = -(-rows // 16) * 16
    if rows < mk.shape[0]:
        padded[whole - 16 :, :] = jnp.zeros((padded.shape[0] - whole + 16, padded.shape[1]), BF16)
    padded[0:rows, :] = memory[...]
    mk[...] = nn(padded[...], wkv[0]).astype(BF16)
    mv[...] = (nn(padded[...], wkv[1]) + row_of(bias, 1)).astype(BF16)
    wq_t[...] = jnp.transpose(wq[...])


def three_back(chips, *refs):
    first = refs[0]
    got = refs[1:chips]
    s3, gain, g_own, resid, message = refs[chips:]
    own = first.shape[0]
    total = first[...]
    for part in got:
        total = total + part[...].astype(F32)
    back, hat = norm_back(s3[...], row_of(gain, 2), total)
    grad = g_own[...].astype(F32) + back
    resid[...] = grad
    message[0:own, :] = grad.astype(BF16)
    sums = jnp.concatenate(
        [
            jnp.sum(total * hat, axis=0, keepdims=True),
            jnp.sum(total, axis=0, keepdims=True),
            jnp.zeros((14, total.shape[1]), F32),
        ],
        0,
    )
    message[own : own + 16, :] = sums.astype(BF16)


def cross_back(chips, group, ids, length, *refs):
    parts, refs = paired(refs, chips, group)
    wout, q_ref, mk, mv, lse, cg_ref, sums, dq_ref, dkv_ref, biases = refs[:10]
    up_ref, dk_acc, dv_acc = refs[10:]
    core, chip = ids[0] % 2, ids[0] // 2
    own = parts[0].shape[0] - 16
    norm_sums = jnp.zeros((2, cg_ref.shape[1]), F32)
    bias_sum = jnp.zeros((1, cg_ref.shape[1]), F32)
    for mask in range(chips):
        lo, hi = ordered(core, parts[2 * mask][...], parts[2 * mask + 1][...])
        norm_sums = norm_sums + lo[own : own + 2].astype(F32) + hi[own : own + 2].astype(F32)
        rows = jnp.concatenate([lo[:own], hi[:own]], 0)
        at = pl.ds(pl.multiple_of((chip ^ mask) * 2 * own, 2 * own), 2 * own)
        cg_ref[at, :] = rows
        bias_sum = bias_sum + jnp.sum(rows.astype(F32), axis=0, keepdims=True)
        up_ref[at, :] = nt(rows, wout[...]).astype(BF16)
    sums[...] = jnp.concatenate([norm_sums, bias_sum], 0)
    attend_back(q_ref, mk, mv, up_ref, lse, dq_ref, dk_acc, dv_acc, length[0], False)
    dkv_ref[0] = dk_acc[...].astype(BF16)
    dv = dv_acc[...].astype(BF16)
    dkv_ref[1] = dv
    biases[0:1, :] = jnp.sum(dq_ref[...].astype(F32), axis=0, keepdims=True)
    biases[1:2, :] = jnp.sum(dv.astype(F32), axis=0, keepdims=True)


def self_upstream(chips, group, ids, *refs):
    parts, refs = paired(refs, chips, group)
    wq, (s2_ref, gain, cg_ref, resid_two, wout) = refs[:2], refs[2:7]
    sg_ref, resid_one, sums, up_ref, base = refs[7:]
    own = resid_two.shape[0]
    mine = pl.ds(pl.multiple_of(ids[0] * own, own), own)
    base[...] = cg_ref[...].astype(F32)
    base[mine, :] = resid_two[...]
    sums[...] = jnp.zeros_like(sums[...])
    for row0 in range(0, s2_ref.shape[0], BLOCK):
        rows = pl.ds(row0, BLOCK)
        upstream = project_pairs(parts, *wq, 0, rows)
        back, hat = norm_back(s2_ref[rows, :], row_of(gain, 1), upstream)
        grad = base[rows, :] + back
        base[rows, :] = grad
        rounded = grad.astype(BF16)
        sg_ref[rows, :] = rounded
        sums[0:1, :] += jnp.sum(upstream * hat, axis=0, keepdims=True)
        sums[1:2, :] += jnp.sum(upstream, axis=0, keepdims=True)
        sums[2:3, :] += jnp.sum(rounded.astype(F32), axis=0, keepdims=True)
        up_ref[rows, :] = nt(rounded, wout[...]).astype(BF16)
    resid_one[...] = base[mine, :]


def self_back(qkv, up_ref, lse, grads, biases, dk_acc, dv_acc):
    attend_back(
        qkv.at[0], qkv.at[1], qkv.at[2], up_ref, lse, grads.at[0], dk_acc, dv_acc, None, True
    )
    grads[1] = dk_acc[...].astype(BF16)
    grads[2] = dv_acc[...].astype(BF16)
    biases[0:1, :] = jnp.sum(grads[0].astype(F32), axis=0, keepdims=True)
    biases[1:2, :] = jnp.sum(grads[2].astype(F32), axis=0, keepdims=True)


def one_back(chips, *refs):
    first = refs[0]
    got = refs[1:chips]
    x_own, gain, resid, out = refs[chips:]
    total = first[...]
    for part in got:
        total = total + part[...].astype(F32)
    back, _ = norm_back(x_own[...].astype(F32), row_of(gain, 0), total)
    out[...] = resid[...] + back


def on_device(
    layer_input,
    output_grad,
    memory,
    memory_length,
    norm_gain,
    norm_bias,
    self_qkv,
    self_bias,
    self_out,
    cross_query,
    cross_kv,
    cross_bias,
    cross_out,
    up_weight,
    up_bias,
    down_weight,
    out_bias,
):
    ranks = lax.axis_size("tensor")
    pages_ranks = lax.axis_size("dp")
    chips = ranks // 2
    rank = lax.axis_index("tensor")
    own, wide = layer_input.shape
    seq = own * ranks
    width = self_qkv.shape[2]
    heads = width // HEAD_DIM
    hidden = up_bias.shape[0]
    mem = memory.shape[0]
    mem_pad = -(-mem // 128) * 128

    line = lax.axis_index("dp")
    ids = jnp.reshape(rank, (1,)).astype(jnp.int32)
    role = jnp.reshape((line ^ (line >> 1)) & 1, (1,)).astype(jnp.int32)

    def swap(values, mask):
        return lax.ppermute(values, "tensor", [(i, i ^ mask) for i in range(ranks)])

    def far_parts(values):
        return [values] + [swap(values, 2 * mask) for mask in range(1, chips)]

    def hold(values, *tokens):
        return lax.optimization_barrier((values, *tokens))[0]

    def grouped(name):
        return min(NEAR.get(name, 1), chips)

    def packed(parts):
        shape = (len(parts), *parts[0].shape)
        return call(pack_all, [sds(shape, parts[0].dtype)], parts)[0]

    def near_parts(far, name):
        group = grouped(name)
        groups = [far[at : at + group] for at in range(0, chips, group)]
        return [*far, *(swap(packed(g) if group > 1 else g[0], 1) for g in groups)]

    def joined(former, latter, after):
        shape = (2 * former.shape[0], *former.shape[1:])
        return call(pack, [sds(shape, BF16)], [former, latter], after=after)[0]

    turns = [1 << at for at in range(1, ranks.bit_length() - 1)]

    def gather(values):
        return near_parts(far_parts(values))

    def along(values, pairs):
        return lax.ppermute(
            values,
            "dp",
            [(at + a, at + b) for at in range(0, pages_ranks, 4) for a, b in pairs],
        )

    outer = [(0, 1), (1, 0), (2, 3), (3, 2)]
    middle = [(0, 3), (3, 0), (1, 2), (2, 1)]
    def bucket(body, rows, ins, flops, after, scratch=()):
        half = sds((rows, 4 * width), BF16)
        keep, send = call(body, [half, half], [role, *ins], flops, scratch, after)
        return keep, along(send, outer)

    def across(state, after):
        keep, got = state
        inner = call(add_halves, [sds(keep.shape, BF16)], [keep, got], after=after)[0]
        return inner, along(inner, middle)

    def back_out(state, after):
        inner, got = state
        half = sds(inner.shape, BF16)
        total = call(add_halves, [half], [inner, got], after=after)[0]
        mask = 4
        while mask < pages_ranks:
            pairs = [(i, i ^ mask) for i in range(pages_ranks)]
            total = call(add_halves, [half], [total, lax.ppermute(total, "dp", pairs)])[0]
            mask *= 2
        return total, along(total, outer)

    def stacks(rows, columns, name):
        group = grouped(name)
        shape = (rows, columns) if group == 1 else (group, rows, columns)
        return [sds(shape, BF16)] * (chips // group)

    def sibling_terms(lhs, rhs, dot, after, name):
        rows = lhs.shape[1] // ranks
        columns = rhs.shape[1 if dot is nt else 2]
        return call(
            functools.partial(partial_sibling, chips, dot),
            stacks(rows, columns, name),
            [ids, lhs, rhs],
            lhs.size * columns,
            after=after,
        )

    def own_terms(lhs, rhs, dot, got, after):
        rows, columns = got[0].shape[-2:]
        return call(
            functools.partial(partial_own, chips, dot),
            [sds((rows, columns), F32)] + [sds((rows, columns), BF16)] * (chips - 1),
            [ids, lhs, rhs, *got],
            lhs.size * columns,
            after=after,
        )

    def scatter_far(sums):
        return [sums[0]] + [swap(sums[mask], 2 * mask) for mask in range(1, chips)]

    held, steps = {}, {}

    def fill(slot, kernel, far=()):
        tokens = [kernel, far[1:2], far[1:]][BASE.get(slot, 0)] if far else kernel
        for name in SLOTS[slot]:
            tokens = [steps[name](tokens)]
        return tokens if SLOTS[slot] else []

    x_far = far_parts(layer_input)
    padded, mem_keys, mem_values, query_t = call(
        prepare,
        [
            sds((mem_pad, wide), BF16),
            sds((mem_pad, width), BF16),
            sds((mem_pad, width), BF16),
            sds((width, wide), BF16),
        ],
        [memory, cross_kv, cross_bias, cross_query],
        4 * mem_pad * wide * width,
    )
    x_far = [layer_input] + [hold(part, mem_keys) for part in x_far[1:]]

    def gather_step(name, order, at, until=()):
        def step(after):
            block, got = held[name]
            block = joined(block, got, after)
            if at + 1 < len(order):
                held[name] = (block, swap(hold(block, *until()) if until else block, order[at + 1]))
            else:
                held[name] = (block, swap(block, 1))
            return block

        return step

    def begin(name, value, order, until=()):
        block = value[None]
        held[name] = (block, swap(hold(block, *until) if until else block, order[0]))
        steps[name + "1"] = gather_step(name, order, 0, lambda: holds.get(name, ()))
        for at in range(1, len(order)):
            steps[name + str(at + 1)] = gather_step(name, order, at)

    def finish(name, order):
        for at in range(2, len(order)):
            steps[name + str(at + 1)]([])
        return held[name]

    holds = {}
    forth, back = turns, turns[::-1]
    begin("so", self_out, forth)
    begin("co", cross_out, forth)
    begin("g", output_grad, back)
    if BASE.get("wq start", 0) == 2:
        begin("wq", query_t, forth)
    x_parts = near_parts(x_far, "x")
    x, hidden_one, qkv, self_mixed, self_lse = call(
        functools.partial(self_forward, chips, grouped("x")),
        [
            sds((seq, wide), BF16),
            sds((seq, wide), BF16),
            sds((3, seq, width), BF16),
            sds((seq, width), BF16),
            sds((heads, seq), F32),
        ],
        [ids, *x_parts, norm_gain, norm_bias, self_qkv, self_bias],
        2 * seq * wide * 3 * width + 4 * seq * seq * width,
        after=fill("x", [mem_keys, *x_far[1:]]),
    )
    tokens = fill("self", [self_mixed])
    mixed_far = far_parts(hold(self_mixed, *tokens) if tokens else self_mixed)
    holds["co"] = holds["g"] = mixed_far[1:]
    for name in ("co", "g"):
        if name + "1" in SLOTS["self"] or name + "1" in SLOTS["x"]:
            block, _ = held[name]
            held[name] = (block, swap(hold(block, *mixed_far[1:]), (forth if name == "co" else back)[1]))
    tokens = fill("mixed", [self_mixed], mixed_far)
    mixed_parts = near_parts(mixed_far, "mixed")
    so_block, so_other = finish("so", forth)
    stream_two, hidden_two, cross_q, cross_mixed, cross_lse = call(
        functools.partial(cross_forward, chips, grouped("mixed")),
        [
            sds((seq, wide), F32),
            sds((seq, wide), BF16),
            sds((seq, width), BF16),
            sds((seq, width), BF16),
            sds((heads, seq), F32),
        ],
        [
            memory_length,
            *mixed_parts,
            so_block,
            so_other,
            x,
            norm_gain,
            norm_bias,
            out_bias,
            cross_query,
            cross_bias,
            mem_keys,
            mem_values,
        ],
        2 * seq * wide * (wide + width) + 4 * seq * mem_pad * width,
        after=tokens,
    )
    if BASE.get("wq start", 0) == 1:
        begin("wq", query_t, forth, mixed_far[1:])
    cross_far = far_parts(cross_mixed)
    holds["wq"] = cross_far[1:]
    tokens = fill("cross", [cross_mixed], cross_far)
    cross_parts = near_parts(cross_far, "cross")
    co_block, co_other = finish("co", forth)
    g_block, g_other = finish("g", back)
    if BASE.get("wq start", 0) == 0:
        begin("wq", query_t, forth, cross_far[1:])
    stream_three, hidden_three, activated, pre_grad, whole_grad, grad_sum, up_bias_grad = call(
        functools.partial(mlp, chips, grouped("cross")),
        [
            sds((own, wide), F32),
            sds((seq, wide), BF16),
            sds((seq, hidden), BF16),
            sds((seq, hidden), BF16),
            sds((seq, wide), BF16),
            sds((1, wide), F32),
            sds((1, hidden), F32),
        ],
        [
            ids,
            *cross_parts,
            co_block,
            co_other,
            g_block,
            g_other,
            stream_two,
            norm_gain,
            norm_bias,
            out_bias,
            up_weight,
            up_bias.reshape(1, -1),
            down_weight,
        ],
        2 * seq * wide * (wide + 2 * hidden),
        [pltpu.VMEM((2 * own, wide), F32)],
        after=tokens,
    )

    def step(name):
        return lambda function: steps.__setitem__(name, function)

    @step("bucket m")
    def _(after):
        held["m"] = bucket(
            mlp_bucket,
            wide,
            [activated, whole_grad, hidden_three, pre_grad],
            4 * seq * wide * hidden,
            after,
        )
        return held["m"][0]

    def mover(key, function):
        def run(after):
            held[key] = function(held[key], after)
            return held[key][0]

        return run

    for key in "mca":
        steps["add " + key] = mover(key, across)
        steps["out " + key] = mover(key, back_out)

    up_item, pre_item = up_weight[None], pre_grad[None]
    sibling = sibling_terms(pre_item, up_item, nt, fill("mlp", [pre_grad]), "three")
    got = [swap(part, 1) for part in sibling]
    three_sums = own_terms(pre_item, up_item, nt, got, fill("three", [sibling[0]]))
    three_far = scatter_far(three_sums)
    resid_two, message = call(
        functools.partial(three_back, chips),
        [sds((own, wide), F32), sds((own + 16, wide), BF16)],
        [*three_far, stream_three, norm_gain, output_grad],
        after=fill("three far", [three_sums[0]], three_far),
    )
    cg_far = far_parts(message)
    cg_parts = near_parts(cg_far, "grad")
    cross_grad, cross_sums, dq2, dkv2, cross_bias_grad = call(
        functools.partial(cross_back, chips, grouped("grad")),
        [
            sds((seq, wide), BF16),
            sds((3, wide), F32),
            sds((seq, width), BF16),
            sds((2, mem_pad, width), BF16),
            sds((2, width), F32),
        ],
        [
            ids,
            memory_length,
            *cg_parts,
            cross_out,
            cross_q,
            mem_keys,
            mem_values,
            cross_lse,
        ],
        2 * seq * wide * width + 10 * seq * mem_pad * width,
        [
            pltpu.VMEM((seq, width), BF16),
            pltpu.VMEM((mem_pad, width), F32),
            pltpu.VMEM((mem_pad, width), F32),
        ],
        after=fill("grad far", [message], cg_far),
    )
    dq2_far = far_parts(dq2)

    @step("bucket c")
    def _(after):
        held["c"] = bucket(
            cross_bucket,
            wide // 2,
            [hidden_two, dq2, padded, dkv2, cross_mixed, cross_grad],
            8 * seq * wide * width,
            after,
        )
        return held["c"][0]

    tokens = fill("query far", [dq2], dq2_far)
    dq2_parts = near_parts(dq2_far, "query")
    wq_block, wq_other = finish("wq", forth)
    self_grad, resid_one, self_sums, self_up = call(
        functools.partial(self_upstream, chips, grouped("query")),
        [
            sds((seq, wide), BF16),
            sds((own, wide), F32),
            sds((3, wide), F32),
            sds((seq, width), BF16),
        ],
        [
            ids,
            *dq2_parts,
            wq_block,
            wq_other,
            stream_two,
            norm_gain,
            cross_grad,
            resid_two,
            self_out,
        ],
        2 * seq * wide * (wide + width),
        [pltpu.VMEM((seq, wide), F32)],
        after=tokens,
    )
    grads, self_bias_grad = call(
        self_back,
        [sds((3, seq, width), BF16), sds((2, width), F32)],
        [qkv, self_up, self_lse],
        10 * seq * seq * width,
        [pltpu.VMEM((seq, width), F32), pltpu.VMEM((seq, width), F32)],
        after=fill("up", [self_up]),
    )

    @step("bucket a")
    def _(after):
        held["a"] = bucket(
            self_bucket,
            wide // 2 + 4 * wide // width,
            [
                hidden_one,
                grads,
                self_mixed,
                self_grad,
                self_qkv,
                norm_gain,
                norm_bias,
                self_sums,
                cross_sums,
                grad_sum,
                self_bias_grad,
                cross_bias_grad,
                up_bias_grad,
            ],
            8 * seq * wide * width,
            after,
            [pltpu.VMEM((16, wide), F32)],
        )
        return held["a"][0]

    sibling = sibling_terms(grads, self_qkv, nt, fill("back", [grads]), "one")
    got = [swap(part, 1) for part in sibling]
    one_sums = own_terms(grads, self_qkv, nt, got, fill("one", [sibling[0]]))
    one_far = scatter_far(one_sums)
    (input_grad,) = call(
        functools.partial(one_back, chips),
        [sds((own, wide), F32)],
        [*one_far, layer_input, norm_gain, resid_one],
        after=fill("one far", [one_sums[0]], one_far),
    )
    tokens = fill("input", [input_grad])
    last_ins = [ids, activated, down_weight, cross_kv, dkv2]
    sibling = call(
        functools.partial(last_sibling, chips),
        stacks(own, wide + mem_pad, "last"),
        last_ins,
        after=tokens,
    )
    got = [swap(part, 1) for part in sibling]
    last = call(
        functools.partial(last_own, chips),
        [sds((own, wide + mem_pad), F32)]
        + [sds((own, wide + mem_pad), BF16)] * (chips - 1),
        [*last_ins, *got],
        after=fill("last", [sibling[0]]),
    )
    last_far = scatter_far(last)

    @step("final m")
    def _(after):
        held["final m"] = call(
            mlp_final,
            [sds((hidden, wide), F32), sds((wide, hidden), F32)],
            [role, *held["m"]],
            after=after,
        )
        return held["final m"][0]

    @step("final c")
    def _(after):
        held["final c"] = call(
            cross_final,
            [sds((wide, width), F32), sds((2, wide, width), F32), sds((width, wide), F32)],
            [role, *held["c"]],
            after=after,
        )
        return held["final c"][0]

    @step("last final")
    def _(after):
        held["last final"] = call(
            functools.partial(last_final, chips),
            [sds((own, wide), BF16), sds((mem, wide // ranks), F32)],
            [*last_far, stream_three, out_bias],
            after=after,
        )
        return held["last final"][0]

    out_a = steps["out a"]

    @step("out a")
    def _(after):
        total = out_a(after)
        small = call(small_rows, [sds((16, wide), F32)], [total])[0]
        pair = call(add_pair, [sds((16, wide), F32)], [small, swap(small, 1)])[0]
        held["small"] = [small, *far_parts(pair)]
        return small

    fill("last far", [last[0]], last_far)
    tokens = fill("end", [held["last final"][0]] if "last final" in held else [last[0]])
    gains, shifts, outs, self_bias_sum, cross_bias_sum, up_bias_sum = call(
        small_final,
        [sds((3, wide), F32)] * 3
        + [sds((2, width), F32), sds((2, width), F32), sds((1, hidden), F32)],
        held["small"],
        after=tokens,
    )
    self_qkv_grad, self_out_grad = call(
        self_final,
        [sds((3, wide, width), F32), sds((width, wide), F32)],
        [role, *held["a"]],
        after=[gains],
    )
    output, memory_grad = held["last final"]
    down_grad, up_grad = held["final m"]
    cross_query_grad, cross_kv_grad, cross_out_grad = held["final c"]
    return (
        output,
        input_grad,
        memory_grad,
        gains,
        shifts,
        self_qkv_grad,
        self_bias_sum,
        self_out_grad,
        cross_query_grad,
        cross_kv_grad,
        cross_bias_sum,
        cross_out_grad,
        up_grad,
        up_bias_sum.reshape(-1),
        down_grad,
        outs,
    )


def solution(mesh):
    return jax.shard_map(
        on_device,
        mesh=mesh,
        in_specs=(
            P(("dp", "tensor"), None),
            P(("dp", "tensor"), None),
            P("dp", None),
            P("dp"),
            P(),
            P(),
            P(None, None, "tensor"),
            P(None, "tensor"),
            P("tensor", None),
            P(None, "tensor"),
            P(None, None, "tensor"),
            P(None, "tensor"),
            P("tensor", None),
            P(None, "tensor"),
            P("tensor"),
            P("tensor", None),
            P(),
        ),
        out_specs=(
            P(("dp", "tensor"), None),
            P(("dp", "tensor"), None),
            P("dp", "tensor"),
            P(),
            P(),
            P(None, None, "tensor"),
            P(None, "tensor"),
            P("tensor", None),
            P(None, "tensor"),
            P(None, None, "tensor"),
            P(None, "tensor"),
            P("tensor", None),
            P(None, "tensor"),
            P("tensor"),
            P("tensor", None),
            P(),
        ),
        check_vma=False,
    )
```
